128 devices in a mesh: line: 32 (over x, y, core), tm: 4 (over z).
Axes of the slice: x: 4, y: 4, z: 4, core: 2. Of those that a mesh axis runs over, the one named last changes fastest.
Arguments:
- gust_coef: bfloat16 [128, 128, 32, 256], P(('line', 'tm')), may hold values from -0.625 to 0.625
- mean_wind: float32 [32, 256], P('line'), may hold values from 0.5 to 2
- drag: float32 [32, 256], P('line'), may hold values from 0.2 to 1
- span_column: int32 [32], replicated, may hold values from 0 to 31, each once
- segment_step: int32 [128], replicated, may hold values from 0 to 1, as said below
- transfer: float32 [32, 2, 512, 256], P('line'), may hold values from -0.75 to 0.75
- span_stiff: float32 [32, 512, 512], P('line')
- mass: float32 [32, 512], P('line'), may hold values from 0.02 to 0.08
- disp0: float32 [32, 512], P('line'), may hold values from -3 to 3
- vel0: float32 [32, 512], P('line'), may hold values from -3 to 3
- acc0: float32 [32, 512], P('line'), may hold values from -3 to 3
Outputs:
- disp_out: float32 [32, 512], P('line')
- vel_out: float32 [32, 512], P('line')
The draws below stay inside these ranges and needn't reach their ends.
Inputs may be any that keep to these rules, and one draw needn't show every extreme that they name: `span_column`: every span number appears exactly once. `segment_step`: exactly half of the 128 segments load each of the two steps.
All inputs are finite; a program needn't handle non-finite values.
Results may differ from the reference program's by a relative error of at most 0.0003.
Values may be sent and summed in bfloat16 or wider, within the bound.
A program may use at most 128 MiB of HBM per device.

```python
import math
import jax
import jax.numpy as jnp
from jax import lax

B = 512
Q = 256
KF = 64
TS = 64
SPANS = 32
SEGS = 128


def draw_segment_step(key, part):
    key = jax.random.fold_in(key, 5)
    shuffled = jax.random.permutation(key, SEGS)
    return (shuffled >= SEGS // 2).astype(jnp.int32)


def draw_span_stiff(key, part):
    key = jax.random.fold_in(key, 11)
    key_entries, key_diag, key_span = jax.random.split(key, 3)
    row_index = jnp.arange(B)[:, None]
    col_index = jnp.arange(B)[None, :]
    distance = jnp.abs(row_index - col_index).astype(jnp.float32)
    entries = jax.random.uniform(key_entries, (SPANS, B, B), jnp.float32, -1.0, 1.0)
    mirrored = jnp.where(row_index < col_index, entries, jnp.swapaxes(entries, 1, 2))
    falloff = 1.0 / (1.0 + distance) ** 2
    offdiag = jnp.where(row_index == col_index, 0.0, mirrored * falloff)
    margin = jax.random.uniform(key_diag, (SPANS, B), jnp.float32, 0.3, 2.5)
    diagonal = 1.3 + margin
    identity = jnp.eye(B, dtype=jnp.float32)
    stiffness = offdiag + diagonal[:, :, None] * identity[None]
    span_scale = jnp.exp(jax.random.uniform(key_span, (SPANS, 1, 1), jnp.float32, -0.5, 0.6))
    return span_scale * stiffness


def spiked(values, rng, source, target, shards_of, factor):
    owner, partner = [(jnp.arange(values.shape[axis_at]) // (values.shape[axis_at] // shards_of)).reshape([-1 if axis == axis_at else 1 for axis in range(values.ndim)]) for axis_at in (source, target)]
    chosen = jax.random.permutation(rng, shards_of)[partner]
    strong = (owner == chosen) | (owner == (partner + shards_of // 2) % shards_of)
    return jnp.where(strong, factor * values, values)


def steps_of(rng, shape, cuts, smallest, high):
    level = 1.0
    for position, parts in cuts:
        heights = jax.random.uniform(jax.random.fold_in(jax.random.fold_in(rng, 6), position), (parts,), jnp.float32, smallest / len(cuts), high / len(cuts))
        level = level * jnp.repeat(jnp.exp(heights), shape[position] // parts).reshape((-1,) + (1,) * (len(shape) - 1 - position))
    return level


def normal_values(stream_key, dims, spread, limit, cuts=(), kind=jnp.bfloat16):
    loudness = steps_of(stream_key, dims, cuts, -0.22, 0.18) if cuts else 1.0
    values = jax.random.normal(stream_key, dims, jnp.float32) * spread * loudness
    return jnp.minimum(jnp.maximum(values, -limit), limit).astype(kind)


def heavy_noise(rng, shape, spread, bound, pieces, heavy, kind=jnp.bfloat16):
    values = spread * jax.random.normal(rng, shape, jnp.float32)
    if pieces:
        values = values * steps_of(rng, shape, pieces, -0.22, 0.18)
    return jnp.clip(spiked(values, jax.random.fold_in(rng, 3), *heavy), -bound, bound).astype(kind)


def setup_inputs(seed: int = 0) -> dict:
    seeds = jax.random.split(jax.random.key(seed), 12)
    return {
        "gust_coef": heavy_noise(seeds[0], (SEGS, 2 * KF, SPANS, Q), 0.05, 0.625, ((0, 128),), (0, 2, 32, 2.75)),
        "mean_wind": jnp.clip(jnp.exp(math.log(2.0) - 1.3862944 * jax.random.uniform(seeds[1], (SPANS, Q), jnp.float32) ** steps_of(seeds[1], (SPANS, Q), ((0, 32),), -0.2, 0.2)), 0.5, 2.0),
        "drag": jnp.clip(jnp.exp(math.log(1.0) - 1.609438 * jax.random.uniform(seeds[2], (SPANS, Q), jnp.float32) ** steps_of(seeds[2], (SPANS, Q), ((0, 32),), -0.2, 0.2)), 0.2, 1.0),
        "span_column": jax.random.permutation(seeds[3], SPANS).astype(jnp.int32),
        "segment_step": draw_segment_step(jax.random.fold_in(seeds[11], 71), 0),
        "transfer": normal_values(seeds[5], (SPANS, 2, B, Q), (Q // 4) ** -0.5, 0.75, ((0, 32),), jnp.float32),
        "span_stiff": draw_span_stiff(jax.random.fold_in(seeds[11], 71), 0),
        "mass": jnp.clip(jnp.exp(math.log(0.08) - 1.3862944 * jax.random.uniform(seeds[7], (SPANS, B), jnp.float32) ** steps_of(seeds[7], (SPANS, B), ((0, 32),), -0.2, 0.2)), 0.02, 0.08),
        "disp0": normal_values(seeds[8], (SPANS, B), 0.5, 3.0, ((0, 32),), jnp.float32),
        "vel0": normal_values(seeds[9], (SPANS, B), 0.5, 3.0, ((0, 32),), jnp.float32),
        "acc0": normal_values(seeds[10], (SPANS, B), 0.5, 3.0, ((0, 32),), jnp.float32),
    }


accel_scale = 4.0
velocity_scale = 4.0
half_step = 0.5

def exact_dot(first, second):
    return jnp.dot(first.astype(jnp.float32), second.astype(jnp.float32), precision=lax.Precision.HIGHEST, preferred_element_type=jnp.float32)

def trig_table(sample_count, freq_count):
    sample_index = jnp.arange(sample_count, dtype=jnp.float32)[:, None]
    frequency = (jnp.arange(freq_count, dtype=jnp.float32)[None, :] + 0.25) * (math.pi / freq_count)
    phase_angle = sample_index * frequency
    return jnp.concatenate([jnp.cos(phase_angle), jnp.sin(phase_angle)], axis=1).astype(jnp.bfloat16)

def factor_chain(diag_blocks, lower_blocks, upper_blocks):

    def advance(carried, scan_items):
        diag_one, lower_one, upper_one = scan_items
        schur = diag_one - exact_dot(lower_one, carried)
        factor = jnp.linalg.cholesky(schur)
        solved = jax.scipy.linalg.cho_solve((factor, True), upper_one)
        return (solved, (factor, solved))
    _, outputs = lax.scan(advance, jnp.zeros_like(diag_blocks[0]), (diag_blocks, lower_blocks, upper_blocks))
    return outputs

def chain_solve(factors, couplings, lower_blocks, right_side):

    def forward(carried, scan_items):
        factor, lower_one, vector = scan_items
        solved = jax.scipy.linalg.cho_solve((factor, True), vector - exact_dot(lower_one, carried))
        return (solved, solved)
    _, partial_solved = lax.scan(forward, jnp.zeros_like(right_side[0]), (factors, lower_blocks, right_side))

    def backward(carried, scan_items):
        coupling, value = scan_items
        result = value - exact_dot(coupling, carried)
        return (result, result)
    _, solution = lax.scan(backward, jnp.zeros_like(right_side[0]), (couplings, partial_solved), reverse=True)
    return solution

def reference(gust_coef, mean_wind, drag, span_column, segment_step, transfer, span_stiff, mass, disp0, vel0, acc0):
    trig_rows = trig_table(TS, KF)

    def synthesize(spectra):
        wind_one = jnp.dot(trig_rows.astype(jnp.float32), spectra.reshape(2 * KF, SPANS * Q).astype(jnp.float32), preferred_element_type=jnp.float32)
        return jnp.take(wind_one.astype(jnp.bfloat16).reshape(TS, SPANS, Q), span_column, axis=1)
    wind_field = lax.map(synthesize, gust_coef)
    left_map = transfer[:, 0]
    right_map = transfer[:, 1]
    before = jnp.concatenate([jnp.zeros((1, B, B), jnp.float32), span_stiff[:-1]], axis=0)
    identity = jnp.eye(B, dtype=jnp.float32)
    diag_blocks = span_stiff + before + (accel_scale * mass)[:, :, None] * identity[None]
    coupled = (jnp.arange(SPANS) < SPANS - 1).astype(jnp.float32)[:, None, None]
    upper_blocks = -span_stiff * coupled
    lower_blocks = -before
    factors, couplings = factor_chain(diag_blocks, lower_blocks, upper_blocks)

    def window_load(offset, window):
        window_flags = (segment_step == window).astype(jnp.float32)

        def accumulate(summed, scan_items):
            wind_one, selected = scan_items
            relative = wind_one.astype(jnp.float32) + offset[None]
            return (summed + selected * jnp.sum(relative * jnp.abs(relative), axis=0), None)
        summed, _ = lax.scan(accumulate, jnp.zeros((SPANS, Q), jnp.float32), (wind_field, window_flags))
        return drag * summed / (TS * (SEGS // 2))
    displacement, velocity, accel_now = (disp0, vel0, acc0)
    zero_row = jnp.zeros((1, B), jnp.float32)
    for window in range(2):
        next_velocity = jnp.concatenate([velocity[1:], zero_row], axis=0)
        interior = jnp.einsum('sbq,sb->sq', left_map, velocity, precision=lax.Precision.HIGHEST)
        interior = interior + jnp.einsum('sbq,sb->sq', right_map, next_velocity, precision=lax.Precision.HIGHEST)
        span_load = window_load(mean_wind - interior, window)
        own_force = jnp.einsum('sbq,sq->sb', left_map, span_load, precision=lax.Precision.HIGHEST)
        passed = jnp.einsum('sbq,sq->sb', right_map, span_load, precision=lax.Precision.HIGHEST)
        force = own_force + jnp.concatenate([zero_row, passed[:-1]], axis=0)
        right_side = force + mass * (accel_scale * displacement + velocity_scale * velocity + accel_now)
        new_disp = chain_solve(factors, couplings, lower_blocks, right_side)
        new_accel = accel_scale * (new_disp - displacement) - velocity_scale * velocity - accel_now
        velocity = velocity + half_step * (accel_now + new_accel)
        displacement, accel_now = (new_disp, new_accel)
    return (displacement, velocity)
```

```python
import math

import jax
import jax.numpy as jnp
from jax import lax
from jax.experimental import pallas as pl
from jax.experimental.pallas import tpu as pltpu
from jax.sharding import PartitionSpec as P

Q = 256
KF = 64
TS = 64


accel_scale = 4.0
velocity_scale = 4.0
half_step = 0.5


def shifted(array, axis, by):
    length = lax.axis_size(axis)
    pairs = [(i, i + by) for i in range(length) if 0 <= i + by < length]
    return lax.ppermute(array, axis, pairs)


def exact_dot(first, second):
    return jnp.dot(
        first, second, precision=lax.Precision.HIGHEST, preferred_element_type=jnp.float32
    )


def trig_table(sample_count, freq_count):
    sample_index = jnp.arange(sample_count, dtype=jnp.float32)[:, None]
    frequency = (jnp.arange(freq_count, dtype=jnp.float32)[None, :] + 0.25) * (math.pi / freq_count)
    phase_angle = sample_index * frequency
    return jnp.concatenate([jnp.cos(phase_angle), jnp.sin(phase_angle)], axis=1).astype(
        jnp.bfloat16
    )


def split_dot(first, second):
    first_hi = first.astype(jnp.bfloat16)
    first_lo = (first - first_hi.astype(jnp.float32)).astype(jnp.bfloat16)
    second_hi = second.astype(jnp.bfloat16)
    second_lo = (second - second_hi.astype(jnp.float32)).astype(jnp.bfloat16)
    left = jnp.concatenate([first_hi, first_hi, first_lo], axis=1)
    right = jnp.concatenate([second_hi, second_lo, second_hi], axis=0)
    return jnp.dot(left, right, preferred_element_type=jnp.float32)


def solve_kernel(diag_ref, sides_ref, inverse_ref, solved_ref):
    order = diag_ref.shape[0]
    rows = lax.broadcasted_iota(jnp.int32, (order, order), 0)
    columns = lax.broadcasted_iota(jnp.int32, (order, order), 1)
    on_diag = rows == columns
    diag = diag_ref[...]
    diag_row = jnp.sum(jnp.where(on_diag, diag, 0.0), axis=0, keepdims=True)
    diag_col = jnp.sum(jnp.where(on_diag, diag, 0.0), axis=1, keepdims=True)
    bound = jnp.max(jnp.sum(jnp.abs(diag), axis=1, keepdims=True) / diag_col)
    scale = jnp.minimum(1.0, 1.8 / bound)
    start = jnp.where(on_diag, 1.0, 0.0) * 2.0 - diag * (scale / diag_row)
    inverse_ref[...] = (scale / diag_col) * start

    def unfinished(state):
        step, error = state
        return (step < 60) & (error > 9e-6)

    def iterate(state):
        step, _ = state
        current = inverse_ref[...]
        residual = jnp.where(on_diag, 1.0, 0.0) - split_dot(diag_ref[...], current)
        inverse_ref[...] = current + jnp.dot(
            current.astype(jnp.bfloat16),
            residual.astype(jnp.bfloat16),
            preferred_element_type=jnp.float32,
        )
        return step + 1, jnp.sum(residual * residual)

    lax.while_loop(unfinished, iterate, (jnp.int32(0), jnp.float32(1.0)))
    solved_ref[...] = split_dot(inverse_ref[...], sides_ref[...])


def solve_block(diag, sides):
    order = diag.shape[0]
    return pl.pallas_call(
        solve_kernel,
        out_shape=(
            jax.ShapeDtypeStruct(diag.shape, jnp.float32),
            jax.ShapeDtypeStruct(sides.shape, jnp.float32),
        ),
        in_specs=[pl.BlockSpec(memory_space=pltpu.VMEM)] * 2,
        out_specs=[pl.BlockSpec(memory_space=pltpu.VMEM)] * 2,
        compiler_params=pltpu.CompilerParams(vmem_limit_bytes=48 * 2**20),
        cost_estimate=pl.CostEstimate(
            flops=24 * order**3, bytes_accessed=24 * order**2, transcendentals=0
        ),
    )(diag, sides)


def local(
    gust_coef,
    mean_wind,
    drag,
    span_column,
    segment_step,
    transfer,
    span_stiff,
    mass,
    disp0,
    vel0,
    acc0,
):
    line_count = lax.axis_size("line")
    time_count = lax.axis_size("tm")
    line_pos = lax.axis_index("line")
    time_pos = lax.axis_index("tm")
    span_count = span_column.shape[0]
    block_order = span_stiff.shape[-1]
    seg_count = segment_step.shape[0]
    trig_rows = trig_table(TS, KF)
    spectra = gust_coef.reshape(2 * KF, span_count * Q)
    wind_field = jnp.dot(trig_rows, spectra, preferred_element_type=jnp.float32).astype(
        jnp.bfloat16
    )
    wind_field = jnp.take(wind_field.reshape(TS, span_count, Q), span_column, axis=1)
    left_map = transfer[0, 0]
    right_map = transfer[0, 1]
    window_scale = 1.0 / (TS * (seg_count // 2))
    arrived = lax.all_to_all(wind_field, "line", split_axis=1, concat_axis=0, tiled=True)
    arrived = arrived.reshape(line_count, TS, Q)
    seg_index = jnp.arange(line_count, dtype=jnp.int32) * time_count + time_pos
    seg_flags = jnp.take(segment_step, seg_index)
    span_block = span_stiff[0]
    before = shifted(span_block, "line", 1)
    identity = jnp.eye(block_order, dtype=jnp.float32)
    diag_block = span_block + before + (accel_scale * mass[0])[:, None] * identity
    coupled = (line_pos < line_count - 1).astype(jnp.float32)
    upper_block = -span_block * coupled
    lower_block = -before
    stored = []
    stride = 1
    while stride < line_count:
        inverse, solved = solve_block(diag_block, jnp.concatenate([lower_block, upper_block], axis=1))
        from_lower = shifted(solved, "line", stride)
        from_upper = shifted(solved, "line", -stride)
        new_diag = (
            diag_block
            - exact_dot(lower_block, from_lower[:, block_order:])
            - exact_dot(upper_block, from_upper[:, :block_order])
        )
        new_lower = -exact_dot(lower_block, from_lower[:, :block_order])
        new_upper = -exact_dot(upper_block, from_upper[:, block_order:])
        stored.append((inverse, lower_block, upper_block))
        diag_block, lower_block, upper_block = (new_diag, new_lower, new_upper)
        stride = stride * 2
    final_inverse, _ = solve_block(diag_block, lower_block)
    displacement, velocity, accel_now = (disp0, vel0, acc0)
    for window in range(2):
        next_velocity = shifted(velocity, "line", -1)
        offset = mean_wind - (exact_dot(velocity, left_map) + exact_dot(next_velocity, right_map))
        relative = arrived.astype(jnp.float32) + offset[None]
        weight = (seg_flags == window).astype(jnp.float32)
        window_partial_value = jnp.sum(
            weight[:, None, None] * relative * jnp.abs(relative), axis=(0, 1)
        )[None]
        summed = lax.psum(window_partial_value, "tm")
        span_load = drag * summed * window_scale
        passed = exact_dot(span_load, right_map.T)
        from_left = shifted(passed, "line", 1)
        force = exact_dot(span_load, left_map.T) + from_left
        right_side = force + mass * (
            accel_scale * displacement + velocity_scale * velocity + accel_now
        )
        vector = right_side[0]
        reach_now = 1
        for solve_inverse, lower_one, upper_one in stored:
            solve_solved = exact_dot(solve_inverse, vector)
            from_below = shifted(solve_solved, "line", reach_now)
            from_above = shifted(solve_solved, "line", -reach_now)
            vector = vector - exact_dot(lower_one, from_below) - exact_dot(upper_one, from_above)
            reach_now = reach_now * 2
        new_disp = exact_dot(final_inverse, vector)[None]
        new_accel = accel_scale * (new_disp - displacement) - velocity_scale * velocity - accel_now
        velocity = velocity + half_step * (accel_now + new_accel)
        displacement, accel_now = (new_disp, new_accel)
    return (displacement, velocity)


def solution(mesh):
    return jax.shard_map(
        local,
        mesh=mesh,
        in_specs=(
            P(("line", "tm"), None, None, None),
            P("line", None),
            P("line", None),
            P(),
            P(),
            P("line", None, None, None),
            P("line", None, None),
            P("line", None),
            P("line", None),
            P("line", None),
            P("line", None),
        ),
        out_specs=(P("line", None), P("line", None)),
        check_vma=False,
    )
```

```python
import math

import jax
import jax.numpy as jnp
from jax import lax
from jax.experimental import pallas as pl
from jax.experimental.pallas import tpu as pltpu
from jax.sharding import PartitionSpec as P

Q = 256
KF = 64
TS = 64


accel_scale = 4.0
velocity_scale = 4.0
half_step = 0.5


def shifted(array, axis, by):
    length = lax.axis_size(axis)
    pairs = [(i, i + by) for i in range(length) if 0 <= i + by < length]
    return lax.ppermute(array, axis, pairs)


def exact_dot(first, second):
    return jnp.dot(
        first, second, precision=lax.Precision.HIGHEST, preferred_element_type=jnp.float32
    )


def trig_table(sample_count, freq_count):
    sample_index = jnp.arange(sample_count, dtype=jnp.float32)[:, None]
    frequency = (jnp.arange(freq_count, dtype=jnp.float32)[None, :] + 0.25) * (math.pi / freq_count)
    phase_angle = sample_index * frequency
    return jnp.concatenate([jnp.cos(phase_angle), jnp.sin(phase_angle)], axis=1).astype(
        jnp.bfloat16
    )


def cho_apply(factor, values):
    return jax.scipy.linalg.cho_solve((factor, True), values)


def blocked_cholesky(matrix):
    order = matrix.shape[0]
    panel_width = min(128, order)
    factor = jnp.zeros_like(matrix)
    trailing = matrix
    for start_row in range(0, order, panel_width):
        end_row = start_row + panel_width
        corner = jnp.linalg.cholesky(trailing[start_row:end_row, start_row:end_row])
        factor = factor.at[start_row:end_row, start_row:end_row].set(corner)
        if end_row < order:
            below = trailing[end_row:, start_row:end_row]
            below_factor = jax.scipy.linalg.solve_triangular(corner, below.T, lower=True).T
            factor = factor.at[end_row:, start_row:end_row].set(below_factor)
            trailing = trailing.at[end_row:, end_row:].add(-exact_dot(below_factor, below_factor.T))
    return factor


def checked_loop(
    line_count,
    time_count,
    arrived,
    seg_flags,
    mean_wind,
    drag,
    transfer,
    span_stiff,
    mass,
    disp0,
    vel0,
    acc0,
    window_scale,
):
    line_pos = lax.axis_index("line")
    block_order = span_stiff.shape[-1]
    left_map = transfer[0, 0]
    right_map = transfer[0, 1]
    span_block = span_stiff[0]
    before = shifted(span_block, "line", 1)
    identity = jnp.eye(block_order, dtype=jnp.float32)
    diag_block = span_block + before + (accel_scale * mass[0])[:, None] * identity
    coupled = (line_pos < line_count - 1).astype(jnp.float32)
    upper_block = -span_block * coupled
    lower_block = -before
    stored = []
    stride = 1
    while stride < line_count:
        factor = blocked_cholesky(diag_block)
        solved = cho_apply(factor, jnp.concatenate([lower_block, upper_block], axis=1))
        from_lower = shifted(solved, "line", stride)
        from_upper = shifted(solved, "line", -stride)
        new_diag = (
            diag_block
            - exact_dot(lower_block, from_lower[:, block_order:])
            - exact_dot(upper_block, from_upper[:, :block_order])
        )
        new_lower = -exact_dot(lower_block, from_lower[:, :block_order])
        new_upper = -exact_dot(upper_block, from_upper[:, block_order:])
        stored.append((factor, lower_block, upper_block))
        diag_block, lower_block, upper_block = (new_diag, new_lower, new_upper)
        stride = stride * 2
    final_factor = blocked_cholesky(diag_block)
    displacement, velocity, accel_now = (disp0, vel0, acc0)
    for window in range(2):
        next_velocity = shifted(velocity, "line", -1)
        offset = mean_wind - (exact_dot(velocity, left_map) + exact_dot(next_velocity, right_map))
        relative = arrived.astype(jnp.float32) + offset[None]
        weight = (seg_flags == window).astype(jnp.float32)
        window_partial_value = jnp.sum(
            weight[:, None, None] * relative * jnp.abs(relative), axis=(0, 1)
        )[None]
        summed = lax.psum(window_partial_value, "tm")
        span_load = drag * summed * window_scale
        passed = exact_dot(span_load, right_map.T)
        from_left = shifted(passed, "line", 1)
        force = exact_dot(span_load, left_map.T) + from_left
        right_side = force + mass * (
            accel_scale * displacement + velocity_scale * velocity + accel_now
        )
        vector = right_side[0]
        reach_now = 1
        for solve_factor, lower_one, upper_one in stored:
            solve_solved = cho_apply(solve_factor, vector)
            from_below = shifted(solve_solved, "line", reach_now)
            from_above = shifted(solve_solved, "line", -reach_now)
            vector = vector - exact_dot(lower_one, from_below) - exact_dot(upper_one, from_above)
            reach_now = reach_now * 2
        new_disp = cho_apply(final_factor, vector)[None]
        new_accel = accel_scale * (new_disp - displacement) - velocity_scale * velocity - accel_now
        velocity = velocity + half_step * (accel_now + new_accel)
        displacement, accel_now = (new_disp, new_accel)
    return (displacement, velocity)


MESH = pl.DeviceIdType.MESH


def halves(value):
    high = value.astype(jnp.bfloat16)
    return high, (value - high.astype(jnp.float32)).astype(jnp.bfloat16)


def split_dot(first, second, first_axis=1, second_axis=0):
    first_hi, first_lo = halves(first)
    second_hi, second_lo = halves(second)
    left = jnp.concatenate([first_hi, first_hi, first_lo], axis=first_axis)
    right = jnp.concatenate([second_hi, second_lo, second_hi], axis=second_axis)
    return lax.dot_general(
        left,
        right,
        (((first_axis,), (second_axis,)), ((), ())),
        preferred_element_type=jnp.float32,
    )


def single_dot(first, second):
    return jnp.dot(
        first.astype(jnp.bfloat16), second.astype(jnp.bfloat16), preferred_element_type=jnp.float32
    )


def eye_mask(order):
    rows = lax.broadcasted_iota(jnp.int32, (order, order), 0)
    return rows == lax.broadcasted_iota(jnp.int32, (order, order), 1)


LANES = 128


def to_column(row):
    mask = eye_mask(LANES)
    parts = [
        jnp.sum(jnp.where(mask, row[:, k : k + LANES], 0.0), axis=1, keepdims=True)
        for k in range(0, row.shape[1], LANES)
    ]
    return jnp.concatenate(parts, axis=0)


def to_row(column):
    mask = eye_mask(LANES)
    parts = [
        jnp.sum(jnp.where(mask, column[k : k + LANES], 0.0), axis=0, keepdims=True)
        for k in range(0, column.shape[0], LANES)
    ]
    return jnp.concatenate(parts, axis=1)


def vec_mat(column, matrix):
    return jnp.sum(column * matrix, axis=0, keepdims=True)


def mat_vec(matrix, row):
    return jnp.sum(matrix * row, axis=1, keepdims=True)


def newton_inverse(diag_ref, inverse_ref, bad_ref, bound_on_residual=9e-6):
    order = diag_ref.shape[0]
    mask = eye_mask(order)
    diag = diag_ref[...]
    on_diag = jnp.where(mask, diag, 0.0)
    diag_row = jnp.sum(on_diag, axis=0, keepdims=True)
    diag_col = jnp.sum(on_diag, axis=1, keepdims=True)
    bound = jnp.max(
        jnp.sum(jnp.abs(diag), axis=0, keepdims=True) / diag_row, axis=1, keepdims=True
    )
    scale = jnp.minimum(1.0, 1.8 / bound)
    identity = jnp.where(mask, 1.0, 0.0)
    inverse_ref[...] = (scale / diag_col) * (2.0 * identity - diag * (scale / diag_row))
    current = inverse_ref[...]
    residual = identity - single_dot(diag_ref[...], current)
    inverse_ref[...] = current + single_dot(current, residual)
    for _ in range(2):
        current = inverse_ref[...]
        residual = identity - split_dot(diag_ref[...], current)
        inverse_ref[...] = current + single_dot(current, residual)
    size = jnp.sum(jnp.sum(residual * residual, axis=0, keepdims=True), axis=1, keepdims=True)
    bad_ref[...] = bad_ref[...] + jnp.where(size < bound_on_residual, 0.0, 1.0)


def line_kernel(
    line_count,
    time_count,
    window_scale,
    levels,
    weight_ref,
    wind_ref,
    mean_ref,
    drag_ref,
    maps_ref,
    span_ref,
    mass_ref,
    disp_in,
    vel_in,
    acc_in,
    disp_ref,
    vel_ref,
    bad_out,
    acc_ref,
    bad_ref,
    side_ref,
    diag_ref,
    inverse_ref,
    prev_span,
    prev_map,
    next_vel,
    couple,
    update,
    scaled,
    update_out,
    couple_out,
    vec_out,
    vec_in,
    load_out,
    load_in,
    sol_out,
    sol_in,
    span_sems,
    map_sems,
    vel_sems,
    update_sems,
    couple_sems,
    vec_sems,
    load_send_sems,
    load_recv_sems,
    sol_sems,
):
    line = lax.axis_index("line")
    time = lax.axis_index("tm")
    core = lax.rem(line, 2)
    order = span_ref.shape[1]
    last = line_count - 1

    barrier = pltpu.get_barrier_semaphore()
    partners = jnp.int32(0)
    for delta in (-1, 1):
        there = (line + delta >= 0) & (line + delta <= last)
        for turn in range(time_count):

            @pl.when(there)
            def _():
                pl.semaphore_signal(
                    barrier,
                    inc=1,
                    device_id=(line + delta, lax.rem(time + turn, time_count)),
                    device_id_type=MESH,
                )

        partners = partners + jnp.where(there, time_count, 0)
    for turn in range(1, time_count):
        pl.semaphore_signal(
            barrier,
            inc=1,
            device_id=(line, lax.rem(time + turn, time_count)),
            device_id_type=MESH,
        )
    partners = partners + (time_count - 1)
    for level in range(1, levels):
        for delta in (-(1 << level), 1 << level):
            there = (core == 0) & (line + delta >= 0) & (line + delta <= last)

            @pl.when(there)
            def _():
                pl.semaphore_signal(
                    barrier, inc=1, device_id=(line + delta, time), device_id_type=MESH
                )

            partners = partners + jnp.where(there, 1, 0)
    pl.semaphore_wait(barrier, partners)

    def remote(source, target, sems, to_line, to_time=None):
        return pltpu.make_async_remote_copy(
            src_ref=source,
            dst_ref=target,
            send_sem=sems[0],
            recv_sem=sems[1],
            device_id=(to_line, time if to_time is None else to_time),
            device_id_type=MESH,
        )

    def span_copy():
        return remote(span_ref.at[0], prev_span, (span_sems.at[0], span_sems.at[1]), line + 1)

    def map_copy():
        return remote(maps_ref.at[0, 1], prev_map, (map_sems.at[0], map_sems.at[1]), line + 1)

    def vel_copy(window):
        return remote(
            vel_ref,
            next_vel.at[window],
            (vel_sems.at[0, window], vel_sems.at[1, window]),
            line - 1,
        )

    def update_copy(level, side):
        stride = jnp.left_shift(1, level)
        return remote(
            update_out.at[side],
            update.at[level, 1 - side],
            (update_sems.at[0, level, side], update_sems.at[1, level, 1 - side]),
            line + (2 * side - 1) * stride,
        )

    def update_wait(level, side):
        remote(
            update_out.at[side],
            update.at[level, side],
            (update_sems.at[0, level, side], update_sems.at[1, level, side]),
            line,
        ).wait_recv()

    def couple_copy(level, side):
        stride = jnp.left_shift(1, level)
        return remote(
            couple_out,
            couple.at[level + 1, 1 - side],
            (couple_sems.at[0, level, side], couple_sems.at[1, level, 1 - side]),
            line + (2 * side - 1) * stride,
        )

    def couple_wait(level, side):
        remote(
            couple_out,
            couple.at[level + 1, side],
            (couple_sems.at[0, level, side], couple_sems.at[1, level, side]),
            line,
        ).wait_recv()

    def vec_copy(window, level, side):
        stride = jnp.left_shift(1, level)
        return remote(
            vec_out.at[window, level, side],
            vec_in.at[window, level, 1 - side],
            (vec_sems.at[0, window, level, side], vec_sems.at[1, window, level, 1 - side]),
            line + (2 * side - 1) * stride,
        )

    def vec_wait(window, level, side):
        remote(
            vec_out.at[window, level, side],
            vec_in.at[window, level, side],
            (vec_sems.at[0, window, level, side], vec_sems.at[1, window, level, side]),
            line,
        ).wait_recv()

    def there(level, side):
        stride = jnp.left_shift(1, level)
        return (line - stride >= 0) if side == 0 else (line + stride <= last)

    def sends(level):
        return core == jnp.where(level == 0, 1, 0)

    vel_ref[...] = vel_in[...]
    disp_ref[...] = disp_in[...]
    acc_ref[...] = acc_in[...]
    bad_ref[...] = jnp.zeros_like(bad_ref)

    @pl.when(core == 0)
    def _():
        span_copy().start()

    @pl.when(line > 0)
    def _():
        vel_copy(0).start()

    @pl.when(line < last)
    def _():
        map_copy().start()

    @pl.when(line == last)
    def _():
        next_vel[...] = jnp.zeros_like(next_vel)

    own_diag = jnp.where(eye_mask(order), accel_scale * to_column(mass_ref[...]), 0.0)
    diag_ref[...] = span_ref[0] + own_diag

    @pl.when(core == 1)
    def _():
        couple[0, 1] = -jnp.where(line < last, 1.0, 0.0) * span_ref[0]
        span_copy().wait_recv()
        diag_ref[...] = diag_ref[...] + prev_span[...]
        couple[0, 0] = -prev_span[...]

    def load_copy(window, turn):
        step = 0 if turn < time_count else 1
        return remote(
            load_out.at[window],
            load_in.at[window, step, time],
            (load_send_sems.at[window, turn], load_recv_sems.at[window, step, time]),
            line + step,
            lax.rem(time + turn, time_count),
        )

    def load_wait(window, step, group):
        remote(
            load_out.at[window],
            load_in.at[window, step, group],
            (load_send_sems.at[window, 0], load_recv_sems.at[window, step, group]),
            line,
        ).wait_recv()

    def begin_loads(window):
        velocity_col = to_column(vel_ref[...])
        next_col = to_column(next_vel[window])
        interior = vec_mat(velocity_col, maps_ref[0, 0]) + vec_mat(next_col, maps_ref[0, 1])
        offset = mean_ref[...] - interior
        count, samples, width = wind_ref.shape

        def add(group, total):
            relative = wind_ref[group].astype(jnp.float32) + offset
            return total + weight_ref[window, group] * (relative * jnp.abs(relative))

        total = lax.fori_loop(0, count, add, jnp.zeros((samples, width), jnp.float32))
        load = drag_ref[...] * jnp.sum(total, axis=0, keepdims=True) * window_scale
        load_out[window] = load
        load_in[window, 0, time] = load
        for turn in range(1, time_count):
            load_copy(window, turn).start()

        @pl.when(line < last)
        def _():
            for turn in range(time_count, 2 * time_count):
                load_copy(window, turn).start()

    def end_loads(window):
        for turn in range(1, time_count):
            load_wait(window, 0, lax.rem(time + turn, time_count))

        @pl.when(line > 0)
        def _():
            for turn in range(time_count):
                load_wait(window, 1, lax.rem(time + turn, time_count))

        def summed(step):
            total = load_in[window, step, 0]
            for group in range(1, time_count):
                total = total + load_in[window, step, group]
            return total

        inertia = mass_ref[...] * (
            accel_scale * disp_ref[...] + velocity_scale * vel_ref[...] + acc_ref[...]
        )
        side_ref[...] = inertia + to_row(mat_vec(maps_ref[0, 0], summed(0)))

        @pl.when(line > 0)
        def _():
            if window == 0:
                map_copy().wait_recv()
            side_ref[...] = side_ref[...] + to_row(mat_vec(prev_map[...], summed(1)))

    def reduce_vector(window, level):
        @pl.when(sends(level))
        def _():
            column = to_column(side_ref[...])
            for side in range(2):
                vec_out[window, level, side, :, :order] = vec_mat(column, scaled[level, side])
                vec_out[window, level, side, :, order:] = bad_ref[...]

                @pl.when(there(level, side))
                def _():
                    vec_copy(window, level, side).start()

        @pl.when(core == 0)
        def _():
            for side in range(2):

                @pl.when(there(level, side))
                def _():
                    vec_wait(window, level, side)
                    side_ref[...] = side_ref[...] - vec_in[window, level, side, :, :order]
                    if window == 1:
                        bad_ref[...] = bad_ref[...] + vec_in[window, level, side, :, order:]

    def factor_level(level, carry):
        @pl.when(sends(level))
        def _():
            newton_inverse(diag_ref, inverse_ref, bad_ref)

        before = jnp.maximum(level - 1, 0)
        for side in range(2):
            expected = (level >= 1) & (level < levels) & (core == 0)

            @pl.when(expected & there(before, side))
            def _():
                couple_wait(before, side)

            @pl.when(expected & jnp.logical_not(there(before, side)))
            def _():
                couple[level, side] = jnp.zeros((order, order), jnp.float32)

        for side in range(2):
            sent = (level >= 1) & sends(before) & there(before, side)

            @pl.when(sent)
            def _():
                update_copy(before, side).wait_send()

            @pl.when(sent & (level < levels))
            def _():
                couple_copy(before, side).wait_send()

        @pl.when(sends(level) & (level < levels))
        def _():
            inverse = inverse_ref[...]
            scaled[level, 0] = split_dot(inverse, couple[level, 0], 1, 1)
            update_out[0] = split_dot(couple[level, 0], scaled[level, 0])

            @pl.when(there(level, 0))
            def _():
                update_copy(level, 0).start()

            scaled[level, 1] = split_dot(inverse, couple[level, 1])
            own = jnp.where(level == 0, 1.0, 0.0)
            update_out[1] = split_dot(couple[level, 1], scaled[level, 1], 0, 0) - own * span_ref[0]

            @pl.when(there(level, 1))
            def _():
                update_copy(level, 1).start()

            @pl.when(level < levels - 1)
            def _():
                couple_out[...] = -split_dot(couple[level, 0], scaled[level, 1])
                for side in range(2):

                    @pl.when(there(level, side))
                    def _():
                        couple_copy(level, side).start()

        @pl.when(level == 0)
        def _():
            @pl.when(line < last)
            def _():
                vel_wait(0)

            begin_loads(0)
            end_loads(0)

        @pl.when(level < levels)
        def _():
            reduce_vector(0, level)

            @pl.when(core == 0)
            def _():
                for side in range(2):

                    @pl.when(there(level, side))
                    def _():
                        update_wait(level, side)
                        diag_ref[...] = diag_ref[...] - update[level, side]

        return carry

    def vel_wait(window):
        remote(
            vel_ref,
            next_vel.at[window],
            (vel_sems.at[0, window], vel_sems.at[1, window]),
            line,
        ).wait_recv()

    lax.fori_loop(0, levels + 1, factor_level, 0)

    def sol_copy(window, side):
        return remote(
            sol_out.at[window],
            sol_in.at[window, 1 - side],
            (sol_sems.at[0, window, side], sol_sems.at[1, window, 1 - side]),
            line + 2 * side - 1,
        )

    def sol_wait(window, side):
        remote(
            sol_out.at[window],
            sol_in.at[window, side],
            (sol_sems.at[0, window, side], sol_sems.at[1, window, side]),
            line,
        ).wait_recv()

    def advance(solution_row):
        new_accel = (
            accel_scale * (solution_row - disp_ref[...])
            - velocity_scale * vel_ref[...]
            - acc_ref[...]
        )
        vel_ref[...] = vel_ref[...] + half_step * (acc_ref[...] + new_accel)
        disp_ref[...] = solution_row
        acc_ref[...] = new_accel

    @pl.when(line > 0)
    def _():
        vel_copy(0).wait_send()

    def finish(window):
        @pl.when(core == 0)
        def _():
            advance(vec_mat(to_column(side_ref[...]), inverse_ref[...]))
            sol_out[window, :, :order] = disp_ref[...]
            sol_out[window, :, order : 2 * order] = vel_ref[...]
            sol_out[window, :, 2 * order :] = bad_ref[...]
            sol_copy(window, 1).start()

            @pl.when(line > 0)
            def _():
                sol_copy(window, 0).start()

        @pl.when(core == 1)
        def _():
            value = vec_mat(to_column(side_ref[...]), inverse_ref[...])
            sol_wait(window, 0)
            behind = mat_vec(scaled[0, 0], sol_in[window, 0, :, :order])
            side_ref[...] = value - to_row(behind)
            if window == 1:
                bad_ref[...] = sol_in[window, 0, :, 2 * order :]

            @pl.when(line < last)
            def _():
                sol_wait(window, 1)
                ahead = mat_vec(scaled[0, 1], sol_in[window, 1, :, :order])
                side_ref[...] = side_ref[...] - to_row(ahead)
                if window == 0:
                    next_vel[1] = sol_in[window, 1, :, order : 2 * order]

            advance(side_ref[...])
            if window == 0:
                vel_copy(1).start()

    finish(0)

    @pl.when(core == 0)
    def _():
        vel_wait(1)

    begin_loads(1)
    end_loads(1)

    def reduce_level(level, carry):
        reduce_vector(1, level)
        return carry

    lax.fori_loop(0, levels, reduce_level, 0)

    @pl.when(core == 1)
    def _():
        vel_copy(1).wait_send()

    finish(1)
    bad_out[...] = bad_ref[...]

    @pl.when(core == 0)
    def _():
        span_copy().wait_send()

    @pl.when(line < last)
    def _():
        map_copy().wait_send()

    for window in range(2):
        for turn in range(1, time_count):
            load_copy(window, turn).wait_send()

        @pl.when(line < last)
        def _():
            for turn in range(time_count, 2 * time_count):
                load_copy(window, turn).wait_send()

        @pl.when(core == 0)
        def _():
            sol_copy(window, 1).wait_send()

            @pl.when(line > 0)
            def _():
                sol_copy(window, 0).wait_send()

    def drain(level, carry):
        for window in range(2):
            for side in range(2):

                @pl.when(sends(level) & there(level, side))
                def _():
                    vec_copy(window, level, side).wait_send()

        return carry

    lax.fori_loop(0, levels, drain, 0)


def run_line(
    line_count,
    time_count,
    window_scale,
    weights,
    arrived,
    mean_wind,
    drag,
    transfer,
    span_stiff,
    mass,
    disp0,
    vel0,
    acc0,
):
    order = span_stiff.shape[-1]
    width = mean_wind.shape[-1]
    levels = (line_count - 1).bit_length()
    row = jax.ShapeDtypeStruct((1, order), jnp.float32)

    def body(*refs):
        line_kernel(line_count, time_count, window_scale, levels, *refs)

    vmem = pl.BlockSpec(memory_space=pltpu.VMEM)
    dma = pltpu.SemaphoreType.DMA

    def buffer(*shape):
        return pltpu.VMEM(shape, jnp.float32)

    return pl.pallas_call(
        body,
        out_shape=(row, row, jax.ShapeDtypeStruct((1, LANES), jnp.float32)),
        in_specs=[pl.BlockSpec(memory_space=pltpu.SMEM)] + [vmem] * 9,
        out_specs=[vmem] * 3,
        scratch_shapes=[
            buffer(1, order),
            buffer(1, LANES),
            buffer(1, order),
            buffer(order, order),
            buffer(order, order),
            buffer(order, order),
            buffer(order, width),
            buffer(2, 1, order),
            buffer(levels, 2, order, order),
            buffer(levels, 2, order, order),
            buffer(levels, 2, order, order),
            buffer(2, order, order),
            buffer(order, order),
            buffer(2, levels, 2, 1, order + LANES),
            buffer(2, levels, 2, 1, order + LANES),
            buffer(2, 1, width),
            buffer(2, 2, time_count, 1, width),
            buffer(2, 1, 2 * order + LANES),
            buffer(2, 2, 1, 2 * order + LANES),
            dma((2,)),
            dma((2,)),
            dma((2, 2)),
            dma((2, levels, 2)),
            dma((2, levels, 2)),
            dma((2, 2, levels, 2)),
            dma((2, 2 * time_count)),
            dma((2, 2, time_count)),
            dma((2, 2, 2)),
        ],
        compiler_params=pltpu.CompilerParams(
            collective_id=0, has_side_effects=True, vmem_limit_bytes=60 * 2**20
        ),
        cost_estimate=pl.CostEstimate(
            flops=100 * order**3, bytes_accessed=5 * 2**20, transcendentals=0
        ),
    )(weights, arrived, mean_wind, drag, transfer, span_stiff, mass, disp0, vel0, acc0)


def local(
    gust_coef,
    mean_wind,
    drag,
    span_column,
    segment_step,
    transfer,
    span_stiff,
    mass,
    disp0,
    vel0,
    acc0,
):
    line_count = lax.axis_size("line")
    time_count = lax.axis_size("tm")
    time_pos = lax.axis_index("tm")
    span_count = span_column.shape[0]
    seg_count = segment_step.shape[0]
    trig_rows = trig_table(TS, KF)
    spectra = gust_coef.reshape(2 * KF, span_count * Q)
    wind_field = jnp.dot(trig_rows, spectra, preferred_element_type=jnp.float32).astype(
        jnp.bfloat16
    )
    wind_field = jnp.take(wind_field.reshape(TS, span_count, Q), span_column, axis=1)
    window_scale = 1.0 / (TS * (seg_count // 2))
    arrived = lax.all_to_all(wind_field, "line", split_axis=1, concat_axis=0, tiled=True)
    arrived = arrived.reshape(line_count, TS, Q)
    seg_index = jnp.arange(line_count, dtype=jnp.int32) * time_count + time_pos
    seg_flags = jnp.take(segment_step, seg_index)
    weights = (seg_flags[None] == jnp.arange(2, dtype=jnp.int32)[:, None]).astype(jnp.float32)
    fast_disp, fast_vel, bad = run_line(
        line_count,
        time_count,
        window_scale,
        weights,
        arrived,
        mean_wind,
        drag,
        transfer,
        span_stiff,
        mass,
        disp0,
        vel0,
        acc0,
    )

    def checked():
        return checked_loop(
            line_count,
            time_count,
            arrived,
            seg_flags,
            mean_wind,
            drag,
            transfer,
            span_stiff,
            mass,
            disp0,
            vel0,
            acc0,
            window_scale,
        )

    return lax.cond(bad[0, 0] < 0.5, lambda: (fast_disp, fast_vel), checked)


def solution(mesh):
    return jax.shard_map(
        local,
        mesh=mesh,
        in_specs=(
            P(("line", "tm"), None, None, None),
            P("line", None),
            P("line", None),
            P(),
            P(),
            P("line", None, None, None),
            P("line", None, None),
            P("line", None),
            P("line", None),
            P("line", None),
            P("line", None),
        ),
        out_specs=(P("line", None), P("line", None)),
        check_vma=False,
    )
```

```python
import math

import jax
import jax.numpy as jnp
from jax import lax
from jax.experimental import pallas as pl
from jax.experimental.pallas import tpu as pltpu
from jax.sharding import PartitionSpec as P

Q = 256
KF = 64
TS = 64


accel_scale = 4.0
velocity_scale = 4.0
half_step = 0.5


def shifted(array, axis, by):
    length = lax.axis_size(axis)
    pairs = [(i, i + by) for i in range(length) if 0 <= i + by < length]
    return lax.ppermute(array, axis, pairs)


def exact_dot(first, second):
    return jnp.dot(
        first, second, precision=lax.Precision.HIGHEST, preferred_element_type=jnp.float32
    )


def trig_table(sample_count, freq_count):
    sample_index = jnp.arange(sample_count, dtype=jnp.float32)[:, None]
    frequency = (jnp.arange(freq_count, dtype=jnp.float32)[None, :] + 0.25) * (math.pi / freq_count)
    phase_angle = sample_index * frequency
    return jnp.concatenate([jnp.cos(phase_angle), jnp.sin(phase_angle)], axis=1).astype(
        jnp.bfloat16
    )


def cho_apply(factor, values):
    return jax.scipy.linalg.cho_solve((factor, True), values)


def blocked_cholesky(matrix):
    order = matrix.shape[0]
    panel_width = min(128, order)
    factor = jnp.zeros_like(matrix)
    trailing = matrix
    for start_row in range(0, order, panel_width):
        end_row = start_row + panel_width
        corner = jnp.linalg.cholesky(trailing[start_row:end_row, start_row:end_row])
        factor = factor.at[start_row:end_row, start_row:end_row].set(corner)
        if end_row < order:
            below = trailing[end_row:, start_row:end_row]
            below_factor = jax.scipy.linalg.solve_triangular(corner, below.T, lower=True).T
            factor = factor.at[end_row:, start_row:end_row].set(below_factor)
            trailing = trailing.at[end_row:, end_row:].add(-exact_dot(below_factor, below_factor.T))
    return factor


def checked_loop(
    line_count,
    time_count,
    arrived,
    seg_flags,
    mean_wind,
    drag,
    transfer,
    span_stiff,
    mass,
    disp0,
    vel0,
    acc0,
    window_scale,
):
    line_pos = lax.axis_index("line")
    block_order = span_stiff.shape[-1]
    left_map = transfer[0, 0]
    right_map = transfer[0, 1]
    span_block = span_stiff[0]
    before = shifted(span_block, "line", 1)
    identity = jnp.eye(block_order, dtype=jnp.float32)
    diag_block = span_block + before + (accel_scale * mass[0])[:, None] * identity
    coupled = (line_pos < line_count - 1).astype(jnp.float32)
    upper_block = -span_block * coupled
    lower_block = -before
    stored = []
    stride = 1
    while stride < line_count:
        factor = blocked_cholesky(diag_block)
        solved = cho_apply(factor, jnp.concatenate([lower_block, upper_block], axis=1))
        from_lower = shifted(solved, "line", stride)
        from_upper = shifted(solved, "line", -stride)
        new_diag = (
            diag_block
            - exact_dot(lower_block, from_lower[:, block_order:])
            - exact_dot(upper_block, from_upper[:, :block_order])
        )
        new_lower = -exact_dot(lower_block, from_lower[:, :block_order])
        new_upper = -exact_dot(upper_block, from_upper[:, block_order:])
        stored.append((factor, lower_block, upper_block))
        diag_block, lower_block, upper_block = (new_diag, new_lower, new_upper)
        stride = stride * 2
    final_factor = blocked_cholesky(diag_block)
    displacement, velocity, accel_now = (disp0, vel0, acc0)
    for window in range(2):
        next_velocity = shifted(velocity, "line", -1)
        offset = mean_wind - (exact_dot(velocity, left_map) + exact_dot(next_velocity, right_map))
        relative = arrived.astype(jnp.float32) + offset[None]
        weight = (seg_flags == window).astype(jnp.float32)
        window_partial_value = jnp.sum(
            weight[:, None, None] * relative * jnp.abs(relative), axis=(0, 1)
        )[None]
        summed = lax.psum(window_partial_value, "tm")
        span_load = drag * summed * window_scale
        passed = exact_dot(span_load, right_map.T)
        from_left = shifted(passed, "line", 1)
        force = exact_dot(span_load, left_map.T) + from_left
        right_side = force + mass * (
            accel_scale * displacement + velocity_scale * velocity + accel_now
        )
        vector = right_side[0]
        reach_now = 1
        for solve_factor, lower_one, upper_one in stored:
            solve_solved = cho_apply(solve_factor, vector)
            from_below = shifted(solve_solved, "line", reach_now)
            from_above = shifted(solve_solved, "line", -reach_now)
            vector = vector - exact_dot(lower_one, from_below) - exact_dot(upper_one, from_above)
            reach_now = reach_now * 2
        new_disp = cho_apply(final_factor, vector)[None]
        new_accel = accel_scale * (new_disp - displacement) - velocity_scale * velocity - accel_now
        velocity = velocity + half_step * (accel_now + new_accel)
        displacement, accel_now = (new_disp, new_accel)
    return (displacement, velocity)


MESH = pl.DeviceIdType.MESH


def halves(value):
    high = value.astype(jnp.bfloat16)
    return high, (value - high.astype(jnp.float32)).astype(jnp.bfloat16)


def split_dot(first, second, first_axis=1, second_axis=0):
    first_hi, first_lo = halves(first)
    second_hi, second_lo = halves(second)
    left = jnp.concatenate([first_hi, first_hi, first_lo], axis=first_axis)
    right = jnp.concatenate([second_hi, second_lo, second_hi], axis=second_axis)
    return lax.dot_general(
        left,
        right,
        (((first_axis,), (second_axis,)), ((), ())),
        preferred_element_type=jnp.float32,
    )


def single_dot(first, second):
    return jnp.dot(
        first.astype(jnp.bfloat16), second.astype(jnp.bfloat16), preferred_element_type=jnp.float32
    )


def eye_mask(order):
    rows = lax.broadcasted_iota(jnp.int32, (order, order), 0)
    return rows == lax.broadcasted_iota(jnp.int32, (order, order), 1)


LANES = 128


def to_column(row):
    mask = eye_mask(LANES)
    parts = [
        jnp.sum(jnp.where(mask, row[:, k : k + LANES], 0.0), axis=1, keepdims=True)
        for k in range(0, row.shape[1], LANES)
    ]
    return jnp.concatenate(parts, axis=0)


def to_row(column):
    mask = eye_mask(LANES)
    parts = [
        jnp.sum(jnp.where(mask, column[k : k + LANES], 0.0), axis=0, keepdims=True)
        for k in range(0, column.shape[0], LANES)
    ]
    return jnp.concatenate(parts, axis=1)


def vec_mat(column, matrix):
    return jnp.sum(column * matrix, axis=0, keepdims=True)


def mat_vec(matrix, row):
    return jnp.sum(matrix * row, axis=1, keepdims=True)


def newton_inverse(diag_ref, inverse_ref, bad_ref, bound_on_residual=0.03):
    order = diag_ref.shape[0]
    mask = eye_mask(order)
    diag = diag_ref[...]
    on_diag = jnp.where(mask, diag, 0.0)
    diag_row = jnp.sum(on_diag, axis=0, keepdims=True)
    diag_col = jnp.sum(on_diag, axis=1, keepdims=True)
    bound = jnp.max(
        jnp.sum(jnp.abs(diag), axis=0, keepdims=True) / diag_row, axis=1, keepdims=True
    )
    scale = jnp.minimum(1.0, 1.8 / bound)
    identity = jnp.where(mask, 1.0, 0.0)
    inverse_ref[...] = (scale / diag_col) * (2.0 * identity - diag * (scale / diag_row))
    current = inverse_ref[...]
    residual = identity - single_dot(diag_ref[...], current)
    estimate = (current + single_dot(current, residual)).astype(jnp.bfloat16)
    diag_hi, diag_lo = halves(diag_ref[...])
    residual = (
        identity
        - jnp.dot(diag_hi, estimate, preferred_element_type=jnp.float32)
        - jnp.dot(diag_lo, estimate, preferred_element_type=jnp.float32)
    )
    size = jnp.max(jnp.sum(jnp.abs(residual), axis=0, keepdims=True), axis=1, keepdims=True)
    bad_ref[...] = bad_ref[...] + jnp.where(size < bound_on_residual, 0.0, 1.0)
    series_hi, series_lo = halves(residual + single_dot(residual, residual))
    inverse_ref[...] = (
        estimate.astype(jnp.float32)
        + jnp.dot(estimate, series_hi, preferred_element_type=jnp.float32)
        + jnp.dot(estimate, series_lo, preferred_element_type=jnp.float32)
    )


def line_kernel(
    line_count,
    time_count,
    window_scale,
    levels,
    weight_ref,
    wind_ref,
    mean_ref,
    drag_ref,
    maps_ref,
    span_ref,
    mass_ref,
    disp_in,
    vel_in,
    acc_in,
    disp_ref,
    vel_ref,
    bad_out,
    acc_ref,
    bad_ref,
    side_ref,
    diag_ref,
    inverse_ref,
    prev_span,
    prev_map,
    next_vel,
    couple,
    update,
    scaled,
    update_out,
    couple_out,
    vec_out,
    vec_in,
    load_out,
    load_in,
    sol_out,
    sol_in,
    span_sems,
    map_sems,
    vel_sems,
    update_sems,
    couple_sems,
    share_send_sems,
    share_recv_sems,
    vec_sems,
    load_send_sems,
    load_recv_sems,
    sol_sems,
):
    line = lax.axis_index("line")
    time = lax.axis_index("tm")
    core = lax.rem(line, 2)
    order = span_ref.shape[1]
    last = line_count - 1

    barrier = pltpu.get_barrier_semaphore()
    partners = jnp.int32(0)
    for delta in (-1, 1):
        there = (line + delta >= 0) & (line + delta <= last)
        for turn in range(time_count):

            @pl.when(there)
            def _():
                pl.semaphore_signal(
                    barrier,
                    inc=1,
                    device_id=(line + delta, lax.rem(time + turn, time_count)),
                    device_id_type=MESH,
                )

        partners = partners + jnp.where(there, time_count, 0)
    for turn in range(1, time_count):
        pl.semaphore_signal(
            barrier,
            inc=1,
            device_id=(line, lax.rem(time + turn, time_count)),
            device_id_type=MESH,
        )
    partners = partners + (time_count - 1)
    for level in range(1, levels):
        for delta in (-(1 << level), 1 << level):
            there = (core == 0) & (line + delta >= 0) & (line + delta <= last)

            @pl.when(there)
            def _():
                pl.semaphore_signal(
                    barrier, inc=1, device_id=(line + delta, time), device_id_type=MESH
                )

            partners = partners + jnp.where(there, 1, 0)
    pl.semaphore_wait(barrier, partners)

    def remote(source, target, sems, to_line, to_time=None):
        return pltpu.make_async_remote_copy(
            src_ref=source,
            dst_ref=target,
            send_sem=sems[0],
            recv_sem=sems[1],
            device_id=(to_line, time if to_time is None else to_time),
            device_id_type=MESH,
        )

    def span_copy():
        return remote(span_ref.at[0], prev_span, (span_sems.at[0], span_sems.at[1]), line + 1)

    def map_copy():
        return remote(maps_ref.at[0, 1], prev_map, (map_sems.at[0], map_sems.at[1]), line + 1)

    def vel_copy(window):
        return remote(
            vel_ref,
            next_vel.at[window],
            (vel_sems.at[0, window], vel_sems.at[1, window]),
            line - 1,
        )

    blocks = order // LANES
    quarter = order // time_count

    def triangle(ref, block):
        start = block * LANES
        return ref.at[pl.ds(start, LANES), pl.ds(start, order - start)]

    def own_rows(ref, group):
        return ref.at[pl.ds(pl.multiple_of(group * quarter, quarter), quarter)]

    def update_copies(level, side):
        stride = jnp.left_shift(1, level)
        return [
            remote(
                triangle(update_out.at[side], block),
                triangle(update.at[level, 1 - side], block),
                (
                    update_sems.at[0, level, side, block],
                    update_sems.at[1, level, 1 - side, block],
                ),
                line + (2 * side - 1) * stride,
            )
            for block in range(blocks)
        ]

    def update_wait(level, side):
        for block in range(blocks):
            remote(
                triangle(update_out.at[side], block),
                triangle(update.at[level, side], block),
                (update_sems.at[0, level, side, block], update_sems.at[1, level, side, block]),
                line,
            ).wait_recv()

    def couple_copy(level, side):
        stride = jnp.left_shift(1, level)
        return remote(
            couple_out,
            own_rows(couple.at[level + 1, 1 - side], time),
            (couple_sems.at[0, level, side], couple_sems.at[1, level, 1 - side]),
            line + (2 * side - 1) * stride,
        )

    def couple_wait(level, side):
        remote(
            couple_out,
            own_rows(couple.at[level + 1, side], time),
            (couple_sems.at[0, level, side], couple_sems.at[1, level, side]),
            line,
        ).wait_recv()

    def share_copy(level, side, turn):
        rows = own_rows(couple.at[level + 1, side], time)
        return remote(
            rows,
            rows,
            (share_send_sems.at[level, side, turn], share_recv_sems.at[level, side, time]),
            line,
            lax.rem(time + turn, time_count),
        )

    def share_wait(level, side, turn):
        group = lax.rem(time + turn, time_count)
        rows = own_rows(couple.at[level + 1, side], group)
        remote(
            rows,
            rows,
            (share_send_sems.at[level, side, turn], share_recv_sems.at[level, side, group]),
            line,
        ).wait_recv()

    def vec_copy(window, level, side):
        stride = jnp.left_shift(1, level)
        return remote(
            vec_out.at[window, level, side],
            vec_in.at[window, level, 1 - side],
            (vec_sems.at[0, window, level, side], vec_sems.at[1, window, level, 1 - side]),
            line + (2 * side - 1) * stride,
        )

    def vec_wait(window, level, side):
        remote(
            vec_out.at[window, level, side],
            vec_in.at[window, level, side],
            (vec_sems.at[0, window, level, side], vec_sems.at[1, window, level, side]),
            line,
        ).wait_recv()

    def there(level, side):
        stride = jnp.left_shift(1, level)
        return (line - stride >= 0) if side == 0 else (line + stride <= last)

    def sends(level):
        return core == jnp.where(level == 0, 1, 0)

    vel_ref[...] = vel_in[...]
    disp_ref[...] = disp_in[...]
    acc_ref[...] = acc_in[...]
    bad_ref[...] = jnp.zeros_like(bad_ref)

    @pl.when(core == 0)
    def _():
        span_copy().start()

    @pl.when(line > 0)
    def _():
        vel_copy(0).start()

    @pl.when(line < last)
    def _():
        map_copy().start()

    @pl.when(line == last)
    def _():
        next_vel[...] = jnp.zeros_like(next_vel)

    own_diag = jnp.where(eye_mask(order), accel_scale * to_column(mass_ref[...]), 0.0)
    diag_ref[...] = span_ref[0] + own_diag

    @pl.when(core == 1)
    def _():
        couple[0, 1] = -jnp.where(line < last, 1.0, 0.0) * span_ref[0]
        span_copy().wait_recv()
        diag_ref[...] = diag_ref[...] + prev_span[...]
        couple[0, 0] = -prev_span[...]

    def load_copy(window, turn):
        step = 0 if turn < time_count else 1
        return remote(
            load_out.at[window],
            load_in.at[window, step, time],
            (load_send_sems.at[window, turn], load_recv_sems.at[window, step, time]),
            line + step,
            lax.rem(time + turn, time_count),
        )

    def load_wait(window, step, group):
        remote(
            load_out.at[window],
            load_in.at[window, step, group],
            (load_send_sems.at[window, 0], load_recv_sems.at[window, step, group]),
            line,
        ).wait_recv()

    def begin_loads(window):
        velocity_col = to_column(vel_ref[...])
        next_col = to_column(next_vel[window])
        interior = vec_mat(velocity_col, maps_ref[0, 0]) + vec_mat(next_col, maps_ref[0, 1])
        offset = mean_ref[...] - interior
        count, samples, width = wind_ref.shape

        def add(group, total):
            relative = wind_ref[group].astype(jnp.float32) + offset
            return total + weight_ref[window, group] * (relative * jnp.abs(relative))

        total = lax.fori_loop(0, count, add, jnp.zeros((samples, width), jnp.float32))
        load = drag_ref[...] * jnp.sum(total, axis=0, keepdims=True) * window_scale
        load_out[window] = load
        load_in[window, 0, time] = load
        for turn in range(1, time_count):
            load_copy(window, turn).start()

        @pl.when(line < last)
        def _():
            for turn in range(time_count, 2 * time_count):
                load_copy(window, turn).start()

    def end_loads(window):
        for turn in range(1, time_count):
            load_wait(window, 0, lax.rem(time + turn, time_count))

        @pl.when(line > 0)
        def _():
            for turn in range(time_count):
                load_wait(window, 1, lax.rem(time + turn, time_count))

        def summed(step):
            total = load_in[window, step, 0]
            for group in range(1, time_count):
                total = total + load_in[window, step, group]
            return total

        inertia = mass_ref[...] * (
            accel_scale * disp_ref[...] + velocity_scale * vel_ref[...] + acc_ref[...]
        )
        side_ref[...] = inertia + to_row(mat_vec(maps_ref[0, 0], summed(0)))

        @pl.when(line > 0)
        def _():
            if window == 0:
                map_copy().wait_recv()
            side_ref[...] = side_ref[...] + to_row(mat_vec(prev_map[...], summed(1)))

    def reduce_vector(window, level):
        @pl.when(sends(level))
        def _():
            column = to_column(side_ref[...])
            for side in range(2):
                vec_out[window, level, side, :, :order] = vec_mat(column, scaled[level, side])
                vec_out[window, level, side, :, order:] = bad_ref[...]

                @pl.when(there(level, side))
                def _():
                    vec_copy(window, level, side).start()

        @pl.when(core == 0)
        def _():
            for side in range(2):

                @pl.when(there(level, side))
                def _():
                    vec_wait(window, level, side)
                    side_ref[...] = side_ref[...] - vec_in[window, level, side, :, :order]
                    if window == 1:
                        bad_ref[...] = bad_ref[...] + vec_in[window, level, side, :, order:]

    def factor_level(level, carry):
        @pl.when(sends(level))
        def _():
            newton_inverse(diag_ref, inverse_ref, bad_ref)

        before = jnp.maximum(level - 1, 0)

        for side in range(2):
            sent = (level >= 1) & sends(before) & there(before, side)

            @pl.when(sent)
            def _():
                for copy in update_copies(before, side):
                    copy.wait_send()

            @pl.when(sent & (level < levels))
            def _():
                couple_copy(before, side).wait_send()

        def coupling(side):
            expected = (level >= 1) & (core == 0)

            @pl.when(expected & there(before, side))
            def _():
                for turn in range(1, time_count):
                    share_wait(before, side, turn)
                    share_copy(before, side, turn).wait_send()

            @pl.when(expected & jnp.logical_not(there(before, side)))
            def _():
                couple[level, side] = jnp.zeros((order, order), jnp.float32)

        @pl.when(sends(level) & (level < levels))
        def _():
            coupling(0)
            scaled[level, 0] = split_dot(inverse_ref[...], couple[level, 0], 1, 1)
            coupling(1)
            scaled[level, 1] = split_dot(inverse_ref[...], couple[level, 1])

            @pl.when(level < levels - 1)
            def _():
                rows = pl.ds(pl.multiple_of(time * quarter, quarter), quarter)
                couple_out[...] = -split_dot(couple[level, 0, rows], scaled[level, 1])
                for side in range(2):

                    @pl.when(there(level, side))
                    def _():
                        couple_copy(level, side).start()

            update_out[0] = split_dot(couple[level, 0], scaled[level, 0])

            @pl.when(there(level, 0))
            def _():
                for copy in update_copies(level, 0):
                    copy.start()

            own = jnp.where(level == 0, 1.0, 0.0)
            update_out[1] = split_dot(couple[level, 1], scaled[level, 1], 0, 0) - own * span_ref[0]

            @pl.when(there(level, 1))
            def _():
                for copy in update_copies(level, 1):
                    copy.start()

        @pl.when(level == 0)
        def _():
            @pl.when(line < last)
            def _():
                vel_wait(0)

            begin_loads(0)

        for side in range(2):

            @pl.when((level < levels - 1) & (core == 0) & there(level, side))
            def _():
                couple_wait(level, side)
                for turn in range(1, time_count):
                    share_copy(level, side, turn).start()

        @pl.when(level == 0)
        def _():
            end_loads(0)

        @pl.when(level < levels)
        def _():
            reduce_vector(0, level)

            @pl.when(core == 0)
            def _():
                for side in range(2):

                    @pl.when(there(level, side))
                    def _():
                        update_wait(level, side)
                        for block in range(blocks):
                            start = block * LANES
                            part = (pl.ds(start, LANES), pl.ds(start, order - start))
                            diag_ref[part] = diag_ref[part] - update[(level, side) + part]

                for block in range(blocks):
                    rows = pl.ds(block * LANES, LANES)
                    for other in range(block + 1, blocks):
                        columns = pl.ds(other * LANES, LANES)
                        diag_ref[columns, rows] = diag_ref[rows, columns].T

        return carry

    def vel_wait(window):
        remote(
            vel_ref,
            next_vel.at[window],
            (vel_sems.at[0, window], vel_sems.at[1, window]),
            line,
        ).wait_recv()

    lax.fori_loop(0, levels + 1, factor_level, 0)

    def sol_copy(window, side):
        return remote(
            sol_out.at[window],
            sol_in.at[window, 1 - side],
            (sol_sems.at[0, window, side], sol_sems.at[1, window, 1 - side]),
            line + 2 * side - 1,
        )

    def sol_wait(window, side):
        remote(
            sol_out.at[window],
            sol_in.at[window, side],
            (sol_sems.at[0, window, side], sol_sems.at[1, window, side]),
            line,
        ).wait_recv()

    def advance(solution_row):
        new_accel = (
            accel_scale * (solution_row - disp_ref[...])
            - velocity_scale * vel_ref[...]
            - acc_ref[...]
        )
        vel_ref[...] = vel_ref[...] + half_step * (acc_ref[...] + new_accel)
        disp_ref[...] = solution_row
        acc_ref[...] = new_accel

    @pl.when(line > 0)
    def _():
        vel_copy(0).wait_send()

    def finish(window):
        @pl.when(core == 0)
        def _():
            advance(vec_mat(to_column(side_ref[...]), inverse_ref[...]))
            sol_out[window, :, :order] = disp_ref[...]
            sol_out[window, :, order : 2 * order] = vel_ref[...]
            sol_out[window, :, 2 * order :] = bad_ref[...]
            sol_copy(window, 1).start()

            @pl.when(line > 0)
            def _():
                sol_copy(window, 0).start()

        @pl.when(core == 1)
        def _():
            value = vec_mat(to_column(side_ref[...]), inverse_ref[...])
            sol_wait(window, 0)
            behind = mat_vec(scaled[0, 0], sol_in[window, 0, :, :order])
            side_ref[...] = value - to_row(behind)
            if window == 1:
                bad_ref[...] = sol_in[window, 0, :, 2 * order :]

            @pl.when(line < last)
            def _():
                sol_wait(window, 1)
                ahead = mat_vec(scaled[0, 1], sol_in[window, 1, :, :order])
                side_ref[...] = side_ref[...] - to_row(ahead)
                if window == 0:
                    next_vel[1] = sol_in[window, 1, :, order : 2 * order]

            advance(side_ref[...])
            if window == 0:
                vel_copy(1).start()

    finish(0)

    @pl.when(core == 0)
    def _():
        vel_wait(1)

    begin_loads(1)
    end_loads(1)

    def reduce_level(level, carry):
        reduce_vector(1, level)
        return carry

    lax.fori_loop(0, levels, reduce_level, 0)

    @pl.when(core == 1)
    def _():
        vel_copy(1).wait_send()

    finish(1)
    bad_out[...] = bad_ref[...]

    @pl.when(core == 0)
    def _():
        span_copy().wait_send()

    @pl.when(line < last)
    def _():
        map_copy().wait_send()

    for window in range(2):
        for turn in range(1, time_count):
            load_copy(window, turn).wait_send()

        @pl.when(line < last)
        def _():
            for turn in range(time_count, 2 * time_count):
                load_copy(window, turn).wait_send()

        @pl.when(core == 0)
        def _():
            sol_copy(window, 1).wait_send()

            @pl.when(line > 0)
            def _():
                sol_copy(window, 0).wait_send()

    def drain(level, carry):
        for window in range(2):
            for side in range(2):

                @pl.when(sends(level) & there(level, side))
                def _():
                    vec_copy(window, level, side).wait_send()

        return carry

    lax.fori_loop(0, levels, drain, 0)


def run_line(
    line_count,
    time_count,
    window_scale,
    weights,
    arrived,
    mean_wind,
    drag,
    transfer,
    span_stiff,
    mass,
    disp0,
    vel0,
    acc0,
):
    order = span_stiff.shape[-1]
    width = mean_wind.shape[-1]
    levels = (line_count - 1).bit_length()
    row = jax.ShapeDtypeStruct((1, order), jnp.float32)

    def body(*refs):
        line_kernel(line_count, time_count, window_scale, levels, *refs)

    vmem = pl.BlockSpec(memory_space=pltpu.VMEM)
    dma = pltpu.SemaphoreType.DMA

    def buffer(*shape):
        return pltpu.VMEM(shape, jnp.float32)

    return pl.pallas_call(
        body,
        out_shape=(row, row, jax.ShapeDtypeStruct((1, LANES), jnp.float32)),
        in_specs=[pl.BlockSpec(memory_space=pltpu.SMEM)] + [vmem] * 9,
        out_specs=[vmem] * 3,
        scratch_shapes=[
            buffer(1, order),
            buffer(1, LANES),
            buffer(1, order),
            buffer(order, order),
            buffer(order, order),
            buffer(order, order),
            buffer(order, width),
            buffer(2, 1, order),
            buffer(levels, 2, order, order),
            buffer(levels, 2, order, order),
            buffer(levels, 2, order, order),
            buffer(2, order, order),
            buffer(order // time_count, order),
            buffer(2, levels, 2, 1, order + LANES),
            buffer(2, levels, 2, 1, order + LANES),
            buffer(2, 1, width),
            buffer(2, 2, time_count, 1, width),
            buffer(2, 1, 2 * order + LANES),
            buffer(2, 2, 1, 2 * order + LANES),
            dma((2,)),
            dma((2,)),
            dma((2, 2)),
            dma((2, levels, 2, order // LANES)),
            dma((2, levels, 2)),
            dma((levels, 2, time_count)),
            dma((levels, 2, time_count)),
            dma((2, 2, levels, 2)),
            dma((2, 2 * time_count)),
            dma((2, 2, time_count)),
            dma((2, 2, 2)),
        ],
        compiler_params=pltpu.CompilerParams(
            collective_id=0, has_side_effects=True, vmem_limit_bytes=60 * 2**20
        ),
        cost_estimate=pl.CostEstimate(
            flops=100 * order**3, bytes_accessed=5 * 2**20, transcendentals=0
        ),
    )(weights, arrived, mean_wind, drag, transfer, span_stiff, mass, disp0, vel0, acc0)


def local(
    gust_coef,
    mean_wind,
    drag,
    span_column,
    segment_step,
    transfer,
    span_stiff,
    mass,
    disp0,
    vel0,
    acc0,
):
    line_count = lax.axis_size("line")
    time_count = lax.axis_size("tm")
    time_pos = lax.axis_index("tm")
    span_count = span_column.shape[0]
    seg_count = segment_step.shape[0]
    trig_rows = trig_table(TS, KF)
    spectra = gust_coef.reshape(2 * KF, span_count * Q)
    wind_field = jnp.dot(trig_rows, spectra, preferred_element_type=jnp.float32).astype(
        jnp.bfloat16
    )
    wind_field = jnp.take(wind_field.reshape(TS, span_count, Q), span_column, axis=1)
    window_scale = 1.0 / (TS * (seg_count // 2))
    arrived = lax.all_to_all(wind_field, "line", split_axis=1, concat_axis=0, tiled=True)
    arrived = arrived.reshape(line_count, TS, Q)
    seg_index = jnp.arange(line_count, dtype=jnp.int32) * time_count + time_pos
    seg_flags = jnp.take(segment_step, seg_index)
    weights = (seg_flags[None] == jnp.arange(2, dtype=jnp.int32)[:, None]).astype(jnp.float32)
    fast_disp, fast_vel, bad = run_line(
        line_count,
        time_count,
        window_scale,
        weights,
        arrived,
        mean_wind,
        drag,
        transfer,
        span_stiff,
        mass,
        disp0,
        vel0,
        acc0,
    )

    def checked():
        return checked_loop(
            line_count,
            time_count,
            arrived,
            seg_flags,
            mean_wind,
            drag,
            transfer,
            span_stiff,
            mass,
            disp0,
            vel0,
            acc0,
            window_scale,
        )

    return lax.cond(bad[0, 0] < 0.5, lambda: (fast_disp, fast_vel), checked)


def solution(mesh):
    return jax.shard_map(
        local,
        mesh=mesh,
        in_specs=(
            P(("line", "tm"), None, None, None),
            P("line", None),
            P("line", None),
            P(),
            P(),
            P("line", None, None, None),
            P("line", None, None),
            P("line", None),
            P("line", None),
            P("line", None),
            P("line", None),
        ),
        out_specs=(P("line", None), P("line", None)),
        check_vma=False,
    )
```

```python
import math

import jax
import jax.numpy as jnp
from jax import lax
from jax.experimental import pallas as pl
from jax.experimental.pallas import tpu as pltpu
from jax.sharding import PartitionSpec as P

Q = 256
KF = 64
TS = 64


accel_scale = 4.0
velocity_scale = 4.0
half_step = 0.5


def shifted(array, axis, by):
    length = lax.axis_size(axis)
    pairs = [(i, i + by) for i in range(length) if 0 <= i + by < length]
    return lax.ppermute(array, axis, pairs)


def exact_dot(first, second):
    return jnp.dot(
        first, second, precision=lax.Precision.HIGHEST, preferred_element_type=jnp.float32
    )


def trig_table(sample_count, freq_count):
    sample_index = jnp.arange(sample_count, dtype=jnp.float32)[:, None]
    frequency = (jnp.arange(freq_count, dtype=jnp.float32)[None, :] + 0.25) * (math.pi / freq_count)
    phase_angle = sample_index * frequency
    return jnp.concatenate([jnp.cos(phase_angle), jnp.sin(phase_angle)], axis=1).astype(
        jnp.bfloat16
    )


def cho_apply(factor, values):
    return jax.scipy.linalg.cho_solve((factor, True), values)


def blocked_cholesky(matrix):
    order = matrix.shape[0]
    panel_width = min(128, order)
    factor = jnp.zeros_like(matrix)
    trailing = matrix
    for start_row in range(0, order, panel_width):
        end_row = start_row + panel_width
        corner = jnp.linalg.cholesky(trailing[start_row:end_row, start_row:end_row])
        factor = factor.at[start_row:end_row, start_row:end_row].set(corner)
        if end_row < order:
            below = trailing[end_row:, start_row:end_row]
            below_factor = jax.scipy.linalg.solve_triangular(corner, below.T, lower=True).T
            factor = factor.at[end_row:, start_row:end_row].set(below_factor)
            trailing = trailing.at[end_row:, end_row:].add(-exact_dot(below_factor, below_factor.T))
    return factor


def checked_loop(
    line_count,
    time_count,
    arrived,
    seg_flags,
    mean_wind,
    drag,
    transfer,
    span_stiff,
    mass,
    disp0,
    vel0,
    acc0,
    window_scale,
):
    line_pos = lax.axis_index("line")
    block_order = span_stiff.shape[-1]
    left_map = transfer[0, 0]
    right_map = transfer[0, 1]
    span_block = span_stiff[0]
    before = shifted(span_block, "line", 1)
    identity = jnp.eye(block_order, dtype=jnp.float32)
    diag_block = span_block + before + (accel_scale * mass[0])[:, None] * identity
    coupled = (line_pos < line_count - 1).astype(jnp.float32)
    upper_block = -span_block * coupled
    lower_block = -before
    stored = []
    stride = 1
    while stride < line_count:
        factor = blocked_cholesky(diag_block)
        solved = cho_apply(factor, jnp.concatenate([lower_block, upper_block], axis=1))
        from_lower = shifted(solved, "line", stride)
        from_upper = shifted(solved, "line", -stride)
        new_diag = (
            diag_block
            - exact_dot(lower_block, from_lower[:, block_order:])
            - exact_dot(upper_block, from_upper[:, :block_order])
        )
        new_lower = -exact_dot(lower_block, from_lower[:, :block_order])
        new_upper = -exact_dot(upper_block, from_upper[:, block_order:])
        stored.append((factor, lower_block, upper_block))
        diag_block, lower_block, upper_block = (new_diag, new_lower, new_upper)
        stride = stride * 2
    final_factor = blocked_cholesky(diag_block)
    displacement, velocity, accel_now = (disp0, vel0, acc0)
    for window in range(2):
        next_velocity = shifted(velocity, "line", -1)
        offset = mean_wind - (exact_dot(velocity, left_map) + exact_dot(next_velocity, right_map))
        relative = arrived.astype(jnp.float32) + offset[None]
        weight = (seg_flags == window).astype(jnp.float32)
        window_partial_value = jnp.sum(
            weight[:, None, None] * relative * jnp.abs(relative), axis=(0, 1)
        )[None]
        summed = lax.psum(window_partial_value, "tm")
        span_load = drag * summed * window_scale
        passed = exact_dot(span_load, right_map.T)
        from_left = shifted(passed, "line", 1)
        force = exact_dot(span_load, left_map.T) + from_left
        right_side = force + mass * (
            accel_scale * displacement + velocity_scale * velocity + accel_now
        )
        vector = right_side[0]
        reach_now = 1
        for solve_factor, lower_one, upper_one in stored:
            solve_solved = cho_apply(solve_factor, vector)
            from_below = shifted(solve_solved, "line", reach_now)
            from_above = shifted(solve_solved, "line", -reach_now)
            vector = vector - exact_dot(lower_one, from_below) - exact_dot(upper_one, from_above)
            reach_now = reach_now * 2
        new_disp = cho_apply(final_factor, vector)[None]
        new_accel = accel_scale * (new_disp - displacement) - velocity_scale * velocity - accel_now
        velocity = velocity + half_step * (accel_now + new_accel)
        displacement, accel_now = (new_disp, new_accel)
    return (displacement, velocity)


MESH = pl.DeviceIdType.MESH


def halves(value):
    high = value.astype(jnp.bfloat16)
    return high, (value - high.astype(jnp.float32)).astype(jnp.bfloat16)


def split_dot(first, second, first_axis=1, second_axis=0):
    first_hi, first_lo = halves(first)
    second_hi, second_lo = halves(second)
    left = jnp.concatenate([first_hi, first_hi, first_lo], axis=first_axis)
    right = jnp.concatenate([second_hi, second_lo, second_hi], axis=second_axis)
    return lax.dot_general(
        left,
        right,
        (((first_axis,), (second_axis,)), ((), ())),
        preferred_element_type=jnp.float32,
    )


def single_dot(first, second):
    return jnp.dot(
        first.astype(jnp.bfloat16), second.astype(jnp.bfloat16), preferred_element_type=jnp.float32
    )


def eye_mask(order):
    rows = lax.broadcasted_iota(jnp.int32, (order, order), 0)
    return rows == lax.broadcasted_iota(jnp.int32, (order, order), 1)


LANES = 128


def to_column(row):
    mask = eye_mask(LANES)
    parts = [
        jnp.sum(jnp.where(mask, row[:, k : k + LANES], 0.0), axis=1, keepdims=True)
        for k in range(0, row.shape[1], LANES)
    ]
    return jnp.concatenate(parts, axis=0)


def to_row(column):
    mask = eye_mask(LANES)
    parts = [
        jnp.sum(jnp.where(mask, column[k : k + LANES], 0.0), axis=0, keepdims=True)
        for k in range(0, column.shape[0], LANES)
    ]
    return jnp.concatenate(parts, axis=1)


def vec_mat(column, matrix):
    return jnp.sum(column * matrix, axis=0, keepdims=True)


def mat_vec(matrix, row):
    return jnp.sum(matrix * row, axis=1, keepdims=True)


def newton_inverse(diag_ref, inverse_ref, bad_ref, bound_on_residual=0.03):
    order = diag_ref.shape[0]
    mask = eye_mask(order)
    diag = diag_ref[...]
    on_diag = jnp.where(mask, diag, 0.0)
    diag_row = jnp.sum(on_diag, axis=0, keepdims=True)
    diag_col = jnp.sum(on_diag, axis=1, keepdims=True)
    bound = jnp.max(
        jnp.sum(jnp.abs(diag), axis=0, keepdims=True) / diag_row, axis=1, keepdims=True
    )
    scale = jnp.minimum(1.0, 1.8 / bound)
    identity = jnp.where(mask, 1.0, 0.0)
    inverse_ref[...] = (scale / diag_col) * (2.0 * identity - diag * (scale / diag_row))
    current = inverse_ref[...]
    residual = identity - single_dot(diag_ref[...], current)
    estimate = (current + single_dot(current, residual)).astype(jnp.bfloat16)
    diag_hi, diag_lo = halves(diag_ref[...])
    residual = (
        identity
        - jnp.dot(diag_hi, estimate, preferred_element_type=jnp.float32)
        - jnp.dot(diag_lo, estimate, preferred_element_type=jnp.float32)
    )
    size = jnp.max(jnp.sum(jnp.abs(residual), axis=0, keepdims=True), axis=1, keepdims=True)
    bad_ref[...] = bad_ref[...] + jnp.where(size < bound_on_residual, 0.0, 1.0)
    series_hi, series_lo = halves(residual + single_dot(residual, residual))
    inverse_ref[...] = (
        estimate.astype(jnp.float32)
        + jnp.dot(estimate, series_hi, preferred_element_type=jnp.float32)
        + jnp.dot(estimate, series_lo, preferred_element_type=jnp.float32)
    )


def line_kernel(
    line_count,
    time_count,
    window_scale,
    levels,
    weight_ref,
    sent_ref,
    mean_ref,
    drag_ref,
    maps_ref,
    span_ref,
    mass_ref,
    disp_in,
    vel_in,
    acc_in,
    disp_ref,
    vel_ref,
    bad_out,
    acc_ref,
    bad_ref,
    side_ref,
    diag_ref,
    inverse_ref,
    prev_span,
    prev_map,
    next_vel,
    couple,
    update,
    scaled,
    update_out,
    couple_out,
    vec_out,
    vec_in,
    load_out,
    load_in,
    sol_out,
    sol_in,
    span_sems,
    map_sems,
    vel_sems,
    update_sems,
    couple_sems,
    share_send_sems,
    share_recv_sems,
    vec_sems,
    load_send_sems,
    load_recv_sems,
    sol_sems,
    wind_ref,
    wind_sems,
):
    line = lax.axis_index("line")
    time = lax.axis_index("tm")
    core = lax.rem(line, 2)
    order = span_ref.shape[1]
    last = line_count - 1

    barrier = pltpu.get_barrier_semaphore()
    partners = jnp.int32(0)
    for delta in (-1, 1):
        there = (line + delta >= 0) & (line + delta <= last)
        for turn in range(1, time_count):

            @pl.when(there)
            def _():
                pl.semaphore_signal(
                    barrier,
                    inc=1,
                    device_id=(line + delta, lax.rem(time + turn, time_count)),
                    device_id_type=MESH,
                )

        partners = partners + jnp.where(there, time_count - 1, 0)
    for turn in range(1, time_count):
        pl.semaphore_signal(
            barrier,
            inc=1,
            device_id=(line, lax.rem(time + turn, time_count)),
            device_id_type=MESH,
        )
    partners = partners + (time_count - 1)

    def greet(turn, carry):
        pl.semaphore_signal(
            barrier,
            inc=1,
            device_id=(lax.rem(line + turn, line_count), time),
            device_id_type=MESH,
        )
        return carry

    lax.fori_loop(1, line_count, greet, 0)
    partners = partners + (line_count - 1)
    pl.semaphore_wait(barrier, partners)

    def remote(source, target, sems, to_line, to_time=None):
        return pltpu.make_async_remote_copy(
            src_ref=source,
            dst_ref=target,
            send_sem=sems[0],
            recv_sem=sems[1],
            device_id=(to_line, time if to_time is None else to_time),
            device_id_type=MESH,
        )

    def span_copy():
        return remote(span_ref.at[0], prev_span, (span_sems.at[0], span_sems.at[1]), line + 1)

    def map_copy():
        return remote(maps_ref.at[0, 1], prev_map, (map_sems.at[0], map_sems.at[1]), line + 1)

    def vel_copy(window):
        return remote(
            vel_ref,
            next_vel.at[window],
            (vel_sems.at[0, window], vel_sems.at[1, window]),
            line - 1,
        )

    blocks = order // LANES
    quarter = order // time_count

    def triangle(ref, block):
        start = block * LANES
        return ref.at[pl.ds(start, LANES), pl.ds(start, order - start)]

    def own_rows(ref, group):
        return ref.at[pl.ds(pl.multiple_of(group * quarter, quarter), quarter)]

    def update_copies(level, side):
        stride = jnp.left_shift(1, level)
        return [
            remote(
                triangle(update_out.at[side], block),
                triangle(update.at[level, 1 - side], block),
                (
                    update_sems.at[0, level, side, block],
                    update_sems.at[1, level, 1 - side, block],
                ),
                line + (2 * side - 1) * stride,
            )
            for block in range(blocks)
        ]

    def update_wait(level, side):
        for block in range(blocks):
            remote(
                triangle(update_out.at[side], block),
                triangle(update.at[level, side], block),
                (update_sems.at[0, level, side, block], update_sems.at[1, level, side, block]),
                line,
            ).wait_recv()

    def couple_copy(level, side):
        stride = jnp.left_shift(1, level)
        return remote(
            couple_out,
            own_rows(couple.at[level + 1, 1 - side], time),
            (couple_sems.at[0, level, side], couple_sems.at[1, level, 1 - side]),
            line + (2 * side - 1) * stride,
        )

    def couple_wait(level, side):
        remote(
            couple_out,
            own_rows(couple.at[level + 1, side], time),
            (couple_sems.at[0, level, side], couple_sems.at[1, level, side]),
            line,
        ).wait_recv()

    def share_copy(level, side, turn):
        rows = own_rows(couple.at[level + 1, side], time)
        return remote(
            rows,
            rows,
            (share_send_sems.at[level, side, turn], share_recv_sems.at[level, side, time]),
            line,
            lax.rem(time + turn, time_count),
        )

    def share_wait(level, side, turn):
        group = lax.rem(time + turn, time_count)
        rows = own_rows(couple.at[level + 1, side], group)
        remote(
            rows,
            rows,
            (share_send_sems.at[level, side, turn], share_recv_sems.at[level, side, group]),
            line,
        ).wait_recv()

    def vec_copy(window, level, side):
        stride = jnp.left_shift(1, level)
        return remote(
            vec_out.at[window, level, side],
            vec_in.at[window, level, 1 - side],
            (vec_sems.at[0, window, level, side], vec_sems.at[1, window, level, 1 - side]),
            line + (2 * side - 1) * stride,
        )

    def vec_wait(window, level, side):
        remote(
            vec_out.at[window, level, side],
            vec_in.at[window, level, side],
            (vec_sems.at[0, window, level, side], vec_sems.at[1, window, level, side]),
            line,
        ).wait_recv()

    def there(level, side):
        stride = jnp.left_shift(1, level)
        return (line - stride >= 0) if side == 0 else (line + stride <= last)

    def sends(level):
        return core == jnp.where(level == 0, 1, 0)

    vel_ref[...] = vel_in[...]
    disp_ref[...] = disp_in[...]
    acc_ref[...] = acc_in[...]
    bad_ref[...] = jnp.zeros_like(bad_ref)

    @pl.when(core == 0)
    def _():
        span_copy().start()

    @pl.when(line > 0)
    def _():
        vel_copy(0).start()

    @pl.when(line < last)
    def _():
        map_copy().start()

    @pl.when(line == last)
    def _():
        next_vel[...] = jnp.zeros_like(next_vel)

    def wind_copy(turn):
        to_line = lax.rem(line + turn, line_count)
        return remote(
            sent_ref.at[to_line],
            wind_ref.at[line],
            (wind_sems.at[0, to_line], wind_sems.at[1, line]),
            to_line,
        )

    def wind_wait(turn):
        from_line = lax.rem(line + turn, line_count)
        remote(
            sent_ref.at[from_line],
            wind_ref.at[from_line],
            (wind_sems.at[0, from_line], wind_sems.at[1, from_line]),
            from_line,
        ).wait_recv()

    def wind_start(turn, carry):
        wind_copy(turn).start()
        return carry

    def wind_done(turn, carry):
        wind_wait(turn)
        return carry

    def wind_left(turn, carry):
        wind_copy(turn).wait_send()
        return carry

    lax.fori_loop(1, line_count, wind_start, 0)
    wind_ref[line] = sent_ref[line]

    own_diag = jnp.where(eye_mask(order), accel_scale * to_column(mass_ref[...]), 0.0)
    diag_ref[...] = span_ref[0] + own_diag

    @pl.when(core == 1)
    def _():
        couple[0, 1] = -jnp.where(line < last, 1.0, 0.0) * span_ref[0]
        span_copy().wait_recv()
        diag_ref[...] = diag_ref[...] + prev_span[...]
        couple[0, 0] = -prev_span[...]

    def load_copy(window, turn):
        step = 0 if turn < time_count else 1
        return remote(
            load_out.at[window],
            load_in.at[window, step, time],
            (load_send_sems.at[window, turn], load_recv_sems.at[window, step, time]),
            line + step,
            lax.rem(time + turn, time_count),
        )

    def load_wait(window, step, group):
        remote(
            load_out.at[window],
            load_in.at[window, step, group],
            (load_send_sems.at[window, 0], load_recv_sems.at[window, step, group]),
            line,
        ).wait_recv()

    def begin_loads(window):
        velocity_col = to_column(vel_ref[...])
        next_col = to_column(next_vel[window])
        interior = vec_mat(velocity_col, maps_ref[0, 0]) + vec_mat(next_col, maps_ref[0, 1])
        offset = mean_ref[...] - interior
        count, samples, width = wind_ref.shape

        def add(group, total):
            relative = wind_ref[group].astype(jnp.float32) + offset
            return total + weight_ref[window, group] * (relative * jnp.abs(relative))

        total = lax.fori_loop(0, count, add, jnp.zeros((samples, width), jnp.float32))
        load = drag_ref[...] * jnp.sum(total, axis=0, keepdims=True) * window_scale
        load_out[window] = load
        load_in[window, 0, time] = load
        for turn in range(1, time_count):
            load_copy(window, turn).start()

        @pl.when(line < last)
        def _():
            for turn in range(time_count, 2 * time_count):
                load_copy(window, turn).start()

    def end_loads(window):
        for turn in range(1, time_count):
            load_wait(window, 0, lax.rem(time + turn, time_count))

        @pl.when(line > 0)
        def _():
            for turn in range(time_count):
                load_wait(window, 1, lax.rem(time + turn, time_count))

        def summed(step):
            total = load_in[window, step, 0]
            for group in range(1, time_count):
                total = total + load_in[window, step, group]
            return total

        inertia = mass_ref[...] * (
            accel_scale * disp_ref[...] + velocity_scale * vel_ref[...] + acc_ref[...]
        )
        side_ref[...] = inertia + to_row(mat_vec(maps_ref[0, 0], summed(0)))

        @pl.when(line > 0)
        def _():
            if window == 0:
                map_copy().wait_recv()
            side_ref[...] = side_ref[...] + to_row(mat_vec(prev_map[...], summed(1)))

    def reduce_vector(window, level):
        @pl.when(sends(level))
        def _():
            column = to_column(side_ref[...])
            for side in range(2):
                vec_out[window, level, side, :, :order] = vec_mat(column, scaled[level, side])
                vec_out[window, level, side, :, order:] = bad_ref[...]

                @pl.when(there(level, side))
                def _():
                    vec_copy(window, level, side).start()

        @pl.when(core == 0)
        def _():
            for side in range(2):

                @pl.when(there(level, side))
                def _():
                    vec_wait(window, level, side)
                    side_ref[...] = side_ref[...] - vec_in[window, level, side, :, :order]
                    if window == 1:
                        bad_ref[...] = bad_ref[...] + vec_in[window, level, side, :, order:]

    def factor_level(level, carry):
        @pl.when(sends(level))
        def _():
            newton_inverse(diag_ref, inverse_ref, bad_ref)

        before = jnp.maximum(level - 1, 0)

        for side in range(2):
            sent = (level >= 1) & sends(before) & there(before, side)

            @pl.when(sent)
            def _():
                for copy in update_copies(before, side):
                    copy.wait_send()

            @pl.when(sent & (level < levels))
            def _():
                couple_copy(before, side).wait_send()

        def coupling(side):
            expected = (level >= 1) & (core == 0)

            @pl.when(expected & there(before, side))
            def _():
                for turn in range(1, time_count):
                    share_wait(before, side, turn)
                    share_copy(before, side, turn).wait_send()

            @pl.when(expected & jnp.logical_not(there(before, side)))
            def _():
                couple[level, side] = jnp.zeros((order, order), jnp.float32)

        @pl.when(sends(level) & (level < levels))
        def _():
            coupling(0)
            scaled[level, 0] = split_dot(inverse_ref[...], couple[level, 0], 1, 1)
            coupling(1)
            scaled[level, 1] = split_dot(inverse_ref[...], couple[level, 1])

            @pl.when(level < levels - 1)
            def _():
                rows = pl.ds(pl.multiple_of(time * quarter, quarter), quarter)
                couple_out[...] = -split_dot(couple[level, 0, rows], scaled[level, 1])
                for side in range(2):

                    @pl.when(there(level, side))
                    def _():
                        couple_copy(level, side).start()

            update_out[0] = split_dot(couple[level, 0], scaled[level, 0])

            @pl.when(there(level, 0))
            def _():
                for copy in update_copies(level, 0):
                    copy.start()

            own = jnp.where(level == 0, 1.0, 0.0)
            update_out[1] = split_dot(couple[level, 1], scaled[level, 1], 0, 0) - own * span_ref[0]

            @pl.when(there(level, 1))
            def _():
                for copy in update_copies(level, 1):
                    copy.start()

        @pl.when(level == 0)
        def _():
            @pl.when(line < last)
            def _():
                vel_wait(0)

            lax.fori_loop(1, line_count, wind_done, 0)
            begin_loads(0)

        for side in range(2):

            @pl.when((level < levels - 1) & (core == 0) & there(level, side))
            def _():
                couple_wait(level, side)
                for turn in range(1, time_count):
                    share_copy(level, side, turn).start()

        @pl.when(level == 0)
        def _():
            end_loads(0)

        @pl.when(level < levels)
        def _():
            reduce_vector(0, level)

            @pl.when(core == 0)
            def _():
                for side in range(2):

                    @pl.when(there(level, side))
                    def _():
                        update_wait(level, side)
                        for block in range(blocks):
                            start = block * LANES
                            part = (pl.ds(start, LANES), pl.ds(start, order - start))
                            diag_ref[part] = diag_ref[part] - update[(level, side) + part]

                for block in range(blocks):
                    rows = pl.ds(block * LANES, LANES)
                    for other in range(block + 1, blocks):
                        columns = pl.ds(other * LANES, LANES)
                        diag_ref[columns, rows] = diag_ref[rows, columns].T

        return carry

    def vel_wait(window):
        remote(
            vel_ref,
            next_vel.at[window],
            (vel_sems.at[0, window], vel_sems.at[1, window]),
            line,
        ).wait_recv()

    lax.fori_loop(0, levels + 1, factor_level, 0)

    def sol_copy(window, side):
        return remote(
            sol_out.at[window],
            sol_in.at[window, 1 - side],
            (sol_sems.at[0, window, side], sol_sems.at[1, window, 1 - side]),
            line + 2 * side - 1,
        )

    def sol_wait(window, side):
        remote(
            sol_out.at[window],
            sol_in.at[window, side],
            (sol_sems.at[0, window, side], sol_sems.at[1, window, side]),
            line,
        ).wait_recv()

    def advance(solution_row):
        new_accel = (
            accel_scale * (solution_row - disp_ref[...])
            - velocity_scale * vel_ref[...]
            - acc_ref[...]
        )
        vel_ref[...] = vel_ref[...] + half_step * (acc_ref[...] + new_accel)
        disp_ref[...] = solution_row
        acc_ref[...] = new_accel

    @pl.when(line > 0)
    def _():
        vel_copy(0).wait_send()

    def finish(window):
        @pl.when(core == 0)
        def _():
            advance(vec_mat(to_column(side_ref[...]), inverse_ref[...]))
            sol_out[window, :, :order] = disp_ref[...]
            sol_out[window, :, order : 2 * order] = vel_ref[...]
            sol_out[window, :, 2 * order :] = bad_ref[...]
            sol_copy(window, 1).start()

            @pl.when(line > 0)
            def _():
                sol_copy(window, 0).start()

        @pl.when(core == 1)
        def _():
            value = vec_mat(to_column(side_ref[...]), inverse_ref[...])
            sol_wait(window, 0)
            behind = mat_vec(scaled[0, 0], sol_in[window, 0, :, :order])
            side_ref[...] = value - to_row(behind)
            if window == 1:
                bad_ref[...] = sol_in[window, 0, :, 2 * order :]

            @pl.when(line < last)
            def _():
                sol_wait(window, 1)
                ahead = mat_vec(scaled[0, 1], sol_in[window, 1, :, :order])
                side_ref[...] = side_ref[...] - to_row(ahead)
                if window == 0:
                    next_vel[1] = sol_in[window, 1, :, order : 2 * order]

            advance(side_ref[...])
            if window == 0:
                vel_copy(1).start()

    finish(0)

    @pl.when(core == 0)
    def _():
        vel_wait(1)

    begin_loads(1)
    end_loads(1)

    def reduce_level(level, carry):
        reduce_vector(1, level)
        return carry

    lax.fori_loop(0, levels, reduce_level, 0)

    @pl.when(core == 1)
    def _():
        vel_copy(1).wait_send()

    finish(1)
    bad_out[...] = bad_ref[...]

    lax.fori_loop(1, line_count, wind_left, 0)

    @pl.when(core == 0)
    def _():
        span_copy().wait_send()

    @pl.when(line < last)
    def _():
        map_copy().wait_send()

    for window in range(2):
        for turn in range(1, time_count):
            load_copy(window, turn).wait_send()

        @pl.when(line < last)
        def _():
            for turn in range(time_count, 2 * time_count):
                load_copy(window, turn).wait_send()

        @pl.when(core == 0)
        def _():
            sol_copy(window, 1).wait_send()

            @pl.when(line > 0)
            def _():
                sol_copy(window, 0).wait_send()

    def drain(level, carry):
        for window in range(2):
            for side in range(2):

                @pl.when(sends(level) & there(level, side))
                def _():
                    vec_copy(window, level, side).wait_send()

        return carry

    lax.fori_loop(0, levels, drain, 0)


def run_line(
    line_count,
    time_count,
    window_scale,
    weights,
    wind_field,
    mean_wind,
    drag,
    transfer,
    span_stiff,
    mass,
    disp0,
    vel0,
    acc0,
):
    order = span_stiff.shape[-1]
    width = mean_wind.shape[-1]
    levels = (line_count - 1).bit_length()
    row = jax.ShapeDtypeStruct((1, order), jnp.float32)

    def body(*refs):
        line_kernel(line_count, time_count, window_scale, levels, *refs)

    vmem = pl.BlockSpec(memory_space=pltpu.VMEM)
    dma = pltpu.SemaphoreType.DMA

    def buffer(*shape):
        return pltpu.VMEM(shape, jnp.float32)

    return pl.pallas_call(
        body,
        out_shape=(row, row, jax.ShapeDtypeStruct((1, LANES), jnp.float32)),
        in_specs=[pl.BlockSpec(memory_space=pltpu.SMEM)] + [vmem] * 9,
        out_specs=[vmem] * 3,
        scratch_shapes=[
            buffer(1, order),
            buffer(1, LANES),
            buffer(1, order),
            buffer(order, order),
            buffer(order, order),
            buffer(order, order),
            buffer(order, width),
            buffer(2, 1, order),
            buffer(levels, 2, order, order),
            buffer(levels, 2, order, order),
            buffer(levels, 2, order, order),
            buffer(2, order, order),
            buffer(order // time_count, order),
            buffer(2, levels, 2, 1, order + LANES),
            buffer(2, levels, 2, 1, order + LANES),
            buffer(2, 1, width),
            buffer(2, 2, time_count, 1, width),
            buffer(2, 1, 2 * order + LANES),
            buffer(2, 2, 1, 2 * order + LANES),
            dma((2,)),
            dma((2,)),
            dma((2, 2)),
            dma((2, levels, 2, order // LANES)),
            dma((2, levels, 2)),
            dma((levels, 2, time_count)),
            dma((levels, 2, time_count)),
            dma((2, 2, levels, 2)),
            dma((2, 2 * time_count)),
            dma((2, 2, time_count)),
            dma((2, 2, 2)),
            pltpu.VMEM(wind_field.shape, wind_field.dtype),
            dma((2, line_count)),
        ],
        compiler_params=pltpu.CompilerParams(
            collective_id=0, has_side_effects=True, vmem_limit_bytes=60 * 2**20
        ),
        cost_estimate=pl.CostEstimate(
            flops=100 * order**3, bytes_accessed=5 * 2**20, transcendentals=0
        ),
    )(weights, wind_field, mean_wind, drag, transfer, span_stiff, mass, disp0, vel0, acc0)


def local(
    gust_coef,
    mean_wind,
    drag,
    span_column,
    segment_step,
    transfer,
    span_stiff,
    mass,
    disp0,
    vel0,
    acc0,
):
    line_count = lax.axis_size("line")
    time_count = lax.axis_size("tm")
    time_pos = lax.axis_index("tm")
    span_count = span_column.shape[0]
    seg_count = segment_step.shape[0]
    trig_rows = trig_table(TS, KF)
    spectra = gust_coef.reshape(2 * KF, span_count * Q)
    wind_field = jnp.dot(trig_rows, spectra, preferred_element_type=jnp.float32).astype(
        jnp.bfloat16
    )
    wind_field = wind_field.reshape(TS, span_count, Q)
    wind_field = wind_field.at[:, span_column].get(mode="promise_in_bounds").transpose(1, 0, 2)
    window_scale = 1.0 / (TS * (seg_count // 2))
    seg_index = jnp.arange(line_count, dtype=jnp.int32) * time_count + time_pos
    seg_flags = segment_step.at[seg_index].get(mode="promise_in_bounds")
    weights = (seg_flags[None] == jnp.arange(2, dtype=jnp.int32)[:, None]).astype(jnp.float32)
    fast_disp, fast_vel, bad = run_line(
        line_count,
        time_count,
        window_scale,
        weights,
        wind_field,
        mean_wind,
        drag,
        transfer,
        span_stiff,
        mass,
        disp0,
        vel0,
        acc0,
    )

    def checked():
        arrived = lax.all_to_all(wind_field, "line", split_axis=0, concat_axis=0, tiled=True)
        return checked_loop(
            line_count,
            time_count,
            arrived,
            seg_flags,
            mean_wind,
            drag,
            transfer,
            span_stiff,
            mass,
            disp0,
            vel0,
            acc0,
            window_scale,
        )

    return lax.cond(bad[0, 0] < 0.5, lambda: (fast_disp, fast_vel), checked)


def solution(mesh):
    return jax.shard_map(
        local,
        mesh=mesh,
        in_specs=(
            P(("line", "tm"), None, None, None),
            P("line", None),
            P("line", None),
            P(),
            P(),
            P("line", None, None, None),
            P("line", None, None),
            P("line", None),
            P("line", None),
            P("line", None),
            P("line", None),
        ),
        out_specs=(P("line", None), P("line", None)),
        check_vma=False,
    )
```

```python
import math

import jax
import jax.numpy as jnp
from jax import lax
from jax.experimental import pallas as pl
from jax.experimental.pallas import tpu as pltpu
from jax.sharding import PartitionSpec as P

Q = 256
KF = 64
TS = 64


accel_scale = 4.0
velocity_scale = 4.0
half_step = 0.5


def shifted(array, axis, by):
    length = lax.axis_size(axis)
    pairs = [(i, i + by) for i in range(length) if 0 <= i + by < length]
    return lax.ppermute(array, axis, pairs)


def exact_dot(first, second):
    return jnp.dot(
        first, second, precision=lax.Precision.HIGHEST, preferred_element_type=jnp.float32
    )


def trig_table(sample_count, freq_count):
    sample_index = jnp.arange(sample_count, dtype=jnp.float32)[:, None]
    frequency = (jnp.arange(freq_count, dtype=jnp.float32)[None, :] + 0.25) * (math.pi / freq_count)
    phase_angle = sample_index * frequency
    return jnp.concatenate([jnp.cos(phase_angle), jnp.sin(phase_angle)], axis=1).astype(
        jnp.bfloat16
    )


def cho_apply(factor, values):
    return jax.scipy.linalg.cho_solve((factor, True), values)


def blocked_cholesky(matrix):
    order = matrix.shape[0]
    panel_width = min(128, order)
    factor = jnp.zeros_like(matrix)
    trailing = matrix
    for start_row in range(0, order, panel_width):
        end_row = start_row + panel_width
        corner = jnp.linalg.cholesky(trailing[start_row:end_row, start_row:end_row])
        factor = factor.at[start_row:end_row, start_row:end_row].set(corner)
        if end_row < order:
            below = trailing[end_row:, start_row:end_row]
            below_factor = jax.scipy.linalg.solve_triangular(corner, below.T, lower=True).T
            factor = factor.at[end_row:, start_row:end_row].set(below_factor)
            trailing = trailing.at[end_row:, end_row:].add(-exact_dot(below_factor, below_factor.T))
    return factor


def checked_loop(
    line_count,
    time_count,
    arrived,
    seg_flags,
    mean_wind,
    drag,
    transfer,
    span_stiff,
    mass,
    disp0,
    vel0,
    acc0,
    window_scale,
):
    line_pos = lax.axis_index("line")
    block_order = span_stiff.shape[-1]
    left_map = transfer[0, 0]
    right_map = transfer[0, 1]
    span_block = span_stiff[0]
    before = shifted(span_block, "line", 1)
    identity = jnp.eye(block_order, dtype=jnp.float32)
    diag_block = span_block + before + (accel_scale * mass[0])[:, None] * identity
    coupled = (line_pos < line_count - 1).astype(jnp.float32)
    upper_block = -span_block * coupled
    lower_block = -before
    stored = []
    stride = 1
    while stride < line_count:
        factor = blocked_cholesky(diag_block)
        solved = cho_apply(factor, jnp.concatenate([lower_block, upper_block], axis=1))
        from_lower = shifted(solved, "line", stride)
        from_upper = shifted(solved, "line", -stride)
        new_diag = (
            diag_block
            - exact_dot(lower_block, from_lower[:, block_order:])
            - exact_dot(upper_block, from_upper[:, :block_order])
        )
        new_lower = -exact_dot(lower_block, from_lower[:, :block_order])
        new_upper = -exact_dot(upper_block, from_upper[:, block_order:])
        stored.append((factor, lower_block, upper_block))
        diag_block, lower_block, upper_block = (new_diag, new_lower, new_upper)
        stride = stride * 2
    final_factor = blocked_cholesky(diag_block)
    displacement, velocity, accel_now = (disp0, vel0, acc0)
    for window in range(2):
        next_velocity = shifted(velocity, "line", -1)
        offset = mean_wind - (exact_dot(velocity, left_map) + exact_dot(next_velocity, right_map))
        relative = arrived.astype(jnp.float32) + offset[None]
        weight = (seg_flags == window).astype(jnp.float32)
        window_partial_value = jnp.sum(
            weight[:, None, None] * relative * jnp.abs(relative), axis=(0, 1)
        )[None]
        summed = lax.psum(window_partial_value, "tm")
        span_load = drag * summed * window_scale
        passed = exact_dot(span_load, right_map.T)
        from_left = shifted(passed, "line", 1)
        force = exact_dot(span_load, left_map.T) + from_left
        right_side = force + mass * (
            accel_scale * displacement + velocity_scale * velocity + accel_now
        )
        vector = right_side[0]
        reach_now = 1
        for solve_factor, lower_one, upper_one in stored:
            solve_solved = cho_apply(solve_factor, vector)
            from_below = shifted(solve_solved, "line", reach_now)
            from_above = shifted(solve_solved, "line", -reach_now)
            vector = vector - exact_dot(lower_one, from_below) - exact_dot(upper_one, from_above)
            reach_now = reach_now * 2
        new_disp = cho_apply(final_factor, vector)[None]
        new_accel = accel_scale * (new_disp - displacement) - velocity_scale * velocity - accel_now
        velocity = velocity + half_step * (accel_now + new_accel)
        displacement, accel_now = (new_disp, new_accel)
    return (displacement, velocity)


MESH = pl.DeviceIdType.MESH


def halves(value):
    high = value.astype(jnp.bfloat16)
    return high, (value - high.astype(jnp.float32)).astype(jnp.bfloat16)


def split_dot(first, second, first_axis=1, second_axis=0):
    first_hi, first_lo = halves(first)
    second_hi, second_lo = halves(second)
    left = jnp.concatenate([first_hi, first_hi, first_lo], axis=first_axis)
    right = jnp.concatenate([second_hi, second_lo, second_hi], axis=second_axis)
    return lax.dot_general(
        left,
        right,
        (((first_axis,), (second_axis,)), ((), ())),
        preferred_element_type=jnp.float32,
    )


def single_dot(first, second):
    return jnp.dot(
        first.astype(jnp.bfloat16), second.astype(jnp.bfloat16), preferred_element_type=jnp.float32
    )


def eye_mask(order):
    rows = lax.broadcasted_iota(jnp.int32, (order, order), 0)
    return rows == lax.broadcasted_iota(jnp.int32, (order, order), 1)


LANES = 128


def to_column(row):
    mask = eye_mask(LANES)
    parts = [
        jnp.sum(jnp.where(mask, row[:, k : k + LANES], 0.0), axis=1, keepdims=True)
        for k in range(0, row.shape[1], LANES)
    ]
    return jnp.concatenate(parts, axis=0)


def to_row(column):
    mask = eye_mask(LANES)
    parts = [
        jnp.sum(jnp.where(mask, column[k : k + LANES], 0.0), axis=0, keepdims=True)
        for k in range(0, column.shape[0], LANES)
    ]
    return jnp.concatenate(parts, axis=1)


def vec_mat(column, matrix):
    return jnp.sum(column * matrix, axis=0, keepdims=True)


def mat_vec(matrix, row):
    return jnp.sum(matrix * row, axis=1, keepdims=True)


def newton_inverse(diag_ref, inverse_ref, bad_ref, bound_on_residual=0.03):
    order = diag_ref.shape[0]
    mask = eye_mask(order)
    diag = diag_ref[...]
    on_diag = jnp.where(mask, diag, 0.0)
    diag_row = jnp.sum(on_diag, axis=0, keepdims=True)
    diag_col = jnp.sum(on_diag, axis=1, keepdims=True)
    bound = jnp.max(
        jnp.sum(jnp.abs(diag), axis=0, keepdims=True) / diag_row, axis=1, keepdims=True
    )
    scale = jnp.minimum(1.0, 1.8 / bound)
    identity = jnp.where(mask, 1.0, 0.0)
    inverse_ref[...] = (scale / diag_col) * (2.0 * identity - diag * (scale / diag_row))
    current = inverse_ref[...]
    residual = identity - single_dot(diag_ref[...], current)
    estimate = (current + single_dot(current, residual)).astype(jnp.bfloat16)
    diag_hi, diag_lo = halves(diag_ref[...])
    residual = (
        identity
        - jnp.dot(diag_hi, estimate, preferred_element_type=jnp.float32)
        - jnp.dot(diag_lo, estimate, preferred_element_type=jnp.float32)
    )
    size = jnp.max(jnp.sum(jnp.abs(residual), axis=0, keepdims=True), axis=1, keepdims=True)
    bad_ref[...] = bad_ref[...] + jnp.where(size < bound_on_residual, 0.0, 1.0)
    series_hi, series_lo = halves(residual + single_dot(residual, residual))
    inverse_ref[...] = (
        estimate.astype(jnp.float32)
        + jnp.dot(estimate, series_hi, preferred_element_type=jnp.float32)
        + jnp.dot(estimate, series_lo, preferred_element_type=jnp.float32)
    )


def line_kernel(
    line_count,
    time_count,
    window_scale,
    levels,
    step_ref,
    sent_ref,
    mean_ref,
    drag_ref,
    maps_ref,
    span_ref,
    mass_ref,
    disp_in,
    vel_in,
    acc_in,
    disp_ref,
    vel_ref,
    bad_out,
    acc_ref,
    bad_ref,
    side_ref,
    diag_ref,
    inverse_ref,
    prev_span,
    prev_map,
    next_vel,
    couple,
    update,
    scaled,
    update_out,
    couple_out,
    vec_out,
    vec_in,
    load_out,
    load_in,
    sol_out,
    sol_in,
    span_sems,
    map_sems,
    vel_sems,
    update_sems,
    couple_sems,
    share_send_sems,
    share_recv_sems,
    vec_sems,
    load_send_sems,
    load_recv_sems,
    sol_sems,
    wind_ref,
    wind_sems,
):
    line = lax.axis_index("line")
    time = lax.axis_index("tm")
    core = lax.rem(line, 2)
    order = span_ref.shape[1]
    last = line_count - 1

    barrier = pltpu.get_barrier_semaphore()
    partners = jnp.int32(0)
    for delta in (-1, 1):
        there = (line + delta >= 0) & (line + delta <= last)
        for turn in range(1, time_count):

            @pl.when(there)
            def _():
                pl.semaphore_signal(
                    barrier,
                    inc=1,
                    device_id=(line + delta, lax.rem(time + turn, time_count)),
                    device_id_type=MESH,
                )

        partners = partners + jnp.where(there, time_count - 1, 0)
    for turn in range(1, time_count):
        pl.semaphore_signal(
            barrier,
            inc=1,
            device_id=(line, lax.rem(time + turn, time_count)),
            device_id_type=MESH,
        )
    partners = partners + (time_count - 1)

    def greet(turn, carry):
        pl.semaphore_signal(
            barrier,
            inc=1,
            device_id=(lax.rem(line + turn, line_count), time),
            device_id_type=MESH,
        )
        return carry

    lax.fori_loop(1, line_count, greet, 0)
    partners = partners + (line_count - 1)

    def remote(source, target, sems, to_line, to_time=None):
        return pltpu.make_async_remote_copy(
            src_ref=source,
            dst_ref=target,
            send_sem=sems[0],
            recv_sem=sems[1],
            device_id=(to_line, time if to_time is None else to_time),
            device_id_type=MESH,
        )

    def span_copy():
        return remote(span_ref.at[0], prev_span, (span_sems.at[0], span_sems.at[1]), line + 1)

    def map_copy():
        return remote(maps_ref.at[0, 1], prev_map, (map_sems.at[0], map_sems.at[1]), line + 1)

    def vel_copy(window):
        return remote(
            vel_ref,
            next_vel.at[window],
            (vel_sems.at[0, window], vel_sems.at[1, window]),
            line - 1,
        )

    blocks = order // LANES
    quarter = order // time_count

    def triangle(ref, block):
        start = block * LANES
        return ref.at[pl.ds(start, LANES), pl.ds(start, order - start)]

    def own_rows(ref, group):
        return ref.at[pl.ds(pl.multiple_of(group * quarter, quarter), quarter)]

    def update_copies(level, side):
        stride = jnp.left_shift(1, level)
        return [
            remote(
                triangle(update_out.at[side], block),
                triangle(update.at[level, 1 - side], block),
                (
                    update_sems.at[0, level, side, block],
                    update_sems.at[1, level, 1 - side, block],
                ),
                line + (2 * side - 1) * stride,
            )
            for block in range(blocks)
        ]

    def update_wait(level, side):
        for block in range(blocks):
            remote(
                triangle(update_out.at[side], block),
                triangle(update.at[level, side], block),
                (update_sems.at[0, level, side, block], update_sems.at[1, level, side, block]),
                line,
            ).wait_recv()

    def couple_copy(level, side):
        stride = jnp.left_shift(1, level)
        return remote(
            couple_out,
            own_rows(couple.at[level + 1, 1 - side], time),
            (couple_sems.at[0, level, side], couple_sems.at[1, level, 1 - side]),
            line + (2 * side - 1) * stride,
        )

    def couple_wait(level, side):
        remote(
            couple_out,
            own_rows(couple.at[level + 1, side], time),
            (couple_sems.at[0, level, side], couple_sems.at[1, level, side]),
            line,
        ).wait_recv()

    def share_copy(level, side, turn):
        rows = own_rows(couple.at[level + 1, side], time)
        return remote(
            rows,
            rows,
            (share_send_sems.at[level, side, turn], share_recv_sems.at[level, side, time]),
            line,
            lax.rem(time + turn, time_count),
        )

    def share_wait(level, side, turn):
        group = lax.rem(time + turn, time_count)
        rows = own_rows(couple.at[level + 1, side], group)
        remote(
            rows,
            rows,
            (share_send_sems.at[level, side, turn], share_recv_sems.at[level, side, group]),
            line,
        ).wait_recv()

    def vec_copy(window, level, side):
        stride = jnp.left_shift(1, level)
        return remote(
            vec_out.at[window, level, side],
            vec_in.at[window, level, 1 - side],
            (vec_sems.at[0, window, level, side], vec_sems.at[1, window, level, 1 - side]),
            line + (2 * side - 1) * stride,
        )

    def vec_wait(window, level, side):
        remote(
            vec_out.at[window, level, side],
            vec_in.at[window, level, side],
            (vec_sems.at[0, window, level, side], vec_sems.at[1, window, level, side]),
            line,
        ).wait_recv()

    def there(level, side):
        stride = jnp.left_shift(1, level)
        return (line - stride >= 0) if side == 0 else (line + stride <= last)

    def sends(level):
        return core == jnp.where(level == 0, 1, 0)

    vel_ref[...] = vel_in[...]
    disp_ref[...] = disp_in[...]
    acc_ref[...] = acc_in[...]
    bad_ref[...] = jnp.zeros_like(bad_ref)
    own_diag = jnp.where(eye_mask(order), accel_scale * to_column(mass_ref[...]), 0.0)
    diag_ref[...] = span_ref[0] + own_diag

    @pl.when(core == 1)
    def _():
        couple[0, 1] = -jnp.where(line < last, 1.0, 0.0) * span_ref[0]

    pl.semaphore_wait(barrier, partners)

    @pl.when(core == 0)
    def _():
        span_copy().start()

    @pl.when(line > 0)
    def _():
        vel_copy(0).start()

    @pl.when(line < last)
    def _():
        map_copy().start()

    @pl.when(line == last)
    def _():
        next_vel[...] = jnp.zeros_like(next_vel)

    def wind_copy(turn):
        to_line = lax.rem(line + turn, line_count)
        return remote(
            sent_ref.at[to_line],
            wind_ref.at[line],
            (wind_sems.at[0, to_line], wind_sems.at[1, line]),
            to_line,
        )

    def wind_wait(turn):
        from_line = lax.rem(line + turn, line_count)
        remote(
            sent_ref.at[from_line],
            wind_ref.at[from_line],
            (wind_sems.at[0, from_line], wind_sems.at[1, from_line]),
            from_line,
        ).wait_recv()

    def wind_start(turn, carry):
        wind_copy(turn).start()
        return carry

    def wind_done(turn, carry):
        wind_wait(turn)
        return carry

    def wind_left(turn, carry):
        wind_copy(turn).wait_send()
        return carry

    lax.fori_loop(1, line_count, wind_start, 0)
    wind_ref[line] = sent_ref[line]

    @pl.when(core == 1)
    def _():
        span_copy().wait_recv()
        diag_ref[...] = diag_ref[...] + prev_span[...]
        couple[0, 0] = -prev_span[...]

    def load_copy(window, turn):
        step = 0 if turn < time_count else 1
        return remote(
            load_out.at[window],
            load_in.at[window, step, time],
            (load_send_sems.at[window, turn], load_recv_sems.at[window, step, time]),
            line + step,
            lax.rem(time + turn, time_count),
        )

    def load_wait(window, step, group):
        remote(
            load_out.at[window],
            load_in.at[window, step, group],
            (load_send_sems.at[window, 0], load_recv_sems.at[window, step, group]),
            line,
        ).wait_recv()

    def begin_loads(window):
        velocity_col = to_column(vel_ref[...])
        next_col = to_column(next_vel[window])
        interior = vec_mat(velocity_col, maps_ref[0, 0]) + vec_mat(next_col, maps_ref[0, 1])
        offset = mean_ref[...] - interior
        count, samples, width = wind_ref.shape

        def add(group, total):
            relative = wind_ref[group].astype(jnp.float32) + offset
            step = step_ref[group * time_count + time].astype(jnp.float32)
            return total + (step if window == 1 else 1.0 - step) * (relative * jnp.abs(relative))

        total = lax.fori_loop(0, count, add, jnp.zeros((samples, width), jnp.float32))
        load = drag_ref[...] * jnp.sum(total, axis=0, keepdims=True) * window_scale
        load_out[window] = load
        load_in[window, 0, time] = load
        for turn in range(1, time_count):
            load_copy(window, turn).start()

        @pl.when(line < last)
        def _():
            for turn in range(time_count, 2 * time_count):
                load_copy(window, turn).start()

    def end_loads(window):
        for turn in range(1, time_count):
            load_wait(window, 0, lax.rem(time + turn, time_count))

        @pl.when(line > 0)
        def _():
            for turn in range(time_count):
                load_wait(window, 1, lax.rem(time + turn, time_count))

        def summed(step):
            total = load_in[window, step, 0]
            for group in range(1, time_count):
                total = total + load_in[window, step, group]
            return total

        inertia = mass_ref[...] * (
            accel_scale * disp_ref[...] + velocity_scale * vel_ref[...] + acc_ref[...]
        )
        side_ref[...] = inertia + to_row(mat_vec(maps_ref[0, 0], summed(0)))

        @pl.when(line > 0)
        def _():
            if window == 0:
                map_copy().wait_recv()
            side_ref[...] = side_ref[...] + to_row(mat_vec(prev_map[...], summed(1)))

    def send_vector(window, level):
        @pl.when(sends(level))
        def _():
            column = to_column(side_ref[...])
            for side in range(2):
                vec_out[window, level, side, :, :order] = vec_mat(column, scaled[level, side])
                vec_out[window, level, side, :, order:] = bad_ref[...]

                @pl.when(there(level, side))
                def _():
                    vec_copy(window, level, side).start()

    def take_vector(window, level):
        @pl.when(core == 0)
        def _():
            for side in range(2):

                @pl.when(there(level, side))
                def _():
                    vec_wait(window, level, side)
                    side_ref[...] = side_ref[...] - vec_in[window, level, side, :, :order]
                    if window == 1:
                        bad_ref[...] = bad_ref[...] + vec_in[window, level, side, :, order:]

    def factor_level(level, carry):
        before = jnp.maximum(level - 1, 0)

        @pl.when(level == levels)
        def _():
            send_vector(0, before)

        @pl.when(sends(level))
        def _():
            newton_inverse(diag_ref, inverse_ref, bad_ref)

        for side in range(2):
            sent = (level >= 1) & sends(before) & there(before, side)

            @pl.when(sent)
            def _():
                for copy in update_copies(before, side):
                    copy.wait_send()

            @pl.when(sent & (level < levels))
            def _():
                couple_copy(before, side).wait_send()

        def coupling(side):
            expected = (level >= 1) & (core == 0)

            @pl.when(expected & there(before, side))
            def _():
                for turn in range(1, time_count):
                    share_wait(before, side, turn)
                    share_copy(before, side, turn).wait_send()

            @pl.when(expected & jnp.logical_not(there(before, side)))
            def _():
                couple[level, side] = jnp.zeros((order, order), jnp.float32)

        @pl.when(sends(level) & (level < levels))
        def _():
            coupling(0)
            scaled[level, 0] = split_dot(inverse_ref[...], couple[level, 0], 1, 1)
            coupling(1)
            scaled[level, 1] = split_dot(inverse_ref[...], couple[level, 1])

            @pl.when(level < levels - 1)
            def _():
                rows = pl.ds(pl.multiple_of(time * quarter, quarter), quarter)
                couple_out[...] = -split_dot(couple[level, 0, rows], scaled[level, 1])
                for side in range(2):

                    @pl.when(there(level, side))
                    def _():
                        couple_copy(level, side).start()

            update_out[0] = split_dot(couple[level, 0], scaled[level, 0])

            @pl.when(there(level, 0))
            def _():
                for copy in update_copies(level, 0):
                    copy.start()

            own = jnp.where(level == 0, 1.0, 0.0)
            update_out[1] = split_dot(couple[level, 1], scaled[level, 1], 0, 0) - own * span_ref[0]

            @pl.when(there(level, 1))
            def _():
                for copy in update_copies(level, 1):
                    copy.start()

        @pl.when(level == 1)
        def _():
            @pl.when(line < last)
            def _():
                vel_wait(0)

            lax.fori_loop(1, line_count, wind_done, 0)
            begin_loads(0)

        for side in range(2):

            @pl.when((level < levels - 1) & (core == 0) & there(level, side))
            def _():
                couple_wait(level, side)
                for turn in range(1, time_count):
                    share_copy(level, side, turn).start()

        @pl.when(level == 1)
        def _():
            end_loads(0)

        @pl.when((level >= 1) & (level < levels))
        def _():
            send_vector(0, before)

        @pl.when(level >= 1)
        def _():
            take_vector(0, before)

        @pl.when(level < levels)
        def _():
            @pl.when(core == 0)
            def _():
                for side in range(2):

                    @pl.when(there(level, side))
                    def _():
                        update_wait(level, side)
                        for block in range(blocks):
                            start = block * LANES
                            part = (pl.ds(start, LANES), pl.ds(start, order - start))
                            diag_ref[part] = diag_ref[part] - update[(level, side) + part]

                for block in range(blocks):
                    rows = pl.ds(block * LANES, LANES)
                    for other in range(block + 1, blocks):
                        columns = pl.ds(other * LANES, LANES)
                        diag_ref[columns, rows] = diag_ref[rows, columns].T

        return carry

    def vel_wait(window):
        remote(
            vel_ref,
            next_vel.at[window],
            (vel_sems.at[0, window], vel_sems.at[1, window]),
            line,
        ).wait_recv()

    lax.fori_loop(0, levels + 1, factor_level, 0)

    def sol_copy(window, side):
        return remote(
            sol_out.at[window],
            sol_in.at[window, 1 - side],
            (sol_sems.at[0, window, side], sol_sems.at[1, window, 1 - side]),
            line + 2 * side - 1,
        )

    def sol_wait(window, side):
        remote(
            sol_out.at[window],
            sol_in.at[window, side],
            (sol_sems.at[0, window, side], sol_sems.at[1, window, side]),
            line,
        ).wait_recv()

    def advance(solution_row):
        new_accel = (
            accel_scale * (solution_row - disp_ref[...])
            - velocity_scale * vel_ref[...]
            - acc_ref[...]
        )
        vel_ref[...] = vel_ref[...] + half_step * (acc_ref[...] + new_accel)
        disp_ref[...] = solution_row
        acc_ref[...] = new_accel

    @pl.when(line > 0)
    def _():
        vel_copy(0).wait_send()

    def finish(window):
        @pl.when(core == 0)
        def _():
            advance(vec_mat(to_column(side_ref[...]), inverse_ref[...]))
            sol_out[window, :, :order] = disp_ref[...]
            sol_out[window, :, order : 2 * order] = vel_ref[...]
            sol_out[window, :, 2 * order :] = bad_ref[...]
            sol_copy(window, 1).start()

            @pl.when(line > 0)
            def _():
                sol_copy(window, 0).start()

        @pl.when(core == 1)
        def _():
            value = vec_mat(to_column(side_ref[...]), inverse_ref[...])
            sol_wait(window, 0)
            behind = mat_vec(scaled[0, 0], sol_in[window, 0, :, :order])
            side_ref[...] = value - to_row(behind)
            if window == 1:
                bad_ref[...] = sol_in[window, 0, :, 2 * order :]

            @pl.when(line < last)
            def _():
                sol_wait(window, 1)
                ahead = mat_vec(scaled[0, 1], sol_in[window, 1, :, :order])
                side_ref[...] = side_ref[...] - to_row(ahead)
                if window == 0:
                    next_vel[1] = sol_in[window, 1, :, order : 2 * order]

            advance(side_ref[...])
            if window == 0:
                vel_copy(1).start()

    finish(0)

    @pl.when(core == 0)
    def _():
        vel_wait(1)

    begin_loads(1)
    end_loads(1)

    def reduce_level(level, carry):
        send_vector(1, level)
        take_vector(1, level)
        return carry

    lax.fori_loop(0, levels, reduce_level, 0)

    @pl.when(core == 1)
    def _():
        vel_copy(1).wait_send()

    finish(1)
    bad_out[...] = bad_ref[...]

    lax.fori_loop(1, line_count, wind_left, 0)

    @pl.when(core == 0)
    def _():
        span_copy().wait_send()

    @pl.when(line < last)
    def _():
        map_copy().wait_send()

    for window in range(2):
        for turn in range(1, time_count):
            load_copy(window, turn).wait_send()

        @pl.when(line < last)
        def _():
            for turn in range(time_count, 2 * time_count):
                load_copy(window, turn).wait_send()

        @pl.when(core == 0)
        def _():
            sol_copy(window, 1).wait_send()

            @pl.when(line > 0)
            def _():
                sol_copy(window, 0).wait_send()

    def drain(level, carry):
        for window in range(2):
            for side in range(2):

                @pl.when(sends(level) & there(level, side))
                def _():
                    vec_copy(window, level, side).wait_send()

        return carry

    lax.fori_loop(0, levels, drain, 0)


def run_line(
    line_count,
    time_count,
    window_scale,
    segment_step,
    wind_field,
    mean_wind,
    drag,
    transfer,
    span_stiff,
    mass,
    disp0,
    vel0,
    acc0,
):
    order = span_stiff.shape[-1]
    width = mean_wind.shape[-1]
    levels = (line_count - 1).bit_length()
    row = jax.ShapeDtypeStruct((1, order), jnp.float32)

    def body(*refs):
        line_kernel(line_count, time_count, window_scale, levels, *refs)

    vmem = pl.BlockSpec(memory_space=pltpu.VMEM)
    dma = pltpu.SemaphoreType.DMA

    def buffer(*shape):
        return pltpu.VMEM(shape, jnp.float32)

    return pl.pallas_call(
        body,
        out_shape=(row, row, jax.ShapeDtypeStruct((1, LANES), jnp.float32)),
        in_specs=[pl.BlockSpec(memory_space=pltpu.SMEM)] + [vmem] * 9,
        out_specs=[vmem] * 3,
        scratch_shapes=[
            buffer(1, order),
            buffer(1, LANES),
            buffer(1, order),
            buffer(order, order),
            buffer(order, order),
            buffer(order, order),
            buffer(order, width),
            buffer(2, 1, order),
            buffer(levels, 2, order, order),
            buffer(levels, 2, order, order),
            buffer(levels, 2, order, order),
            buffer(2, order, order),
            buffer(order // time_count, order),
            buffer(2, levels, 2, 1, order + LANES),
            buffer(2, levels, 2, 1, order + LANES),
            buffer(2, 1, width),
            buffer(2, 2, time_count, 1, width),
            buffer(2, 1, 2 * order + LANES),
            buffer(2, 2, 1, 2 * order + LANES),
            dma((2,)),
            dma((2,)),
            dma((2, 2)),
            dma((2, levels, 2, order // LANES)),
            dma((2, levels, 2)),
            dma((levels, 2, time_count)),
            dma((levels, 2, time_count)),
            dma((2, 2, levels, 2)),
            dma((2, 2 * time_count)),
            dma((2, 2, time_count)),
            dma((2, 2, 2)),
            pltpu.VMEM(wind_field.shape, wind_field.dtype),
            dma((2, line_count)),
        ],
        compiler_params=pltpu.CompilerParams(
            collective_id=0, has_side_effects=True, vmem_limit_bytes=60 * 2**20
        ),
        cost_estimate=pl.CostEstimate(
            flops=100 * order**3, bytes_accessed=5 * 2**20, transcendentals=0
        ),
    )(segment_step, wind_field, mean_wind, drag, transfer, span_stiff, mass, disp0, vel0, acc0)


def local(
    gust_coef,
    mean_wind,
    drag,
    span_column,
    segment_step,
    transfer,
    span_stiff,
    mass,
    disp0,
    vel0,
    acc0,
):
    line_count = lax.axis_size("line")
    time_count = lax.axis_size("tm")
    time_pos = lax.axis_index("tm")
    span_count = span_column.shape[0]
    seg_count = segment_step.shape[0]
    trig_rows = trig_table(TS, KF)
    spectra = gust_coef.reshape(2 * KF, span_count * Q)
    wind_field = jnp.dot(trig_rows, spectra, preferred_element_type=jnp.float32).astype(
        jnp.bfloat16
    )
    wind_field = wind_field.reshape(TS, span_count, Q)
    wind_field = wind_field.at[:, span_column].get(mode="promise_in_bounds").transpose(1, 0, 2)
    window_scale = 1.0 / (TS * (seg_count // 2))
    fast_disp, fast_vel, bad = run_line(
        line_count,
        time_count,
        window_scale,
        segment_step,
        wind_field,
        mean_wind,
        drag,
        transfer,
        span_stiff,
        mass,
        disp0,
        vel0,
        acc0,
    )

    def checked():
        arrived = lax.all_to_all(wind_field, "line", split_axis=0, concat_axis=0, tiled=True)
        seg_index = jnp.arange(line_count, dtype=jnp.int32) * time_count + time_pos
        seg_flags = jnp.take(segment_step, seg_index)
        return checked_loop(
            line_count,
            time_count,
            arrived,
            seg_flags,
            mean_wind,
            drag,
            transfer,
            span_stiff,
            mass,
            disp0,
            vel0,
            acc0,
            window_scale,
        )

    return lax.cond(bad[0, 0] < 0.5, lambda: (fast_disp, fast_vel), checked)


def solution(mesh):
    return jax.shard_map(
        local,
        mesh=mesh,
        in_specs=(
            P(("line", "tm"), None, None, None),
            P("line", None),
            P("line", None),
            P(),
            P(),
            P("line", None, None, None),
            P("line", None, None),
            P("line", None),
            P("line", None),
            P("line", None),
            P("line", None),
        ),
        out_specs=(P("line", None), P("line", None)),
        check_vma=False,
    )
```

```python
import math

import jax
import jax.numpy as jnp
from jax import lax
from jax.experimental import pallas as pl
from jax.experimental.pallas import tpu as pltpu
from jax.sharding import PartitionSpec as P

Q = 256
KF = 64
TS = 64


accel_scale = 4.0
velocity_scale = 4.0
half_step = 0.5


def shifted(array, axis, by):
    length = lax.axis_size(axis)
    pairs = [(i, i + by) for i in range(length) if 0 <= i + by < length]
    return lax.ppermute(array, axis, pairs)


def exact_dot(first, second):
    return jnp.dot(
        first, second, precision=lax.Precision.HIGHEST, preferred_element_type=jnp.float32
    )


def trig_table(sample_count, freq_count):
    sample_index = jnp.arange(sample_count, dtype=jnp.float32)[:, None]
    frequency = (jnp.arange(freq_count, dtype=jnp.float32)[None, :] + 0.25) * (math.pi / freq_count)
    phase_angle = sample_index * frequency
    return jnp.concatenate([jnp.cos(phase_angle), jnp.sin(phase_angle)], axis=1).astype(
        jnp.bfloat16
    )


def cho_apply(factor, values):
    return jax.scipy.linalg.cho_solve((factor, True), values)


def blocked_cholesky(matrix):
    order = matrix.shape[0]
    panel_width = min(128, order)
    factor = jnp.zeros_like(matrix)
    trailing = matrix
    for start_row in range(0, order, panel_width):
        end_row = start_row + panel_width
        corner = jnp.linalg.cholesky(trailing[start_row:end_row, start_row:end_row])
        factor = factor.at[start_row:end_row, start_row:end_row].set(corner)
        if end_row < order:
            below = trailing[end_row:, start_row:end_row]
            below_factor = jax.scipy.linalg.solve_triangular(corner, below.T, lower=True).T
            factor = factor.at[end_row:, start_row:end_row].set(below_factor)
            trailing = trailing.at[end_row:, end_row:].add(-exact_dot(below_factor, below_factor.T))
    return factor


def checked_loop(
    line_count,
    time_count,
    arrived,
    seg_flags,
    mean_wind,
    drag,
    transfer,
    span_stiff,
    mass,
    disp0,
    vel0,
    acc0,
    window_scale,
):
    line_pos = lax.axis_index("line")
    block_order = span_stiff.shape[-1]
    left_map = transfer[0, 0]
    right_map = transfer[0, 1]
    span_block = span_stiff[0]
    before = shifted(span_block, "line", 1)
    identity = jnp.eye(block_order, dtype=jnp.float32)
    diag_block = span_block + before + (accel_scale * mass[0])[:, None] * identity
    coupled = (line_pos < line_count - 1).astype(jnp.float32)
    upper_block = -span_block * coupled
    lower_block = -before
    stored = []
    stride = 1
    while stride < line_count:
        factor = blocked_cholesky(diag_block)
        solved = cho_apply(factor, jnp.concatenate([lower_block, upper_block], axis=1))
        from_lower = shifted(solved, "line", stride)
        from_upper = shifted(solved, "line", -stride)
        new_diag = (
            diag_block
            - exact_dot(lower_block, from_lower[:, block_order:])
            - exact_dot(upper_block, from_upper[:, :block_order])
        )
        new_lower = -exact_dot(lower_block, from_lower[:, :block_order])
        new_upper = -exact_dot(upper_block, from_upper[:, block_order:])
        stored.append((factor, lower_block, upper_block))
        diag_block, lower_block, upper_block = (new_diag, new_lower, new_upper)
        stride = stride * 2
    final_factor = blocked_cholesky(diag_block)
    displacement, velocity, accel_now = (disp0, vel0, acc0)
    for window in range(2):
        next_velocity = shifted(velocity, "line", -1)
        offset = mean_wind - (exact_dot(velocity, left_map) + exact_dot(next_velocity, right_map))
        relative = arrived.astype(jnp.float32) + offset[None]
        weight = (seg_flags == window).astype(jnp.float32)
        window_partial_value = jnp.sum(
            weight[:, None, None] * relative * jnp.abs(relative), axis=(0, 1)
        )[None]
        summed = lax.psum(window_partial_value, "tm")
        span_load = drag * summed * window_scale
        passed = exact_dot(span_load, right_map.T)
        from_left = shifted(passed, "line", 1)
        force = exact_dot(span_load, left_map.T) + from_left
        right_side = force + mass * (
            accel_scale * displacement + velocity_scale * velocity + accel_now
        )
        vector = right_side[0]
        reach_now = 1
        for solve_factor, lower_one, upper_one in stored:
            solve_solved = cho_apply(solve_factor, vector)
            from_below = shifted(solve_solved, "line", reach_now)
            from_above = shifted(solve_solved, "line", -reach_now)
            vector = vector - exact_dot(lower_one, from_below) - exact_dot(upper_one, from_above)
            reach_now = reach_now * 2
        new_disp = cho_apply(final_factor, vector)[None]
        new_accel = accel_scale * (new_disp - displacement) - velocity_scale * velocity - accel_now
        velocity = velocity + half_step * (accel_now + new_accel)
        displacement, accel_now = (new_disp, new_accel)
    return (displacement, velocity)


MESH = pl.DeviceIdType.MESH


def halves(value):
    high = value.astype(jnp.bfloat16)
    return high, (value - high.astype(jnp.float32)).astype(jnp.bfloat16)


def split_dot(first, second, first_axis=1, second_axis=0):
    first_hi, first_lo = halves(first)
    second_hi, second_lo = halves(second)
    left = jnp.concatenate([first_hi, first_hi, first_lo], axis=first_axis)
    right = jnp.concatenate([second_hi, second_lo, second_hi], axis=second_axis)
    return lax.dot_general(
        left,
        right,
        (((first_axis,), (second_axis,)), ((), ())),
        preferred_element_type=jnp.float32,
    )


def single_dot(first, second):
    return jnp.dot(
        first.astype(jnp.bfloat16), second.astype(jnp.bfloat16), preferred_element_type=jnp.float32
    )


def eye_mask(order):
    rows = lax.broadcasted_iota(jnp.int32, (order, order), 0)
    return rows == lax.broadcasted_iota(jnp.int32, (order, order), 1)


LANES = 128


def to_column(row):
    mask = eye_mask(LANES)
    parts = [
        jnp.sum(jnp.where(mask, row[:, k : k + LANES], 0.0), axis=1, keepdims=True)
        for k in range(0, row.shape[1], LANES)
    ]
    return jnp.concatenate(parts, axis=0)


def to_row(column):
    mask = eye_mask(LANES)
    parts = [
        jnp.sum(jnp.where(mask, column[k : k + LANES], 0.0), axis=0, keepdims=True)
        for k in range(0, column.shape[0], LANES)
    ]
    return jnp.concatenate(parts, axis=1)


def vec_mat(column, matrix):
    return jnp.sum(column * matrix, axis=0, keepdims=True)


def mat_vec(matrix, row):
    return jnp.sum(matrix * row, axis=1, keepdims=True)


def newton_inverse(diag_ref, inverse_ref, bad_ref, bound_on_residual=0.03):
    order = diag_ref.shape[0]
    mask = eye_mask(order)
    diag = diag_ref[...]
    on_diag = jnp.where(mask, diag, 0.0)
    diag_row = jnp.sum(on_diag, axis=0, keepdims=True)
    diag_col = jnp.sum(on_diag, axis=1, keepdims=True)
    bound = jnp.max(
        jnp.sum(jnp.abs(diag), axis=0, keepdims=True) / diag_row, axis=1, keepdims=True
    )
    scale = jnp.minimum(1.0, 1.8 / bound)
    identity = jnp.where(mask, 1.0, 0.0)
    inverse_ref[...] = (scale / diag_col) * (2.0 * identity - diag * (scale / diag_row))
    current = inverse_ref[...]
    residual = identity - single_dot(diag_ref[...], current)
    estimate = (current + single_dot(current, residual)).astype(jnp.bfloat16)
    diag_hi, diag_lo = halves(diag_ref[...])
    residual = (
        identity
        - jnp.dot(diag_hi, estimate, preferred_element_type=jnp.float32)
        - jnp.dot(diag_lo, estimate, preferred_element_type=jnp.float32)
    )
    size = jnp.max(jnp.sum(jnp.abs(residual), axis=0, keepdims=True), axis=1, keepdims=True)
    bad_ref[...] = bad_ref[...] + jnp.where(size < bound_on_residual, 0.0, 1.0)
    series_hi, series_lo = halves(residual + single_dot(residual, residual))
    inverse_ref[...] = (
        estimate.astype(jnp.float32)
        + jnp.dot(estimate, series_hi, preferred_element_type=jnp.float32)
        + jnp.dot(estimate, series_lo, preferred_element_type=jnp.float32)
    )


def line_kernel(
    line_count,
    time_count,
    window_scale,
    levels,
    step_ref,
    sent_ref,
    mean_ref,
    drag_ref,
    maps_ref,
    span_ref,
    mass_ref,
    disp_in,
    vel_in,
    acc_in,
    disp_ref,
    vel_ref,
    bad_out,
    acc_ref,
    bad_ref,
    side_ref,
    diag_ref,
    inverse_ref,
    prev_span,
    prev_map,
    next_vel,
    couple,
    update,
    scaled,
    update_out,
    couple_out,
    vec_out,
    vec_in,
    load_out,
    load_in,
    sol_out,
    sol_in,
    span_sems,
    map_sems,
    vel_sems,
    update_sems,
    couple_sems,
    share_send_sems,
    share_recv_sems,
    vec_sems,
    load_send_sems,
    load_recv_sems,
    sol_sems,
    halfway,
    wind_ref,
    halfway_sems,
    wind_sems,
):
    line = lax.axis_index("line")
    time = lax.axis_index("tm")
    core = lax.rem(line, 2)
    order = span_ref.shape[1]
    last = line_count - 1

    barrier = pltpu.get_barrier_semaphore()
    partners = jnp.int32(0)
    for delta in (-1, 1):
        there = (line + delta >= 0) & (line + delta <= last)
        for turn in range(1, time_count):

            @pl.when(there)
            def _():
                pl.semaphore_signal(
                    barrier,
                    inc=1,
                    device_id=(line + delta, lax.rem(time + turn, time_count)),
                    device_id_type=MESH,
                )

        partners = partners + jnp.where(there, time_count - 1, 0)
    for turn in range(1, time_count):
        pl.semaphore_signal(
            barrier,
            inc=1,
            device_id=(line, lax.rem(time + turn, time_count)),
            device_id_type=MESH,
        )
    partners = partners + (time_count - 1)

    inner = max(2, line_count // 4)
    outer = line_count // inner
    place_x = lax.div(line, inner)
    place_y = lax.rem(line, inner)
    for turn in range(1, outer):
        pl.semaphore_signal(
            barrier,
            inc=1,
            device_id=(lax.rem(place_x + turn, outer) * inner + place_y, time),
            device_id_type=MESH,
        )
    for turn in range(1, inner):
        pl.semaphore_signal(
            barrier,
            inc=1,
            device_id=(place_x * inner + lax.rem(place_y + turn, inner), time),
            device_id_type=MESH,
        )
    partners = partners + (outer + inner - 2)
    stride = 1
    while stride < inner:
        for delta in (-stride, stride):
            near = (line + delta >= 0) & (line + delta <= last)
            if stride > 1:
                near = near & (core == 0)

            @pl.when(near)
            def _():
                pl.semaphore_signal(
                    barrier, inc=1, device_id=(line + delta, time), device_id_type=MESH
                )

            partners = partners + jnp.where(near, 1, 0)
        stride = stride * 2

    def remote(source, target, sems, to_line, to_time=None):
        return pltpu.make_async_remote_copy(
            src_ref=source,
            dst_ref=target,
            send_sem=sems[0],
            recv_sem=sems[1],
            device_id=(to_line, time if to_time is None else to_time),
            device_id_type=MESH,
        )

    def span_copy():
        return remote(span_ref.at[0], prev_span, (span_sems.at[0], span_sems.at[1]), line + 1)

    def map_copy():
        return remote(maps_ref.at[0, 1], prev_map, (map_sems.at[0], map_sems.at[1]), line + 1)

    def vel_copy(window):
        return remote(
            vel_ref,
            next_vel.at[window],
            (vel_sems.at[0, window], vel_sems.at[1, window]),
            line - 1,
        )

    blocks = order // LANES
    quarter = order // time_count

    def triangle(ref, block):
        start = block * LANES
        return ref.at[pl.ds(start, LANES), pl.ds(start, order - start)]

    def own_rows(ref, group):
        return ref.at[pl.ds(pl.multiple_of(group * quarter, quarter), quarter)]

    def update_copies(level, side):
        stride = jnp.left_shift(1, level)
        return [
            remote(
                triangle(update_out.at[side], block),
                triangle(update.at[level, 1 - side], block),
                (
                    update_sems.at[0, level, side, block],
                    update_sems.at[1, level, 1 - side, block],
                ),
                line + (2 * side - 1) * stride,
            )
            for block in range(blocks)
        ]

    def update_wait(level, side):
        for block in range(blocks):
            remote(
                triangle(update_out.at[side], block),
                triangle(update.at[level, side], block),
                (update_sems.at[0, level, side, block], update_sems.at[1, level, side, block]),
                line,
            ).wait_recv()

    def couple_copy(level, side):
        stride = jnp.left_shift(1, level)
        return remote(
            couple_out,
            own_rows(couple.at[level + 1, 1 - side], time),
            (couple_sems.at[0, level, side], couple_sems.at[1, level, 1 - side]),
            line + (2 * side - 1) * stride,
        )

    def couple_wait(level, side):
        remote(
            couple_out,
            own_rows(couple.at[level + 1, side], time),
            (couple_sems.at[0, level, side], couple_sems.at[1, level, side]),
            line,
        ).wait_recv()

    def share_copy(level, side, turn):
        rows = own_rows(couple.at[level + 1, side], time)
        return remote(
            rows,
            rows,
            (share_send_sems.at[level, side, turn], share_recv_sems.at[level, side, time]),
            line,
            lax.rem(time + turn, time_count),
        )

    def share_wait(level, side, turn):
        group = lax.rem(time + turn, time_count)
        rows = own_rows(couple.at[level + 1, side], group)
        remote(
            rows,
            rows,
            (share_send_sems.at[level, side, turn], share_recv_sems.at[level, side, group]),
            line,
        ).wait_recv()

    def vec_copy(window, level, side):
        stride = jnp.left_shift(1, level)
        return remote(
            vec_out.at[window, level, side],
            vec_in.at[window, level, 1 - side],
            (vec_sems.at[0, window, level, side], vec_sems.at[1, window, level, 1 - side]),
            line + (2 * side - 1) * stride,
        )

    def vec_wait(window, level, side):
        remote(
            vec_out.at[window, level, side],
            vec_in.at[window, level, side],
            (vec_sems.at[0, window, level, side], vec_sems.at[1, window, level, side]),
            line,
        ).wait_recv()

    def there(level, side):
        stride = jnp.left_shift(1, level)
        return (line - stride >= 0) if side == 0 else (line + stride <= last)

    def sends(level):
        return core == jnp.where(level == 0, 1, 0)

    vel_ref[...] = vel_in[...]
    disp_ref[...] = disp_in[...]
    acc_ref[...] = acc_in[...]
    bad_ref[...] = jnp.zeros_like(bad_ref)
    own_diag = jnp.where(eye_mask(order), accel_scale * to_column(mass_ref[...]), 0.0)
    diag_ref[...] = span_ref[0] + own_diag

    @pl.when(core == 1)
    def _():
        couple[0, 1] = -jnp.where(line < last, 1.0, 0.0) * span_ref[0]

    pl.semaphore_wait(barrier, partners)

    @pl.when(core == 0)
    def _():
        span_copy().start()

    @pl.when(line > 0)
    def _():
        vel_copy(0).start()

    @pl.when(line < last)
    def _():
        map_copy().start()

    @pl.when(line == last)
    def _():
        next_vel[...] = jnp.zeros_like(next_vel)

    def along_x(turn):
        to_x = lax.rem(place_x + turn, outer)
        return remote(
            sent_ref.at[pl.ds(pl.multiple_of(to_x * inner, inner), inner)],
            halfway.at[place_x],
            (halfway_sems.at[0, to_x], halfway_sems.at[1, place_x]),
            to_x * inner + place_y,
        )

    def along_x_wait(turn):
        from_x = lax.rem(place_x + turn, outer)
        remote(
            sent_ref.at[pl.ds(pl.multiple_of(from_x * inner, inner), inner)],
            halfway.at[from_x],
            (halfway_sems.at[0, from_x], halfway_sems.at[1, from_x]),
            line,
        ).wait_recv()

    def along_y(turn):
        to_y = lax.rem(place_y + turn, inner)
        return remote(
            halfway.at[:, to_y],
            wind_ref.at[:, place_y],
            (wind_sems.at[0, to_y], wind_sems.at[1, place_y]),
            place_x * inner + to_y,
        )

    def along_y_wait(turn):
        from_y = lax.rem(place_y + turn, inner)
        remote(
            halfway.at[:, from_y],
            wind_ref.at[:, from_y],
            (wind_sems.at[0, from_y], wind_sems.at[1, from_y]),
            line,
        ).wait_recv()

    for turn in range(1, outer):
        along_x(turn).start()
    halfway[place_x] = sent_ref[pl.ds(pl.multiple_of(place_x * inner, inner), inner)]

    @pl.when(core == 1)
    def _():
        span_copy().wait_recv()
        diag_ref[...] = diag_ref[...] + prev_span[...]
        couple[0, 0] = -prev_span[...]

    def load_copy(window, turn):
        step = 0 if turn < time_count else 1
        return remote(
            load_out.at[window],
            load_in.at[window, step, time],
            (load_send_sems.at[window, turn], load_recv_sems.at[window, step, time]),
            line + step,
            lax.rem(time + turn, time_count),
        )

    def load_wait(window, step, group):
        remote(
            load_out.at[window],
            load_in.at[window, step, group],
            (load_send_sems.at[window, 0], load_recv_sems.at[window, step, group]),
            line,
        ).wait_recv()

    def begin_loads(window):
        velocity_col = to_column(vel_ref[...])
        next_col = to_column(next_vel[window])
        interior = vec_mat(velocity_col, maps_ref[0, 0]) + vec_mat(next_col, maps_ref[0, 1])
        offset = mean_ref[...] - interior
        samples, width = wind_ref.shape[2:]

        def add(group, total):
            field = wind_ref[lax.div(group, inner), lax.rem(group, inner)]
            relative = field.astype(jnp.float32) + offset
            step = step_ref[group * time_count + time].astype(jnp.float32)
            return total + (step if window == 1 else 1.0 - step) * (relative * jnp.abs(relative))

        total = lax.fori_loop(0, line_count, add, jnp.zeros((samples, width), jnp.float32))
        load = drag_ref[...] * jnp.sum(total, axis=0, keepdims=True) * window_scale
        load_out[window] = load
        load_in[window, 0, time] = load
        for turn in range(1, time_count):
            load_copy(window, turn).start()

        @pl.when(line < last)
        def _():
            for turn in range(time_count, 2 * time_count):
                load_copy(window, turn).start()

    def end_loads(window):
        for turn in range(1, time_count):
            load_wait(window, 0, lax.rem(time + turn, time_count))

        @pl.when(line > 0)
        def _():
            for turn in range(time_count):
                load_wait(window, 1, lax.rem(time + turn, time_count))

        def summed(step):
            total = load_in[window, step, 0]
            for group in range(1, time_count):
                total = total + load_in[window, step, group]
            return total

        inertia = mass_ref[...] * (
            accel_scale * disp_ref[...] + velocity_scale * vel_ref[...] + acc_ref[...]
        )
        side_ref[...] = inertia + to_row(mat_vec(maps_ref[0, 0], summed(0)))

        @pl.when(line > 0)
        def _():
            if window == 0:
                map_copy().wait_recv()
            side_ref[...] = side_ref[...] + to_row(mat_vec(prev_map[...], summed(1)))

    def send_vector(window, level):
        @pl.when(sends(level))
        def _():
            column = to_column(side_ref[...])
            for side in range(2):

                @pl.when(there(level, side))
                def _():
                    vec_out[window, level, side, :, :order] = vec_mat(column, scaled[level, side])
                    vec_out[window, level, side, :, order:] = bad_ref[...]
                    vec_copy(window, level, side).start()

    def take_vector(window, level):
        @pl.when(core == 0)
        def _():
            for side in range(2):

                @pl.when(there(level, side))
                def _():
                    vec_wait(window, level, side)
                    side_ref[...] = side_ref[...] - vec_in[window, level, side, :, :order]
                    if window == 1:
                        bad_ref[...] = bad_ref[...] + vec_in[window, level, side, :, order:]

    def loads_left(window):
        for turn in range(1, time_count):
            load_copy(window, turn).wait_send()

        @pl.when(line < last)
        def _():
            for turn in range(time_count, 2 * time_count):
                load_copy(window, turn).wait_send()

    def vectors_left(window, level):
        for side in range(2):

            @pl.when(sends(level) & there(level, side))
            def _():
                vec_copy(window, level, side).wait_send()

    def factor_level(level, carry):
        before = jnp.maximum(level - 1, 0)

        @pl.when(level == levels)
        def _():
            send_vector(0, before)

        @pl.when(sends(level))
        def _():
            newton_inverse(diag_ref, inverse_ref, bad_ref)

        for side in range(2):
            sent = (level >= 1) & sends(before) & there(before, side)

            @pl.when(sent)
            def _():
                for copy in update_copies(before, side):
                    copy.wait_send()

            @pl.when(sent & (level < levels))
            def _():
                couple_copy(before, side).wait_send()

        def coupling(side):
            expected = (level >= 1) & (core == 0)

            @pl.when(expected & there(before, side))
            def _():
                for turn in range(1, time_count):
                    share_wait(before, side, turn)
                    share_copy(before, side, turn).wait_send()

            @pl.when(expected & jnp.logical_not(there(before, side)))
            def _():
                couple[level, side] = jnp.zeros((order, order), jnp.float32)

        @pl.when(sends(level) & (level < levels))
        def _():
            coupling(0)

            @pl.when(there(level, 0))
            def _():
                scaled[level, 0] = split_dot(inverse_ref[...], couple[level, 0], 1, 1)

            coupling(1)

            @pl.when(there(level, 1))
            def _():
                scaled[level, 1] = split_dot(inverse_ref[...], couple[level, 1])

            @pl.when(level < levels - 1)
            def _():
                rows = pl.ds(pl.multiple_of(time * quarter, quarter), quarter)
                both = there(level, 0) & there(level, 1)

                @pl.when(both)
                def _():
                    couple_out[...] = -split_dot(couple[level, 0, rows], scaled[level, 1])

                @pl.when(jnp.logical_not(both))
                def _():
                    couple_out[...] = jnp.zeros_like(couple_out)

                for side in range(2):

                    @pl.when(there(level, side))
                    def _():
                        couple_copy(level, side).start()

            @pl.when(there(level, 0))
            def _():
                update_out[0] = split_dot(couple[level, 0], scaled[level, 0])
                for copy in update_copies(level, 0):
                    copy.start()

            @pl.when(there(level, 1))
            def _():
                own = jnp.where(level == 0, 1.0, 0.0)
                update_out[1] = (
                    split_dot(couple[level, 1], scaled[level, 1], 0, 0) - own * span_ref[0]
                )
                for copy in update_copies(level, 1):
                    copy.start()

        @pl.when(level == 0)
        def _():
            for turn in range(1, outer):
                along_x_wait(turn)
            for turn in range(1, inner):
                along_y(turn).start()
            wind_ref[:, place_y] = halfway[:, place_y]

        for side in range(2):

            @pl.when((level < levels - 1) & (core == 0) & there(level, side))
            def _():
                couple_wait(level, side)
                for turn in range(1, time_count):
                    share_copy(level, side, turn).start()

        @pl.when(level == 1)
        def _():
            @pl.when(line < last)
            def _():
                vel_wait(0)

            for turn in range(1, inner):
                along_y_wait(turn)
            begin_loads(0)
            end_loads(0)

        @pl.when(level == 2)
        def _():
            for turn in range(1, outer):
                along_x(turn).wait_send()
            for turn in range(1, inner):
                along_y(turn).wait_send()
            loads_left(0)

            @pl.when(core == 0)
            def _():
                span_copy().wait_send()

            @pl.when(line < last)
            def _():
                map_copy().wait_send()

        @pl.when(level >= 2)
        def _():
            vectors_left(0, level - 2)

        @pl.when((level >= 1) & (level < levels))
        def _():
            send_vector(0, before)

        @pl.when(level >= 1)
        def _():
            take_vector(0, before)

        @pl.when(level < levels)
        def _():
            @pl.when(core == 0)
            def _():
                for side in range(2):

                    @pl.when(there(level, side))
                    def _():
                        update_wait(level, side)
                        for block in range(blocks):
                            start = block * LANES
                            part = (pl.ds(start, LANES), pl.ds(start, order - start))
                            diag_ref[part] = diag_ref[part] - update[(level, side) + part]

                for block in range(blocks):
                    rows = pl.ds(block * LANES, LANES)
                    for other in range(block + 1, blocks):
                        columns = pl.ds(other * LANES, LANES)
                        diag_ref[columns, rows] = diag_ref[rows, columns].T

        return carry

    def vel_wait(window):
        remote(
            vel_ref,
            next_vel.at[window],
            (vel_sems.at[0, window], vel_sems.at[1, window]),
            line,
        ).wait_recv()

    lax.fori_loop(0, levels + 1, factor_level, 0)

    def sol_copy(window, side):
        return remote(
            sol_out.at[window],
            sol_in.at[window, 1 - side],
            (sol_sems.at[0, window, side], sol_sems.at[1, window, 1 - side]),
            line + 2 * side - 1,
        )

    def sol_wait(window, side):
        remote(
            sol_out.at[window],
            sol_in.at[window, side],
            (sol_sems.at[0, window, side], sol_sems.at[1, window, side]),
            line,
        ).wait_recv()

    def advance(solution_row):
        new_accel = (
            accel_scale * (solution_row - disp_ref[...])
            - velocity_scale * vel_ref[...]
            - acc_ref[...]
        )
        vel_ref[...] = vel_ref[...] + half_step * (acc_ref[...] + new_accel)
        disp_ref[...] = solution_row
        acc_ref[...] = new_accel

    @pl.when(line > 0)
    def _():
        vel_copy(0).wait_send()

    def finish(window):
        @pl.when(core == 0)
        def _():
            advance(vec_mat(to_column(side_ref[...]), inverse_ref[...]))
            sol_out[window, :, :order] = disp_ref[...]
            sol_out[window, :, order : 2 * order] = vel_ref[...]
            sol_out[window, :, 2 * order :] = bad_ref[...]
            sol_copy(window, 1).start()

            @pl.when(line > 0)
            def _():
                sol_copy(window, 0).start()

        @pl.when(core == 1)
        def _():
            value = vec_mat(to_column(side_ref[...]), inverse_ref[...])
            sol_wait(window, 0)
            behind = mat_vec(scaled[0, 0], sol_in[window, 0, :, :order])
            side_ref[...] = value - to_row(behind)
            if window == 1:
                bad_ref[...] = sol_in[window, 0, :, 2 * order :]

            @pl.when(line < last)
            def _():
                sol_wait(window, 1)
                ahead = mat_vec(scaled[0, 1], sol_in[window, 1, :, :order])
                side_ref[...] = side_ref[...] - to_row(ahead)
                if window == 0:
                    next_vel[1] = sol_in[window, 1, :, order : 2 * order]

            advance(side_ref[...])
            if window == 0:
                vel_copy(1).start()

    finish(0)

    @pl.when(core == 0)
    def _():
        vel_wait(1)

    begin_loads(1)
    end_loads(1)

    def reduce_level(level, carry):
        send_vector(1, level)
        take_vector(1, level)
        return carry

    lax.fori_loop(0, levels, reduce_level, 0)

    @pl.when(core == 1)
    def _():
        vel_copy(1).wait_send()

    finish(1)
    bad_out[...] = bad_ref[...]

    loads_left(1)

    for window in range(2):

        @pl.when(core == 0)
        def _():
            sol_copy(window, 1).wait_send()

            @pl.when(line > 0)
            def _():
                sol_copy(window, 0).wait_send()

    vectors_left(0, levels - 1)

    def drain(level, carry):
        vectors_left(1, level)
        return carry

    lax.fori_loop(0, levels, drain, 0)


def run_line(
    line_count,
    time_count,
    window_scale,
    segment_step,
    wind_field,
    mean_wind,
    drag,
    transfer,
    span_stiff,
    mass,
    disp0,
    vel0,
    acc0,
):
    order = span_stiff.shape[-1]
    width = mean_wind.shape[-1]
    levels = (line_count - 1).bit_length()
    row = jax.ShapeDtypeStruct((1, order), jnp.float32)
    inner = max(2, line_count // 4)
    outer = line_count // inner

    def body(*refs):
        line_kernel(line_count, time_count, window_scale, levels, *refs)

    vmem = pl.BlockSpec(memory_space=pltpu.VMEM)
    dma = pltpu.SemaphoreType.DMA

    def buffer(*shape):
        return pltpu.VMEM(shape, jnp.float32)

    return pl.pallas_call(
        body,
        out_shape=(row, row, jax.ShapeDtypeStruct((1, LANES), jnp.float32)),
        in_specs=[pl.BlockSpec(memory_space=pltpu.SMEM)] + [vmem] * 9,
        out_specs=[vmem] * 3,
        scratch_shapes=[
            buffer(1, order),
            buffer(1, LANES),
            buffer(1, order),
            buffer(order, order),
            buffer(order, order),
            buffer(order, order),
            buffer(order, width),
            buffer(2, 1, order),
            buffer(levels, 2, order, order),
            buffer(levels, 2, order, order),
            buffer(levels, 2, order, order),
            buffer(2, order, order),
            buffer(order // time_count, order),
            buffer(2, levels, 2, 1, order + LANES),
            buffer(2, levels, 2, 1, order + LANES),
            buffer(2, 1, width),
            buffer(2, 2, time_count, 1, width),
            buffer(2, 1, 2 * order + LANES),
            buffer(2, 2, 1, 2 * order + LANES),
            dma((2,)),
            dma((2,)),
            dma((2, 2)),
            dma((2, levels, 2, order // LANES)),
            dma((2, levels, 2)),
            dma((levels, 2, time_count)),
            dma((levels, 2, time_count)),
            dma((2, 2, levels, 2)),
            dma((2, 2 * time_count)),
            dma((2, 2, time_count)),
            dma((2, 2, 2)),
            pltpu.VMEM((outer, inner) + wind_field.shape[1:], wind_field.dtype),
            pltpu.VMEM((outer, inner) + wind_field.shape[1:], wind_field.dtype),
            dma((2, outer)),
            dma((2, inner)),
        ],
        compiler_params=pltpu.CompilerParams(
            collective_id=0, has_side_effects=True, vmem_limit_bytes=60 * 2**20
        ),
        cost_estimate=pl.CostEstimate(
            flops=100 * order**3, bytes_accessed=5 * 2**20, transcendentals=0
        ),
    )(segment_step, wind_field, mean_wind, drag, transfer, span_stiff, mass, disp0, vel0, acc0)


def local(
    gust_coef,
    mean_wind,
    drag,
    span_column,
    segment_step,
    transfer,
    span_stiff,
    mass,
    disp0,
    vel0,
    acc0,
):
    line_count = lax.axis_size("line")
    time_count = lax.axis_size("tm")
    time_pos = lax.axis_index("tm")
    span_count = span_column.shape[0]
    seg_count = segment_step.shape[0]
    trig_rows = trig_table(TS, KF)
    spectra = gust_coef.reshape(2 * KF, span_count * Q)
    wind_field = jnp.dot(trig_rows, spectra, preferred_element_type=jnp.float32).astype(
        jnp.bfloat16
    )
    wind_field = wind_field.reshape(TS, span_count, Q)
    wind_field = wind_field.at[:, span_column].get(mode="promise_in_bounds").transpose(1, 0, 2)
    window_scale = 1.0 / (TS * (seg_count // 2))
    fast_disp, fast_vel, bad = run_line(
        line_count,
        time_count,
        window_scale,
        segment_step,
        wind_field,
        mean_wind,
        drag,
        transfer,
        span_stiff,
        mass,
        disp0,
        vel0,
        acc0,
    )

    def checked():
        arrived = lax.all_to_all(wind_field, "line", split_axis=0, concat_axis=0, tiled=True)
        seg_index = jnp.arange(line_count, dtype=jnp.int32) * time_count + time_pos
        seg_flags = jnp.take(segment_step, seg_index)
        return checked_loop(
            line_count,
            time_count,
            arrived,
            seg_flags,
            mean_wind,
            drag,
            transfer,
            span_stiff,
            mass,
            disp0,
            vel0,
            acc0,
            window_scale,
        )

    return lax.cond(bad[0, 0] < 0.5, lambda: (fast_disp, fast_vel), checked)


def solution(mesh):
    return jax.shard_map(
        local,
        mesh=mesh,
        in_specs=(
            P(("line", "tm"), None, None, None),
            P("line", None),
            P("line", None),
            P(),
            P(),
            P("line", None, None, None),
            P("line", None, None),
            P("line", None),
            P("line", None),
            P("line", None),
            P("line", None),
        ),
        out_specs=(P("line", None), P("line", None)),
        check_vma=False,
    )
```

```python
import math

import jax
import jax.numpy as jnp
from jax import lax
from jax.experimental import pallas as pl
from jax.experimental.pallas import tpu as pltpu
from jax.sharding import PartitionSpec as P

Q = 256
KF = 64
TS = 64


accel_scale = 4.0
velocity_scale = 4.0
half_step = 0.5


def shifted(array, axis, by):
    length = lax.axis_size(axis)
    pairs = [(i, i + by) for i in range(length) if 0 <= i + by < length]
    return lax.ppermute(array, axis, pairs)


def exact_dot(first, second):
    return jnp.dot(
        first, second, precision=lax.Precision.HIGHEST, preferred_element_type=jnp.float32
    )


def trig_table(sample_count, freq_count):
    sample_index = jnp.arange(sample_count, dtype=jnp.float32)[:, None]
    frequency = (jnp.arange(freq_count, dtype=jnp.float32)[None, :] + 0.25) * (math.pi / freq_count)
    phase_angle = sample_index * frequency
    return jnp.concatenate([jnp.cos(phase_angle), jnp.sin(phase_angle)], axis=1).astype(
        jnp.bfloat16
    )


def cho_apply(factor, values):
    return jax.scipy.linalg.cho_solve((factor, True), values)


def blocked_cholesky(matrix):
    order = matrix.shape[0]
    panel_width = min(128, order)
    factor = jnp.zeros_like(matrix)
    trailing = matrix
    for start_row in range(0, order, panel_width):
        end_row = start_row + panel_width
        corner = jnp.linalg.cholesky(trailing[start_row:end_row, start_row:end_row])
        factor = factor.at[start_row:end_row, start_row:end_row].set(corner)
        if end_row < order:
            below = trailing[end_row:, start_row:end_row]
            below_factor = jax.scipy.linalg.solve_triangular(corner, below.T, lower=True).T
            factor = factor.at[end_row:, start_row:end_row].set(below_factor)
            trailing = trailing.at[end_row:, end_row:].add(-exact_dot(below_factor, below_factor.T))
    return factor


def checked_loop(
    line_count,
    time_count,
    arrived,
    seg_flags,
    mean_wind,
    drag,
    transfer,
    span_stiff,
    mass,
    disp0,
    vel0,
    acc0,
    window_scale,
):
    line_pos = lax.axis_index("line")
    block_order = span_stiff.shape[-1]
    left_map = transfer[0, 0]
    right_map = transfer[0, 1]
    span_block = span_stiff[0]
    before = shifted(span_block, "line", 1)
    identity = jnp.eye(block_order, dtype=jnp.float32)
    diag_block = span_block + before + (accel_scale * mass[0])[:, None] * identity
    coupled = (line_pos < line_count - 1).astype(jnp.float32)
    upper_block = -span_block * coupled
    lower_block = -before
    stored = []
    stride = 1
    while stride < line_count:
        factor = blocked_cholesky(diag_block)
        solved = cho_apply(factor, jnp.concatenate([lower_block, upper_block], axis=1))
        from_lower = shifted(solved, "line", stride)
        from_upper = shifted(solved, "line", -stride)
        new_diag = (
            diag_block
            - exact_dot(lower_block, from_lower[:, block_order:])
            - exact_dot(upper_block, from_upper[:, :block_order])
        )
        new_lower = -exact_dot(lower_block, from_lower[:, :block_order])
        new_upper = -exact_dot(upper_block, from_upper[:, block_order:])
        stored.append((factor, lower_block, upper_block))
        diag_block, lower_block, upper_block = (new_diag, new_lower, new_upper)
        stride = stride * 2
    final_factor = blocked_cholesky(diag_block)
    displacement, velocity, accel_now = (disp0, vel0, acc0)
    for window in range(2):
        next_velocity = shifted(velocity, "line", -1)
        offset = mean_wind - (exact_dot(velocity, left_map) + exact_dot(next_velocity, right_map))
        relative = arrived.astype(jnp.float32) + offset[None]
        weight = (seg_flags == window).astype(jnp.float32)
        window_partial_value = jnp.sum(
            weight[:, None, None] * relative * jnp.abs(relative), axis=(0, 1)
        )[None]
        summed = lax.psum(window_partial_value, "tm")
        span_load = drag * summed * window_scale
        passed = exact_dot(span_load, right_map.T)
        from_left = shifted(passed, "line", 1)
        force = exact_dot(span_load, left_map.T) + from_left
        right_side = force + mass * (
            accel_scale * displacement + velocity_scale * velocity + accel_now
        )
        vector = right_side[0]
        reach_now = 1
        for solve_factor, lower_one, upper_one in stored:
            solve_solved = cho_apply(solve_factor, vector)
            from_below = shifted(solve_solved, "line", reach_now)
            from_above = shifted(solve_solved, "line", -reach_now)
            vector = vector - exact_dot(lower_one, from_below) - exact_dot(upper_one, from_above)
            reach_now = reach_now * 2
        new_disp = cho_apply(final_factor, vector)[None]
        new_accel = accel_scale * (new_disp - displacement) - velocity_scale * velocity - accel_now
        velocity = velocity + half_step * (accel_now + new_accel)
        displacement, accel_now = (new_disp, new_accel)
    return (displacement, velocity)


MESH = pl.DeviceIdType.MESH


def halves(value):
    high = value.astype(jnp.bfloat16)
    return high, (value - high.astype(jnp.float32)).astype(jnp.bfloat16)


def split_dot(first, second, first_axis=1, second_axis=0):
    first_hi, first_lo = halves(first)
    second_hi, second_lo = halves(second)
    left = jnp.concatenate([first_hi, first_hi, first_lo], axis=first_axis)
    right = jnp.concatenate([second_hi, second_lo, second_hi], axis=second_axis)
    return lax.dot_general(
        left,
        right,
        (((first_axis,), (second_axis,)), ((), ())),
        preferred_element_type=jnp.float32,
    )


def single_dot(first, second):
    return jnp.dot(
        first.astype(jnp.bfloat16), second.astype(jnp.bfloat16), preferred_element_type=jnp.float32
    )


def eye_mask(order):
    rows = lax.broadcasted_iota(jnp.int32, (order, order), 0)
    return rows == lax.broadcasted_iota(jnp.int32, (order, order), 1)


LANES = 128


def to_column(row):
    mask = eye_mask(LANES)
    parts = [
        jnp.sum(jnp.where(mask, row[:, k : k + LANES], 0.0), axis=1, keepdims=True)
        for k in range(0, row.shape[1], LANES)
    ]
    return jnp.concatenate(parts, axis=0)


def to_row(column):
    mask = eye_mask(LANES)
    parts = [
        jnp.sum(jnp.where(mask, column[k : k + LANES], 0.0), axis=0, keepdims=True)
        for k in range(0, column.shape[0], LANES)
    ]
    return jnp.concatenate(parts, axis=1)


def vec_mat(column, matrix):
    return jnp.sum(column * matrix, axis=0, keepdims=True)


def mat_vec(matrix, row):
    return jnp.sum(matrix * row, axis=1, keepdims=True)


def newton_inverse(diag_ref, inverse_ref, bad_ref, bound_on_residual=0.03):
    order = diag_ref.shape[0]
    mask = eye_mask(order)
    diag = diag_ref[...]
    on_diag = jnp.where(mask, diag, 0.0)
    diag_row = jnp.sum(on_diag, axis=0, keepdims=True)
    diag_col = jnp.sum(on_diag, axis=1, keepdims=True)
    bound = jnp.max(
        jnp.sum(jnp.abs(diag), axis=0, keepdims=True) / diag_row, axis=1, keepdims=True
    )
    scale = jnp.minimum(1.0, 1.8 / bound)
    identity = jnp.where(mask, 1.0, 0.0)
    inverse_ref[...] = (scale / diag_col) * (2.0 * identity - diag * (scale / diag_row))
    current = inverse_ref[...]
    residual = identity - single_dot(diag_ref[...], current)
    estimate = (current + single_dot(current, residual)).astype(jnp.bfloat16)
    diag_hi, diag_lo = halves(diag_ref[...])
    residual = (
        identity
        - jnp.dot(diag_hi, estimate, preferred_element_type=jnp.float32)
        - jnp.dot(diag_lo, estimate, preferred_element_type=jnp.float32)
    )
    size = jnp.max(jnp.sum(jnp.abs(residual), axis=0, keepdims=True), axis=1, keepdims=True)
    bad_ref[...] = bad_ref[...] + jnp.where(size < bound_on_residual, 0.0, 1.0)
    series_hi, series_lo = halves(residual + single_dot(residual, residual))
    inverse_ref[...] = (
        estimate.astype(jnp.float32)
        + jnp.dot(estimate, series_hi, preferred_element_type=jnp.float32)
        + jnp.dot(estimate, series_lo, preferred_element_type=jnp.float32)
    )


def line_kernel(
    line_count,
    time_count,
    window_scale,
    levels,
    step_ref,
    sent_ref,
    mean_ref,
    drag_ref,
    maps_ref,
    span_ref,
    mass_ref,
    disp_in,
    vel_in,
    acc_in,
    disp_ref,
    vel_ref,
    bad_out,
    acc_ref,
    bad_ref,
    side_ref,
    diag_ref,
    inverse_ref,
    prev_span,
    prev_map,
    next_vel,
    couple,
    update,
    scaled,
    update_out,
    couple_out,
    vec_out,
    vec_in,
    load_out,
    load_in,
    sol_out,
    sol_in,
    span_sems,
    map_sems,
    vel_sems,
    update_sems,
    couple_sems,
    share_send_sems,
    share_recv_sems,
    vec_sems,
    load_send_sems,
    load_recv_sems,
    sol_sems,
    halfway,
    wind_ref,
    halfway_sems,
    wind_sems,
):
    line = lax.axis_index("line")
    time = lax.axis_index("tm")
    core = lax.rem(line, 2)
    order = span_ref.shape[1]
    last = line_count - 1

    barrier = pltpu.get_barrier_semaphore()
    partners = jnp.int32(0)
    for delta in (-1, 1):
        there = (line + delta >= 0) & (line + delta <= last)
        for turn in range(1, time_count):

            @pl.when(there)
            def _():
                pl.semaphore_signal(
                    barrier,
                    inc=1,
                    device_id=(line + delta, lax.rem(time + turn, time_count)),
                    device_id_type=MESH,
                )

        partners = partners + jnp.where(there, time_count - 1, 0)
    for turn in range(1, time_count):
        pl.semaphore_signal(
            barrier,
            inc=1,
            device_id=(line, lax.rem(time + turn, time_count)),
            device_id_type=MESH,
        )
    partners = partners + (time_count - 1)

    inner = max(2, line_count // 4)
    outer = line_count // inner
    place_x = lax.div(line, inner)
    place_y = lax.rem(line, inner)
    for turn in range(1, outer):
        pl.semaphore_signal(
            barrier,
            inc=1,
            device_id=(lax.rem(place_x + turn, outer) * inner + place_y, time),
            device_id_type=MESH,
        )
    for turn in range(1, inner):
        pl.semaphore_signal(
            barrier,
            inc=1,
            device_id=(place_x * inner + lax.rem(place_y + turn, inner), time),
            device_id_type=MESH,
        )
    partners = partners + (outer + inner - 2)
    stride = 1
    while stride < inner:
        for delta in (-stride, stride):
            near = (line + delta >= 0) & (line + delta <= last)
            if stride > 1:
                near = near & (core == 0)

            @pl.when(near)
            def _():
                pl.semaphore_signal(
                    barrier, inc=1, device_id=(line + delta, time), device_id_type=MESH
                )

            partners = partners + jnp.where(near, 1, 0)
        stride = stride * 2

    def remote(source, target, sems, to_line, to_time=None):
        return pltpu.make_async_remote_copy(
            src_ref=source,
            dst_ref=target,
            send_sem=sems[0],
            recv_sem=sems[1],
            device_id=(to_line, time if to_time is None else to_time),
            device_id_type=MESH,
        )

    def span_copy():
        return remote(span_ref.at[0], prev_span, (span_sems.at[0], span_sems.at[1]), line + 1)

    def map_copy():
        return remote(maps_ref.at[0, 1], prev_map, (map_sems.at[0], map_sems.at[1]), line + 1)

    def vel_copy(window):
        return remote(
            vel_ref,
            next_vel.at[window],
            (vel_sems.at[0, window], vel_sems.at[1, window]),
            line - 1,
        )

    blocks = order // LANES
    quarter = order // time_count

    def triangle(ref, block):
        start = block * LANES
        return ref.at[pl.ds(start, LANES), pl.ds(start, order - start)]

    def own_rows(ref, group):
        return ref.at[pl.ds(pl.multiple_of(group * quarter, quarter), quarter)]

    def update_copies(level, side):
        stride = jnp.left_shift(1, level)
        return [
            remote(
                triangle(update_out.at[side], block),
                triangle(update.at[level, 1 - side], block),
                (
                    update_sems.at[0, level, side, block],
                    update_sems.at[1, level, 1 - side, block],
                ),
                line + (2 * side - 1) * stride,
            )
            for block in range(blocks)
        ]

    def update_wait(level, side):
        for block in range(blocks):
            remote(
                triangle(update_out.at[side], block),
                triangle(update.at[level, side], block),
                (update_sems.at[0, level, side, block], update_sems.at[1, level, side, block]),
                line,
            ).wait_recv()

    def couple_copy(level, side):
        stride = jnp.left_shift(1, level)
        return remote(
            couple_out,
            own_rows(couple.at[level + 1, 1 - side], time),
            (couple_sems.at[0, level, side], couple_sems.at[1, level, 1 - side]),
            line + (2 * side - 1) * stride,
        )

    def couple_wait(level, side):
        remote(
            couple_out,
            own_rows(couple.at[level + 1, side], time),
            (couple_sems.at[0, level, side], couple_sems.at[1, level, side]),
            line,
        ).wait_recv()

    def share_copy(level, side, turn):
        rows = own_rows(couple.at[level + 1, side], time)
        return remote(
            rows,
            rows,
            (share_send_sems.at[level, side, turn], share_recv_sems.at[level, side, time]),
            line,
            lax.rem(time + turn, time_count),
        )

    def share_wait(level, side, turn):
        group = lax.rem(time + turn, time_count)
        rows = own_rows(couple.at[level + 1, side], group)
        remote(
            rows,
            rows,
            (share_send_sems.at[level, side, turn], share_recv_sems.at[level, side, group]),
            line,
        ).wait_recv()

    def vec_copy(window, level, side):
        stride = jnp.left_shift(1, level)
        return remote(
            vec_out.at[window, level, side],
            vec_in.at[window, level, 1 - side],
            (vec_sems.at[0, window, level, side], vec_sems.at[1, window, level, 1 - side]),
            line + (2 * side - 1) * stride,
        )

    def vec_wait(window, level, side):
        remote(
            vec_out.at[window, level, side],
            vec_in.at[window, level, side],
            (vec_sems.at[0, window, level, side], vec_sems.at[1, window, level, side]),
            line,
        ).wait_recv()

    def there(level, side):
        stride = jnp.left_shift(1, level)
        return (line - stride >= 0) if side == 0 else (line + stride <= last)

    def sends(level):
        return core == jnp.where(level == 0, 1, 0)

    vel_ref[...] = vel_in[...]
    disp_ref[...] = disp_in[...]
    acc_ref[...] = acc_in[...]
    bad_ref[...] = jnp.zeros_like(bad_ref)
    own_diag = jnp.where(eye_mask(order), accel_scale * to_column(mass_ref[...]), 0.0)
    diag_ref[...] = span_ref[0] + own_diag

    @pl.when(core == 1)
    def _():
        couple[0, 1] = -jnp.where(line < last, 1.0, 0.0) * span_ref[0]

    pl.semaphore_wait(barrier, partners)

    @pl.when(core == 0)
    def _():
        span_copy().start()

    @pl.when(line > 0)
    def _():
        vel_copy(0).start()

    @pl.when(line < last)
    def _():
        map_copy().start()

    @pl.when(line == last)
    def _():
        next_vel[...] = jnp.zeros_like(next_vel)

    def along_y(turn):
        to_y = lax.rem(place_y + turn, inner)
        return remote(
            sent_ref.at[:, to_y],
            halfway.at[:, place_y],
            (halfway_sems.at[0, to_y], halfway_sems.at[1, place_y]),
            place_x * inner + to_y,
        )

    def along_y_wait(turn):
        from_y = lax.rem(place_y + turn, inner)
        remote(
            sent_ref.at[:, from_y],
            halfway.at[:, from_y],
            (halfway_sems.at[0, from_y], halfway_sems.at[1, from_y]),
            line,
        ).wait_recv()

    def along_x(turn):
        to_x = lax.rem(place_x + turn, outer)
        return remote(
            halfway.at[to_x],
            wind_ref.at[place_x],
            (wind_sems.at[0, to_x], wind_sems.at[1, place_x]),
            to_x * inner + place_y,
        )

    def along_x_wait(turn):
        from_x = lax.rem(place_x + turn, outer)
        remote(
            halfway.at[from_x],
            wind_ref.at[from_x],
            (wind_sems.at[0, from_x], wind_sems.at[1, from_x]),
            line,
        ).wait_recv()

    for turn in range(1, inner):
        along_y(turn).start()
    halfway[:, place_y] = sent_ref[:, place_y]

    @pl.when(core == 1)
    def _():
        span_copy().wait_recv()
        diag_ref[...] = diag_ref[...] + prev_span[...]
        couple[0, 0] = -prev_span[...]

    def load_copy(window, turn):
        step = 0 if turn < time_count else 1
        return remote(
            load_out.at[window],
            load_in.at[window, step, time],
            (load_send_sems.at[window, turn], load_recv_sems.at[window, step, time]),
            line + step,
            lax.rem(time + turn, time_count),
        )

    def load_wait(window, step, group):
        remote(
            load_out.at[window],
            load_in.at[window, step, group],
            (load_send_sems.at[window, 0], load_recv_sems.at[window, step, group]),
            line,
        ).wait_recv()

    def begin_loads(window):
        velocity_col = to_column(vel_ref[...])
        next_col = to_column(next_vel[window])
        interior = vec_mat(velocity_col, maps_ref[0, 0]) + vec_mat(next_col, maps_ref[0, 1])
        offset = mean_ref[...] - interior
        samples, width = wind_ref.shape[2:]

        def add(group, total):
            field = wind_ref[lax.div(group, inner), lax.rem(group, inner)]
            relative = field.astype(jnp.float32) + offset
            step = step_ref[group * time_count + time].astype(jnp.float32)
            return total + (step if window == 1 else 1.0 - step) * (relative * jnp.abs(relative))

        total = lax.fori_loop(0, line_count, add, jnp.zeros((samples, width), jnp.float32))
        load = drag_ref[...] * jnp.sum(total, axis=0, keepdims=True) * window_scale
        load_out[window] = load
        load_in[window, 0, time] = load
        for turn in range(1, time_count):
            load_copy(window, turn).start()

        @pl.when(line < last)
        def _():
            for turn in range(time_count, 2 * time_count):
                load_copy(window, turn).start()

    def end_loads(window):
        for turn in range(1, time_count):
            load_wait(window, 0, lax.rem(time + turn, time_count))

        @pl.when(line > 0)
        def _():
            for turn in range(time_count):
                load_wait(window, 1, lax.rem(time + turn, time_count))

        def summed(step):
            total = load_in[window, step, 0]
            for group in range(1, time_count):
                total = total + load_in[window, step, group]
            return total

        inertia = mass_ref[...] * (
            accel_scale * disp_ref[...] + velocity_scale * vel_ref[...] + acc_ref[...]
        )
        side_ref[...] = inertia + to_row(mat_vec(maps_ref[0, 0], summed(0)))

        @pl.when(line > 0)
        def _():
            if window == 0:
                map_copy().wait_recv()
            side_ref[...] = side_ref[...] + to_row(mat_vec(prev_map[...], summed(1)))

    def send_vector(window, level):
        @pl.when(sends(level))
        def _():
            column = to_column(side_ref[...])
            for side in range(2):

                @pl.when(there(level, side))
                def _():
                    vec_out[window, level, side, :, :order] = vec_mat(column, scaled[level, side])
                    vec_out[window, level, side, :, order:] = bad_ref[...]
                    vec_copy(window, level, side).start()

    def take_vector(window, level):
        @pl.when(core == 0)
        def _():
            for side in range(2):

                @pl.when(there(level, side))
                def _():
                    vec_wait(window, level, side)
                    side_ref[...] = side_ref[...] - vec_in[window, level, side, :, :order]
                    if window == 1:
                        bad_ref[...] = bad_ref[...] + vec_in[window, level, side, :, order:]

    def loads_left(window):
        for turn in range(1, time_count):
            load_copy(window, turn).wait_send()

        @pl.when(line < last)
        def _():
            for turn in range(time_count, 2 * time_count):
                load_copy(window, turn).wait_send()

    def vectors_left(window, level):
        for side in range(2):

            @pl.when(sends(level) & there(level, side))
            def _():
                vec_copy(window, level, side).wait_send()

    def factor_level(level, carry):
        before = jnp.maximum(level - 1, 0)

        @pl.when(level == levels)
        def _():
            send_vector(0, before)

        @pl.when(sends(level))
        def _():
            newton_inverse(diag_ref, inverse_ref, bad_ref)

        for side in range(2):
            sent = (level >= 1) & sends(before) & there(before, side)

            @pl.when(sent)
            def _():
                for copy in update_copies(before, side):
                    copy.wait_send()

            @pl.when(sent & (level < levels))
            def _():
                couple_copy(before, side).wait_send()

        def coupling(side):
            expected = (level >= 1) & (core == 0)

            @pl.when(expected & there(before, side))
            def _():
                for turn in range(1, time_count):
                    share_wait(before, side, turn)
                    share_copy(before, side, turn).wait_send()

            @pl.when(expected & jnp.logical_not(there(before, side)))
            def _():
                couple[level, side] = jnp.zeros((order, order), jnp.float32)

        @pl.when(sends(level) & (level < levels))
        def _():
            coupling(0)

            @pl.when(there(level, 0))
            def _():
                scaled[level, 0] = split_dot(inverse_ref[...], couple[level, 0], 1, 1)

            coupling(1)

            @pl.when(there(level, 1))
            def _():
                scaled[level, 1] = split_dot(inverse_ref[...], couple[level, 1])

            @pl.when(level < levels - 1)
            def _():
                rows = pl.ds(pl.multiple_of(time * quarter, quarter), quarter)
                both = there(level, 0) & there(level, 1)

                @pl.when(both)
                def _():
                    couple_out[...] = -split_dot(couple[level, 0, rows], scaled[level, 1])

                @pl.when(jnp.logical_not(both))
                def _():
                    couple_out[...] = jnp.zeros_like(couple_out)

                for side in range(2):

                    @pl.when(there(level, side))
                    def _():
                        couple_copy(level, side).start()

            @pl.when(there(level, 0))
            def _():
                update_out[0] = split_dot(couple[level, 0], scaled[level, 0])
                for copy in update_copies(level, 0):
                    copy.start()

            @pl.when(there(level, 1))
            def _():
                own = jnp.where(level == 0, 1.0, 0.0)
                update_out[1] = (
                    split_dot(couple[level, 1], scaled[level, 1], 0, 0) - own * span_ref[0]
                )
                for copy in update_copies(level, 1):
                    copy.start()

        for side in range(2):

            @pl.when((level < levels - 1) & (core == 0) & there(level, side))
            def _():
                couple_wait(level, side)
                for turn in range(1, time_count):
                    share_copy(level, side, turn).start()

        @pl.when(level == 0)
        def _():
            for turn in range(1, inner):
                along_y_wait(turn)
            for turn in range(1, outer):
                along_x(turn).start()
            wind_ref[place_x] = halfway[place_x]

        @pl.when(level == 1)
        def _():
            @pl.when(line < last)
            def _():
                vel_wait(0)

            for turn in range(1, outer):
                along_x_wait(turn)
            begin_loads(0)

        @pl.when(level == 2)
        def _():
            end_loads(0)
            send_vector(0, level - 2)
            take_vector(0, level - 2)

        @pl.when((level >= 2) & (level < levels))
        def _():
            send_vector(0, before)

        @pl.when(level >= 2)
        def _():
            take_vector(0, before)
            vectors_left(0, before)

        @pl.when(level == 3)
        def _():
            vectors_left(0, level - 3)
            for turn in range(1, outer):
                along_x(turn).wait_send()
            for turn in range(1, inner):
                along_y(turn).wait_send()
            loads_left(0)

            @pl.when(core == 0)
            def _():
                span_copy().wait_send()

            @pl.when(line < last)
            def _():
                map_copy().wait_send()

        @pl.when(level < levels)
        def _():
            @pl.when(core == 0)
            def _():
                for side in range(2):

                    @pl.when(there(level, side))
                    def _():
                        update_wait(level, side)
                        for block in range(blocks):
                            start = block * LANES
                            part = (pl.ds(start, LANES), pl.ds(start, order - start))
                            diag_ref[part] = diag_ref[part] - update[(level, side) + part]

                for block in range(blocks):
                    rows = pl.ds(block * LANES, LANES)
                    for other in range(block + 1, blocks):
                        columns = pl.ds(other * LANES, LANES)
                        diag_ref[columns, rows] = diag_ref[rows, columns].T

        return carry

    def vel_wait(window):
        remote(
            vel_ref,
            next_vel.at[window],
            (vel_sems.at[0, window], vel_sems.at[1, window]),
            line,
        ).wait_recv()

    lax.fori_loop(0, levels + 1, factor_level, 0)

    def sol_copy(window, side):
        return remote(
            sol_out.at[window],
            sol_in.at[window, 1 - side],
            (sol_sems.at[0, window, side], sol_sems.at[1, window, 1 - side]),
            line + 2 * side - 1,
        )

    def sol_wait(window, side):
        remote(
            sol_out.at[window],
            sol_in.at[window, side],
            (sol_sems.at[0, window, side], sol_sems.at[1, window, side]),
            line,
        ).wait_recv()

    def advance(solution_row):
        new_accel = (
            accel_scale * (solution_row - disp_ref[...])
            - velocity_scale * vel_ref[...]
            - acc_ref[...]
        )
        vel_ref[...] = vel_ref[...] + half_step * (acc_ref[...] + new_accel)
        disp_ref[...] = solution_row
        acc_ref[...] = new_accel

    @pl.when(line > 0)
    def _():
        vel_copy(0).wait_send()

    def finish(window):
        @pl.when(core == 0)
        def _():
            advance(vec_mat(to_column(side_ref[...]), inverse_ref[...]))
            sol_out[window, :, :order] = disp_ref[...]
            sol_out[window, :, order : 2 * order] = vel_ref[...]
            sol_out[window, :, 2 * order :] = bad_ref[...]
            sol_copy(window, 1).start()

            @pl.when(line > 0)
            def _():
                sol_copy(window, 0).start()

        @pl.when(core == 1)
        def _():
            value = vec_mat(to_column(side_ref[...]), inverse_ref[...])
            sol_wait(window, 0)
            behind = mat_vec(scaled[0, 0], sol_in[window, 0, :, :order])
            side_ref[...] = value - to_row(behind)
            if window == 1:
                bad_ref[...] = sol_in[window, 0, :, 2 * order :]

            @pl.when(line < last)
            def _():
                sol_wait(window, 1)
                ahead = mat_vec(scaled[0, 1], sol_in[window, 1, :, :order])
                side_ref[...] = side_ref[...] - to_row(ahead)
                if window == 0:
                    next_vel[1] = sol_in[window, 1, :, order : 2 * order]

            advance(side_ref[...])
            if window == 0:
                vel_copy(1).start()

    finish(0)

    @pl.when(core == 0)
    def _():
        vel_wait(1)

    begin_loads(1)
    end_loads(1)

    def reduce_level(level, carry):
        send_vector(1, level)
        take_vector(1, level)
        return carry

    lax.fori_loop(0, levels, reduce_level, 0)

    @pl.when(core == 1)
    def _():
        vel_copy(1).wait_send()

    finish(1)
    bad_out[...] = bad_ref[...]

    loads_left(1)

    for window in range(2):

        @pl.when(core == 0)
        def _():
            sol_copy(window, 1).wait_send()

            @pl.when(line > 0)
            def _():
                sol_copy(window, 0).wait_send()

    def drain(level, carry):
        vectors_left(1, level)
        return carry

    lax.fori_loop(0, levels, drain, 0)


def run_line(
    line_count,
    time_count,
    window_scale,
    segment_step,
    wind_field,
    mean_wind,
    drag,
    transfer,
    span_stiff,
    mass,
    disp0,
    vel0,
    acc0,
):
    order = span_stiff.shape[-1]
    width = mean_wind.shape[-1]
    levels = (line_count - 1).bit_length()
    row = jax.ShapeDtypeStruct((1, order), jnp.float32)
    inner = max(2, line_count // 4)
    outer = line_count // inner
    wind_field = wind_field.reshape((outer, inner) + wind_field.shape[1:])

    def body(*refs):
        line_kernel(line_count, time_count, window_scale, levels, *refs)

    vmem = pl.BlockSpec(memory_space=pltpu.VMEM)
    dma = pltpu.SemaphoreType.DMA

    def buffer(*shape):
        return pltpu.VMEM(shape, jnp.float32)

    return pl.pallas_call(
        body,
        out_shape=(row, row, jax.ShapeDtypeStruct((1, LANES), jnp.float32)),
        in_specs=[pl.BlockSpec(memory_space=pltpu.SMEM)] + [vmem] * 9,
        out_specs=[vmem] * 3,
        scratch_shapes=[
            buffer(1, order),
            buffer(1, LANES),
            buffer(1, order),
            buffer(order, order),
            buffer(order, order),
            buffer(order, order),
            buffer(order, width),
            buffer(2, 1, order),
            buffer(levels, 2, order, order),
            buffer(levels, 2, order, order),
            buffer(levels, 2, order, order),
            buffer(2, order, order),
            buffer(order // time_count, order),
            buffer(2, levels, 2, 1, order + LANES),
            buffer(2, levels, 2, 1, order + LANES),
            buffer(2, 1, width),
            buffer(2, 2, time_count, 1, width),
            buffer(2, 1, 2 * order + LANES),
            buffer(2, 2, 1, 2 * order + LANES),
            dma((2,)),
            dma((2,)),
            dma((2, 2)),
            dma((2, levels, 2, order // LANES)),
            dma((2, levels, 2)),
            dma((levels, 2, time_count)),
            dma((levels, 2, time_count)),
            dma((2, 2, levels, 2)),
            dma((2, 2 * time_count)),
            dma((2, 2, time_count)),
            dma((2, 2, 2)),
            pltpu.VMEM(wind_field.shape, wind_field.dtype),
            pltpu.VMEM(wind_field.shape, wind_field.dtype),
            dma((2, inner)),
            dma((2, outer)),
        ],
        compiler_params=pltpu.CompilerParams(
            collective_id=0, has_side_effects=True, vmem_limit_bytes=60 * 2**20
        ),
        cost_estimate=pl.CostEstimate(
            flops=100 * order**3, bytes_accessed=5 * 2**20, transcendentals=0
        ),
    )(segment_step, wind_field, mean_wind, drag, transfer, span_stiff, mass, disp0, vel0, acc0)


def local(
    gust_coef,
    mean_wind,
    drag,
    span_column,
    segment_step,
    transfer,
    span_stiff,
    mass,
    disp0,
    vel0,
    acc0,
):
    line_count = lax.axis_size("line")
    time_count = lax.axis_size("tm")
    time_pos = lax.axis_index("tm")
    span_count = span_column.shape[0]
    seg_count = segment_step.shape[0]
    trig_rows = trig_table(TS, KF)
    spectra = gust_coef.reshape(2 * KF, span_count * Q)
    wind_field = jnp.dot(trig_rows, spectra, preferred_element_type=jnp.float32).astype(
        jnp.bfloat16
    )
    wind_field = wind_field.reshape(TS, span_count, Q)
    wind_field = wind_field.at[:, span_column].get(mode="promise_in_bounds").transpose(1, 0, 2)
    window_scale = 1.0 / (TS * (seg_count // 2))
    fast_disp, fast_vel, bad = run_line(
        line_count,
        time_count,
        window_scale,
        segment_step,
        wind_field,
        mean_wind,
        drag,
        transfer,
        span_stiff,
        mass,
        disp0,
        vel0,
        acc0,
    )

    def checked():
        arrived = lax.all_to_all(wind_field, "line", split_axis=0, concat_axis=0, tiled=True)
        seg_index = jnp.arange(line_count, dtype=jnp.int32) * time_count + time_pos
        seg_flags = jnp.take(segment_step, seg_index)
        return checked_loop(
            line_count,
            time_count,
            arrived,
            seg_flags,
            mean_wind,
            drag,
            transfer,
            span_stiff,
            mass,
            disp0,
            vel0,
            acc0,
            window_scale,
        )

    return lax.cond(bad[0, 0] < 0.5, lambda: (fast_disp, fast_vel), checked)


def solution(mesh):
    return jax.shard_map(
        local,
        mesh=mesh,
        in_specs=(
            P(("line", "tm"), None, None, None),
            P("line", None),
            P("line", None),
            P(),
            P(),
            P("line", None, None, None),
            P("line", None, None),
            P("line", None),
            P("line", None),
            P("line", None),
            P("line", None),
        ),
        out_specs=(P("line", None), P("line", None)),
        check_vma=False,
    )
```

```python
import math

import jax
import jax.numpy as jnp
from jax import lax
from jax.experimental import pallas as pl
from jax.experimental.pallas import tpu as pltpu
from jax.sharding import PartitionSpec as P

Q = 256
KF = 64
TS = 64


accel_scale = 4.0
velocity_scale = 4.0
half_step = 0.5


def shifted(array, axis, by):
    length = lax.axis_size(axis)
    pairs = [(i, i + by) for i in range(length) if 0 <= i + by < length]
    return lax.ppermute(array, axis, pairs)


def exact_dot(first, second):
    return jnp.dot(
        first, second, precision=lax.Precision.HIGHEST, preferred_element_type=jnp.float32
    )


def trig_table(sample_count, freq_count):
    sample_index = jnp.arange(sample_count, dtype=jnp.float32)[:, None]
    frequency = (jnp.arange(freq_count, dtype=jnp.float32)[None, :] + 0.25) * (math.pi / freq_count)
    phase_angle = sample_index * frequency
    return jnp.concatenate([jnp.cos(phase_angle), jnp.sin(phase_angle)], axis=1).astype(
        jnp.bfloat16
    )


def cho_apply(factor, values):
    return jax.scipy.linalg.cho_solve((factor, True), values)


def blocked_cholesky(matrix):
    order = matrix.shape[0]
    panel_width = min(128, order)
    factor = jnp.zeros_like(matrix)
    trailing = matrix
    for start_row in range(0, order, panel_width):
        end_row = start_row + panel_width
        corner = jnp.linalg.cholesky(trailing[start_row:end_row, start_row:end_row])
        factor = factor.at[start_row:end_row, start_row:end_row].set(corner)
        if end_row < order:
            below = trailing[end_row:, start_row:end_row]
            below_factor = jax.scipy.linalg.solve_triangular(corner, below.T, lower=True).T
            factor = factor.at[end_row:, start_row:end_row].set(below_factor)
            trailing = trailing.at[end_row:, end_row:].add(-exact_dot(below_factor, below_factor.T))
    return factor


def checked_loop(
    line_count,
    time_count,
    arrived,
    seg_flags,
    mean_wind,
    drag,
    transfer,
    span_stiff,
    mass,
    disp0,
    vel0,
    acc0,
    window_scale,
):
    line_pos = lax.axis_index("line")
    block_order = span_stiff.shape[-1]
    left_map = transfer[0, 0]
    right_map = transfer[0, 1]
    span_block = span_stiff[0]
    before = shifted(span_block, "line", 1)
    identity = jnp.eye(block_order, dtype=jnp.float32)
    diag_block = span_block + before + (accel_scale * mass[0])[:, None] * identity
    coupled = (line_pos < line_count - 1).astype(jnp.float32)
    upper_block = -span_block * coupled
    lower_block = -before
    stored = []
    stride = 1
    while stride < line_count:
        factor = blocked_cholesky(diag_block)
        solved = cho_apply(factor, jnp.concatenate([lower_block, upper_block], axis=1))
        from_lower = shifted(solved, "line", stride)
        from_upper = shifted(solved, "line", -stride)
        new_diag = (
            diag_block
            - exact_dot(lower_block, from_lower[:, block_order:])
            - exact_dot(upper_block, from_upper[:, :block_order])
        )
        new_lower = -exact_dot(lower_block, from_lower[:, :block_order])
        new_upper = -exact_dot(upper_block, from_upper[:, block_order:])
        stored.append((factor, lower_block, upper_block))
        diag_block, lower_block, upper_block = (new_diag, new_lower, new_upper)
        stride = stride * 2
    final_factor = blocked_cholesky(diag_block)
    displacement, velocity, accel_now = (disp0, vel0, acc0)
    for window in range(2):
        next_velocity = shifted(velocity, "line", -1)
        offset = mean_wind - (exact_dot(velocity, left_map) + exact_dot(next_velocity, right_map))
        relative = arrived.astype(jnp.float32) + offset[None]
        weight = (seg_flags == window).astype(jnp.float32)
        window_partial_value = jnp.sum(
            weight[:, None, None] * relative * jnp.abs(relative), axis=(0, 1)
        )[None]
        summed = lax.psum(window_partial_value, "tm")
        span_load = drag * summed * window_scale
        passed = exact_dot(span_load, right_map.T)
        from_left = shifted(passed, "line", 1)
        force = exact_dot(span_load, left_map.T) + from_left
        right_side = force + mass * (
            accel_scale * displacement + velocity_scale * velocity + accel_now
        )
        vector = right_side[0]
        reach_now = 1
        for solve_factor, lower_one, upper_one in stored:
            solve_solved = cho_apply(solve_factor, vector)
            from_below = shifted(solve_solved, "line", reach_now)
            from_above = shifted(solve_solved, "line", -reach_now)
            vector = vector - exact_dot(lower_one, from_below) - exact_dot(upper_one, from_above)
            reach_now = reach_now * 2
        new_disp = cho_apply(final_factor, vector)[None]
        new_accel = accel_scale * (new_disp - displacement) - velocity_scale * velocity - accel_now
        velocity = velocity + half_step * (accel_now + new_accel)
        displacement, accel_now = (new_disp, new_accel)
    return (displacement, velocity)


MESH = pl.DeviceIdType.MESH


def halves(value):
    high = value.astype(jnp.bfloat16)
    return high, (value - high.astype(jnp.float32)).astype(jnp.bfloat16)


def split_dot(first, second, first_axis=1, second_axis=0):
    first_hi, first_lo = halves(first)
    second_hi, second_lo = halves(second)
    left = jnp.concatenate([first_hi, first_hi, first_lo], axis=first_axis)
    right = jnp.concatenate([second_hi, second_lo, second_hi], axis=second_axis)
    return lax.dot_general(
        left,
        right,
        (((first_axis,), (second_axis,)), ((), ())),
        preferred_element_type=jnp.float32,
    )


def single_dot(first, second):
    return jnp.dot(
        first.astype(jnp.bfloat16), second.astype(jnp.bfloat16), preferred_element_type=jnp.float32
    )


def eye_mask(order):
    rows = lax.broadcasted_iota(jnp.int32, (order, order), 0)
    return rows == lax.broadcasted_iota(jnp.int32, (order, order), 1)


LANES = 128


def to_column(row):
    mask = eye_mask(LANES)
    parts = [
        jnp.sum(jnp.where(mask, row[:, k : k + LANES], 0.0), axis=1, keepdims=True)
        for k in range(0, row.shape[1], LANES)
    ]
    return jnp.concatenate(parts, axis=0)


def to_row(column):
    mask = eye_mask(LANES)
    parts = [
        jnp.sum(jnp.where(mask, column[k : k + LANES], 0.0), axis=0, keepdims=True)
        for k in range(0, column.shape[0], LANES)
    ]
    return jnp.concatenate(parts, axis=1)


def vec_mat(column, matrix):
    return jnp.sum(column * matrix, axis=0, keepdims=True)


def mat_vec(matrix, row):
    return jnp.sum(matrix * row, axis=1, keepdims=True)


def newton_inverse(diag_ref, inverse_ref, bad_ref, bound_on_residual=0.03):
    order = diag_ref.shape[0]
    mask = eye_mask(order)
    diag = diag_ref[...]
    on_diag = jnp.where(mask, diag, 0.0)
    diag_row = jnp.sum(on_diag, axis=0, keepdims=True)
    diag_col = jnp.sum(on_diag, axis=1, keepdims=True)
    bound = jnp.max(
        jnp.sum(jnp.abs(diag), axis=0, keepdims=True) / diag_row, axis=1, keepdims=True
    )
    scale = jnp.minimum(1.0, 1.8 / bound)
    identity = jnp.where(mask, 1.0, 0.0)
    inverse_ref[...] = (scale / diag_col) * (2.0 * identity - diag * (scale / diag_row))
    current = inverse_ref[...]
    residual = identity - single_dot(diag_ref[...], current)
    estimate = (current + single_dot(current, residual)).astype(jnp.bfloat16)
    diag_hi, diag_lo = halves(diag_ref[...])
    residual = (
        identity
        - jnp.dot(diag_hi, estimate, preferred_element_type=jnp.float32)
        - jnp.dot(diag_lo, estimate, preferred_element_type=jnp.float32)
    )
    size = jnp.max(jnp.sum(jnp.abs(residual), axis=0, keepdims=True), axis=1, keepdims=True)
    bad_ref[...] = bad_ref[...] + jnp.where(size < bound_on_residual, 0.0, 1.0)
    series_hi, series_lo = halves(residual + single_dot(residual, residual))
    inverse_ref[...] = (
        estimate.astype(jnp.float32)
        + jnp.dot(estimate, series_hi, preferred_element_type=jnp.float32)
        + jnp.dot(estimate, series_lo, preferred_element_type=jnp.float32)
    )


def line_kernel(
    line_count,
    time_count,
    window_scale,
    levels,
    step_ref,
    sent_ref,
    mean_ref,
    drag_ref,
    maps_ref,
    span_ref,
    mass_ref,
    disp_in,
    vel_in,
    acc_in,
    disp_ref,
    vel_ref,
    bad_out,
    acc_ref,
    bad_ref,
    side_ref,
    diag_ref,
    inverse_ref,
    prev_span,
    prev_map,
    next_vel,
    couple,
    update,
    scaled,
    update_out,
    couple_out,
    vec_out,
    vec_in,
    load_out,
    load_in,
    sol_out,
    sol_in,
    span_sems,
    map_sems,
    vel_sems,
    update_sems,
    couple_sems,
    share_send_sems,
    share_recv_sems,
    vec_sems,
    load_send_sems,
    load_recv_sems,
    sol_sems,
    halfway,
    wind_ref,
    halfway_sems,
    wind_sems,
):
    line = lax.axis_index("line")
    time = lax.axis_index("tm")
    core = lax.rem(line, 2)
    order = span_ref.shape[1]
    last = line_count - 1

    barrier = pltpu.get_barrier_semaphore()
    partners = jnp.int32(0)
    for delta in (-1, 1):
        there = (line + delta >= 0) & (line + delta <= last)
        for turn in range(1, time_count):

            @pl.when(there)
            def _():
                pl.semaphore_signal(
                    barrier,
                    inc=1,
                    device_id=(line + delta, lax.rem(time + turn, time_count)),
                    device_id_type=MESH,
                )

        partners = partners + jnp.where(there, time_count - 1, 0)
    for turn in range(1, time_count):
        pl.semaphore_signal(
            barrier,
            inc=1,
            device_id=(line, lax.rem(time + turn, time_count)),
            device_id_type=MESH,
        )
    partners = partners + (time_count - 1)

    inner = max(2, line_count // 4)
    outer = line_count // inner
    place_x = lax.div(line, inner)
    place_y = lax.rem(line, inner)
    for turn in range(1, outer):
        pl.semaphore_signal(
            barrier,
            inc=1,
            device_id=(lax.rem(place_x + turn, outer) * inner + place_y, time),
            device_id_type=MESH,
        )
    for turn in range(1, inner):
        pl.semaphore_signal(
            barrier,
            inc=1,
            device_id=(place_x * inner + lax.rem(place_y + turn, inner), time),
            device_id_type=MESH,
        )
    partners = partners + (outer + inner - 2)
    stride = 1
    while stride < inner:
        for delta in (-stride, stride):
            near = (line + delta >= 0) & (line + delta <= last)
            if stride > 1:
                near = near & (core == 0)

            @pl.when(near)
            def _():
                pl.semaphore_signal(
                    barrier, inc=1, device_id=(line + delta, time), device_id_type=MESH
                )

            partners = partners + jnp.where(near, 1, 0)
        stride = stride * 2

    def remote(source, target, sems, to_line, to_time=None):
        return pltpu.make_async_remote_copy(
            src_ref=source,
            dst_ref=target,
            send_sem=sems[0],
            recv_sem=sems[1],
            device_id=(to_line, time if to_time is None else to_time),
            device_id_type=MESH,
        )

    def span_copy():
        return remote(span_ref.at[0], prev_span, (span_sems.at[0], span_sems.at[1]), line + 1)

    def map_copy():
        return remote(maps_ref.at[0, 1], prev_map, (map_sems.at[0], map_sems.at[1]), line + 1)

    def vel_copy(window):
        return remote(
            vel_ref,
            next_vel.at[window],
            (vel_sems.at[0, window], vel_sems.at[1, window]),
            line - 1,
        )

    blocks = order // LANES
    quarter = order // time_count

    def triangle(ref, block):
        start = block * LANES
        return ref.at[pl.ds(start, LANES), pl.ds(start, order - start)]

    def own_rows(ref, group):
        return ref.at[pl.ds(pl.multiple_of(group * quarter, quarter), quarter)]

    def update_copies(level, side):
        stride = jnp.left_shift(1, level)
        return [
            remote(
                triangle(update_out.at[side], block),
                triangle(update.at[level, 1 - side], block),
                (
                    update_sems.at[0, level, side, block],
                    update_sems.at[1, level, 1 - side, block],
                ),
                line + (2 * side - 1) * stride,
            )
            for block in range(blocks)
        ]

    def update_wait(level, side):
        for block in range(blocks):
            remote(
                triangle(update_out.at[side], block),
                triangle(update.at[level, side], block),
                (update_sems.at[0, level, side, block], update_sems.at[1, level, side, block]),
                line,
            ).wait_recv()

    def couple_copy(level, side):
        stride = jnp.left_shift(1, level)
        return remote(
            couple_out,
            own_rows(couple.at[level + 1, 1 - side], time),
            (couple_sems.at[0, level, side], couple_sems.at[1, level, 1 - side]),
            line + (2 * side - 1) * stride,
        )

    def couple_wait(level, side):
        remote(
            couple_out,
            own_rows(couple.at[level + 1, side], time),
            (couple_sems.at[0, level, side], couple_sems.at[1, level, side]),
            line,
        ).wait_recv()

    def share_copy(level, side, turn):
        rows = own_rows(couple.at[level + 1, side], time)
        return remote(
            rows,
            rows,
            (share_send_sems.at[level, side, turn], share_recv_sems.at[level, side, time]),
            line,
            lax.rem(time + turn, time_count),
        )

    def share_wait(level, side, turn):
        group = lax.rem(time + turn, time_count)
        rows = own_rows(couple.at[level + 1, side], group)
        remote(
            rows,
            rows,
            (share_send_sems.at[level, side, turn], share_recv_sems.at[level, side, group]),
            line,
        ).wait_recv()

    def vec_copy(window, level, side):
        stride = jnp.left_shift(1, level)
        return remote(
            vec_out.at[window, level, side],
            vec_in.at[window, level, 1 - side],
            (vec_sems.at[0, window, level, side], vec_sems.at[1, window, level, 1 - side]),
            line + (2 * side - 1) * stride,
        )

    def vec_wait(window, level, side):
        remote(
            vec_out.at[window, level, side],
            vec_in.at[window, level, side],
            (vec_sems.at[0, window, level, side], vec_sems.at[1, window, level, side]),
            line,
        ).wait_recv()

    def there(level, side):
        stride = jnp.left_shift(1, level)
        return (line - stride >= 0) if side == 0 else (line + stride <= last)

    def sends(level):
        return core == jnp.where(level == 0, 1, 0)

    vel_ref[...] = vel_in[...]
    disp_ref[...] = disp_in[...]
    acc_ref[...] = acc_in[...]
    bad_ref[...] = jnp.zeros_like(bad_ref)
    own_diag = jnp.where(eye_mask(order), accel_scale * to_column(mass_ref[...]), 0.0)
    diag_ref[...] = span_ref[0] + own_diag

    @pl.when(core == 1)
    def _():
        couple[0, 1] = -jnp.where(line < last, 1.0, 0.0) * span_ref[0]

    pl.semaphore_wait(barrier, partners)

    @pl.when(core == 0)
    def _():
        span_copy().start()

    @pl.when(line > 0)
    def _():
        vel_copy(0).start()

    @pl.when(line < last)
    def _():
        map_copy().start()

    @pl.when(line == last)
    def _():
        next_vel[...] = jnp.zeros_like(next_vel)

    def along_y(turn):
        to_y = lax.rem(place_y + turn, inner)
        return remote(
            sent_ref.at[:, to_y],
            halfway.at[:, place_y],
            (halfway_sems.at[0, to_y], halfway_sems.at[1, place_y]),
            place_x * inner + to_y,
        )

    def along_y_wait(turn):
        from_y = lax.rem(place_y + turn, inner)
        remote(
            sent_ref.at[:, from_y],
            halfway.at[:, from_y],
            (halfway_sems.at[0, from_y], halfway_sems.at[1, from_y]),
            line,
        ).wait_recv()

    def along_x(turn):
        to_x = lax.rem(place_x + turn, outer)
        return remote(
            halfway.at[to_x],
            wind_ref.at[place_x],
            (wind_sems.at[0, to_x], wind_sems.at[1, place_x]),
            to_x * inner + place_y,
        )

    def along_x_wait(turn):
        from_x = lax.rem(place_x + turn, outer)
        remote(
            halfway.at[from_x],
            wind_ref.at[from_x],
            (wind_sems.at[0, from_x], wind_sems.at[1, from_x]),
            line,
        ).wait_recv()

    for turn in range(1, inner):
        along_y(turn).start()
    halfway[:, place_y] = sent_ref[:, place_y]

    @pl.when(core == 1)
    def _():
        span_copy().wait_recv()
        diag_ref[...] = diag_ref[...] + prev_span[...]
        couple[0, 0] = -prev_span[...]

    def load_copy(window, turn):
        step = 0 if turn < time_count else 1
        return remote(
            load_out.at[window],
            load_in.at[window, step, time],
            (load_send_sems.at[window, turn], load_recv_sems.at[window, step, time]),
            line + step,
            lax.rem(time + turn, time_count),
        )

    def load_wait(window, step, group):
        remote(
            load_out.at[window],
            load_in.at[window, step, group],
            (load_send_sems.at[window, 0], load_recv_sems.at[window, step, group]),
            line,
        ).wait_recv()

    def begin_loads(window):
        velocity_col = to_column(vel_ref[...])
        next_col = to_column(next_vel[window])
        interior = vec_mat(velocity_col, maps_ref[0, 0]) + vec_mat(next_col, maps_ref[0, 1])
        offset = mean_ref[...] - interior
        samples, width = wind_ref.shape[2:]

        def add(from_y, total):
            for from_x in range(outer):
                relative = wind_ref[from_x, from_y].astype(jnp.float32) + offset
                group = (from_x * inner + from_y) * time_count + time
                step = step_ref[group].astype(jnp.float32)
                total = total + (step if window == 1 else 1.0 - step) * (
                    relative * jnp.abs(relative)
                )
            return total

        total = lax.fori_loop(0, inner, add, jnp.zeros((samples, width), jnp.float32))
        load = drag_ref[...] * jnp.sum(total, axis=0, keepdims=True) * window_scale
        load_out[window] = load
        load_in[window, 0, time] = load
        for turn in range(1, time_count):
            load_copy(window, turn).start()

        @pl.when(line < last)
        def _():
            for turn in range(time_count, 2 * time_count):
                load_copy(window, turn).start()

    def end_loads(window):
        for turn in range(1, time_count):
            load_wait(window, 0, lax.rem(time + turn, time_count))

        @pl.when(line > 0)
        def _():
            for turn in range(time_count):
                load_wait(window, 1, lax.rem(time + turn, time_count))

        def summed(step):
            total = load_in[window, step, 0]
            for group in range(1, time_count):
                total = total + load_in[window, step, group]
            return total

        inertia = mass_ref[...] * (
            accel_scale * disp_ref[...] + velocity_scale * vel_ref[...] + acc_ref[...]
        )
        side_ref[...] = inertia + to_row(mat_vec(maps_ref[0, 0], summed(0)))

        @pl.when(line > 0)
        def _():
            if window == 0:
                map_copy().wait_recv()
            side_ref[...] = side_ref[...] + to_row(mat_vec(prev_map[...], summed(1)))

    def send_vector(window, level):
        @pl.when(sends(level))
        def _():
            column = to_column(side_ref[...])
            for side in range(2):

                @pl.when(there(level, side))
                def _():
                    vec_out[window, level, side, :, :order] = vec_mat(column, scaled[level, side])
                    vec_out[window, level, side, :, order:] = bad_ref[...]
                    vec_copy(window, level, side).start()

    def take_vector(window, level):
        @pl.when(core == 0)
        def _():
            for side in range(2):

                @pl.when(there(level, side))
                def _():
                    vec_wait(window, level, side)
                    side_ref[...] = side_ref[...] - vec_in[window, level, side, :, :order]
                    if window == 1:
                        bad_ref[...] = bad_ref[...] + vec_in[window, level, side, :, order:]

    def loads_left(window):
        for turn in range(1, time_count):
            load_copy(window, turn).wait_send()

        @pl.when(line < last)
        def _():
            for turn in range(time_count, 2 * time_count):
                load_copy(window, turn).wait_send()

    def vectors_left(window, level):
        for side in range(2):

            @pl.when(sends(level) & there(level, side))
            def _():
                vec_copy(window, level, side).wait_send()

    def factor_level(level, carry):
        before = jnp.maximum(level - 1, 0)

        @pl.when(level == levels)
        def _():
            send_vector(0, before)

        @pl.when(sends(level))
        def _():
            newton_inverse(diag_ref, inverse_ref, bad_ref)

        for side in range(2):
            sent = (level >= 1) & sends(before) & there(before, side)

            @pl.when(sent)
            def _():
                for copy in update_copies(before, side):
                    copy.wait_send()

            @pl.when(sent & (level < levels))
            def _():
                couple_copy(before, side).wait_send()

        def coupling(side):
            expected = (level >= 1) & (core == 0)

            @pl.when(expected & there(before, side))
            def _():
                for turn in range(1, time_count):
                    share_wait(before, side, turn)
                    share_copy(before, side, turn).wait_send()

            @pl.when(expected & jnp.logical_not(there(before, side)))
            def _():
                couple[level, side] = jnp.zeros((order, order), jnp.float32)

        @pl.when(sends(level) & (level < levels))
        def _():
            coupling(0)

            @pl.when(there(level, 0))
            def _():
                scaled[level, 0] = split_dot(inverse_ref[...], couple[level, 0], 1, 1)

            half = order // 2

            @pl.when(there(level, 0))
            def _():
                copies = update_copies(level, 0)
                for start in (0, half):
                    rows, columns = pl.ds(start, half), pl.ds(start, order - start)
                    update_out[0, rows, columns] = split_dot(
                        couple[level, 0, rows], scaled[level, 0, :, columns]
                    )
                    for block in range(start // LANES, (start + half) // LANES):
                        copies[block].start()

            coupling(1)

            @pl.when(there(level, 1))
            def _():
                scaled[level, 1] = split_dot(inverse_ref[...], couple[level, 1])

            @pl.when(level < levels - 1)
            def _():
                rows = pl.ds(pl.multiple_of(time * quarter, quarter), quarter)
                both = there(level, 0) & there(level, 1)

                @pl.when(both)
                def _():
                    couple_out[...] = -split_dot(couple[level, 0, rows], scaled[level, 1])

                @pl.when(jnp.logical_not(both))
                def _():
                    couple_out[...] = jnp.zeros_like(couple_out)

                for side in range(2):

                    @pl.when(there(level, side))
                    def _():
                        couple_copy(level, side).start()

            @pl.when(there(level, 1))
            def _():
                own = jnp.where(level == 0, 1.0, 0.0)
                copies = update_copies(level, 1)
                for start in (0, half):
                    rows, columns = pl.ds(start, half), pl.ds(start, order - start)
                    update_out[1, rows, columns] = (
                        split_dot(couple[level, 1, :, rows], scaled[level, 1, :, columns], 0, 0)
                        - own * span_ref[0, rows, columns]
                    )
                    for block in range(start // LANES, (start + half) // LANES):
                        copies[block].start()

        for side in range(2):

            @pl.when((level < levels - 1) & (core == 0) & there(level, side))
            def _():
                couple_wait(level, side)
                for turn in range(1, time_count):
                    share_copy(level, side, turn).start()

        @pl.when(level == 0)
        def _():
            for turn in range(1, inner):
                along_y_wait(turn)
            for turn in range(1, outer):
                along_x(turn).start()
            wind_ref[place_x] = halfway[place_x]

        @pl.when(level == 1)
        def _():
            @pl.when(line < last)
            def _():
                vel_wait(0)

            for turn in range(1, outer):
                along_x_wait(turn)
            begin_loads(0)

        @pl.when(level == 2)
        def _():
            end_loads(0)
            send_vector(0, level - 2)
            take_vector(0, level - 2)

        @pl.when((level >= 2) & (level < levels))
        def _():
            send_vector(0, before)

        @pl.when(level >= 2)
        def _():
            take_vector(0, before)
            vectors_left(0, before)

        @pl.when(level == 3)
        def _():
            vectors_left(0, level - 3)
            for turn in range(1, outer):
                along_x(turn).wait_send()
            for turn in range(1, inner):
                along_y(turn).wait_send()
            loads_left(0)

            @pl.when(core == 0)
            def _():
                span_copy().wait_send()

            @pl.when(line < last)
            def _():
                map_copy().wait_send()

        @pl.when(level < levels)
        def _():
            @pl.when(core == 0)
            def _():
                for side in range(2):

                    @pl.when(there(level, side))
                    def _():
                        update_wait(level, side)
                        for block in range(blocks):
                            start = block * LANES
                            part = (pl.ds(start, LANES), pl.ds(start, order - start))
                            diag_ref[part] = diag_ref[part] - update[(level, side) + part]

                for block in range(blocks):
                    rows = pl.ds(block * LANES, LANES)
                    for other in range(block + 1, blocks):
                        columns = pl.ds(other * LANES, LANES)
                        diag_ref[columns, rows] = diag_ref[rows, columns].T

        return carry

    def vel_wait(window):
        remote(
            vel_ref,
            next_vel.at[window],
            (vel_sems.at[0, window], vel_sems.at[1, window]),
            line,
        ).wait_recv()

    lax.fori_loop(0, levels + 1, factor_level, 0)

    def sol_copy(window, side):
        return remote(
            sol_out.at[window],
            sol_in.at[window, 1 - side],
            (sol_sems.at[0, window, side], sol_sems.at[1, window, 1 - side]),
            line + 2 * side - 1,
        )

    def sol_wait(window, side):
        remote(
            sol_out.at[window],
            sol_in.at[window, side],
            (sol_sems.at[0, window, side], sol_sems.at[1, window, side]),
            line,
        ).wait_recv()

    def advance(solution_row):
        new_accel = (
            accel_scale * (solution_row - disp_ref[...])
            - velocity_scale * vel_ref[...]
            - acc_ref[...]
        )
        vel_ref[...] = vel_ref[...] + half_step * (acc_ref[...] + new_accel)
        disp_ref[...] = solution_row
        acc_ref[...] = new_accel

    @pl.when(line > 0)
    def _():
        vel_copy(0).wait_send()

    def finish(window):
        @pl.when(core == 0)
        def _():
            advance(vec_mat(to_column(side_ref[...]), inverse_ref[...]))
            sol_out[window, :, :order] = disp_ref[...]
            sol_out[window, :, order : 2 * order] = vel_ref[...]
            sol_out[window, :, 2 * order :] = bad_ref[...]
            sol_copy(window, 1).start()

            @pl.when(line > 0)
            def _():
                sol_copy(window, 0).start()

        @pl.when(core == 1)
        def _():
            value = vec_mat(to_column(side_ref[...]), inverse_ref[...])
            sol_wait(window, 0)
            behind = mat_vec(scaled[0, 0], sol_in[window, 0, :, :order])
            side_ref[...] = value - to_row(behind)
            if window == 1:
                bad_ref[...] = sol_in[window, 0, :, 2 * order :]

            @pl.when(line < last)
            def _():
                sol_wait(window, 1)
                ahead = mat_vec(scaled[0, 1], sol_in[window, 1, :, :order])
                side_ref[...] = side_ref[...] - to_row(ahead)
                if window == 0:
                    next_vel[1] = sol_in[window, 1, :, order : 2 * order]

            advance(side_ref[...])
            if window == 0:
                vel_copy(1).start()

    finish(0)

    @pl.when(core == 0)
    def _():
        vel_wait(1)

    begin_loads(1)
    end_loads(1)

    def reduce_level(level, carry):
        send_vector(1, level)
        take_vector(1, level)
        return carry

    lax.fori_loop(0, levels, reduce_level, 0)

    @pl.when(core == 1)
    def _():
        vel_copy(1).wait_send()

    finish(1)
    bad_out[...] = bad_ref[...]

    loads_left(1)

    for window in range(2):

        @pl.when(core == 0)
        def _():
            sol_copy(window, 1).wait_send()

            @pl.when(line > 0)
            def _():
                sol_copy(window, 0).wait_send()

    def drain(level, carry):
        vectors_left(1, level)
        return carry

    lax.fori_loop(0, levels, drain, 0)


def run_line(
    line_count,
    time_count,
    window_scale,
    segment_step,
    wind_field,
    mean_wind,
    drag,
    transfer,
    span_stiff,
    mass,
    disp0,
    vel0,
    acc0,
):
    order = span_stiff.shape[-1]
    width = mean_wind.shape[-1]
    levels = (line_count - 1).bit_length()
    row = jax.ShapeDtypeStruct((1, order), jnp.float32)
    inner = max(2, line_count // 4)
    outer = line_count // inner
    wind_field = wind_field.reshape((outer, inner) + wind_field.shape[1:])

    def body(*refs):
        line_kernel(line_count, time_count, window_scale, levels, *refs)

    vmem = pl.BlockSpec(memory_space=pltpu.VMEM)
    dma = pltpu.SemaphoreType.DMA

    def buffer(*shape):
        return pltpu.VMEM(shape, jnp.float32)

    return pl.pallas_call(
        body,
        out_shape=(row, row, jax.ShapeDtypeStruct((1, LANES), jnp.float32)),
        in_specs=[pl.BlockSpec(memory_space=pltpu.SMEM)] + [vmem] * 9,
        out_specs=[vmem] * 3,
        scratch_shapes=[
            buffer(1, order),
            buffer(1, LANES),
            buffer(1, order),
            buffer(order, order),
            buffer(order, order),
            buffer(order, order),
            buffer(order, width),
            buffer(2, 1, order),
            buffer(levels, 2, order, order),
            buffer(levels, 2, order, order),
            buffer(levels, 2, order, order),
            buffer(2, order, order),
            buffer(order // time_count, order),
            buffer(2, levels, 2, 1, order + LANES),
            buffer(2, levels, 2, 1, order + LANES),
            buffer(2, 1, width),
            buffer(2, 2, time_count, 1, width),
            buffer(2, 1, 2 * order + LANES),
            buffer(2, 2, 1, 2 * order + LANES),
            dma((2,)),
            dma((2,)),
            dma((2, 2)),
            dma((2, levels, 2, order // LANES)),
            dma((2, levels, 2)),
            dma((levels, 2, time_count)),
            dma((levels, 2, time_count)),
            dma((2, 2, levels, 2)),
            dma((2, 2 * time_count)),
            dma((2, 2, time_count)),
            dma((2, 2, 2)),
            pltpu.VMEM(wind_field.shape, wind_field.dtype),
            pltpu.VMEM(wind_field.shape, wind_field.dtype),
            dma((2, inner)),
            dma((2, outer)),
        ],
        compiler_params=pltpu.CompilerParams(
            collective_id=0, has_side_effects=True, vmem_limit_bytes=60 * 2**20
        ),
        cost_estimate=pl.CostEstimate(
            flops=100 * order**3, bytes_accessed=5 * 2**20, transcendentals=0
        ),
    )(segment_step, wind_field, mean_wind, drag, transfer, span_stiff, mass, disp0, vel0, acc0)


def local(
    gust_coef,
    mean_wind,
    drag,
    span_column,
    segment_step,
    transfer,
    span_stiff,
    mass,
    disp0,
    vel0,
    acc0,
):
    line_count = lax.axis_size("line")
    time_count = lax.axis_size("tm")
    time_pos = lax.axis_index("tm")
    span_count = span_column.shape[0]
    seg_count = segment_step.shape[0]
    trig_rows = trig_table(TS, KF)
    spectra = gust_coef.reshape(2 * KF, span_count * Q)
    wind_field = jnp.dot(trig_rows, spectra, preferred_element_type=jnp.float32).astype(
        jnp.bfloat16
    )
    wind_field = wind_field.reshape(TS, span_count, Q)
    wind_field = wind_field.at[:, span_column].get(mode="promise_in_bounds").transpose(1, 0, 2)
    window_scale = 1.0 / (TS * (seg_count // 2))
    fast_disp, fast_vel, bad = run_line(
        line_count,
        time_count,
        window_scale,
        segment_step,
        wind_field,
        mean_wind,
        drag,
        transfer,
        span_stiff,
        mass,
        disp0,
        vel0,
        acc0,
    )

    def checked():
        arrived = lax.all_to_all(wind_field, "line", split_axis=0, concat_axis=0, tiled=True)
        seg_index = jnp.arange(line_count, dtype=jnp.int32) * time_count + time_pos
        seg_flags = jnp.take(segment_step, seg_index)
        return checked_loop(
            line_count,
            time_count,
            arrived,
            seg_flags,
            mean_wind,
            drag,
            transfer,
            span_stiff,
            mass,
            disp0,
            vel0,
            acc0,
            window_scale,
        )

    def chosen():
        return jnp.concatenate(checked(), axis=0)

    both = lax.cond(
        bad[0, 0] < 0.5, lambda: jnp.concatenate([fast_disp, fast_vel], axis=0), chosen
    )
    return both[:1], both[1:]


def solution(mesh):
    return jax.shard_map(
        local,
        mesh=mesh,
        in_specs=(
            P(("line", "tm"), None, None, None),
            P("line", None),
            P("line", None),
            P(),
            P(),
            P("line", None, None, None),
            P("line", None, None),
            P("line", None),
            P("line", None),
            P("line", None),
            P("line", None),
        ),
        out_specs=(P("line", None), P("line", None)),
        check_vma=False,
    )
```

```python
import math

import jax
import jax.numpy as jnp
from jax import lax
from jax.experimental import pallas as pl
from jax.experimental.pallas import tpu as pltpu
from jax.sharding import PartitionSpec as P

Q = 256
KF = 64
TS = 64


accel_scale = 4.0
velocity_scale = 4.0
half_step = 0.5


def shifted(array, axis, by):
    length = lax.axis_size(axis)
    pairs = [(i, i + by) for i in range(length) if 0 <= i + by < length]
    return lax.ppermute(array, axis, pairs)


def exact_dot(first, second):
    return jnp.dot(
        first, second, precision=lax.Precision.HIGHEST, preferred_element_type=jnp.float32
    )


def trig_table(sample_count, freq_count):
    sample_index = jnp.arange(sample_count, dtype=jnp.float32)[:, None]
    frequency = (jnp.arange(freq_count, dtype=jnp.float32)[None, :] + 0.25) * (math.pi / freq_count)
    phase_angle = sample_index * frequency
    return jnp.concatenate([jnp.cos(phase_angle), jnp.sin(phase_angle)], axis=1).astype(
        jnp.bfloat16
    )


def cho_apply(factor, values):
    return jax.scipy.linalg.cho_solve((factor, True), values)


def blocked_cholesky(matrix):
    order = matrix.shape[0]
    panel_width = min(128, order)
    factor = jnp.zeros_like(matrix)
    trailing = matrix
    for start_row in range(0, order, panel_width):
        end_row = start_row + panel_width
        corner = jnp.linalg.cholesky(trailing[start_row:end_row, start_row:end_row])
        factor = factor.at[start_row:end_row, start_row:end_row].set(corner)
        if end_row < order:
            below = trailing[end_row:, start_row:end_row]
            below_factor = jax.scipy.linalg.solve_triangular(corner, below.T, lower=True).T
            factor = factor.at[end_row:, start_row:end_row].set(below_factor)
            trailing = trailing.at[end_row:, end_row:].add(-exact_dot(below_factor, below_factor.T))
    return factor


def checked_loop(
    line_count,
    time_count,
    arrived,
    seg_flags,
    mean_wind,
    drag,
    transfer,
    span_stiff,
    mass,
    disp0,
    vel0,
    acc0,
    window_scale,
):
    line_pos = lax.axis_index("line")
    block_order = span_stiff.shape[-1]
    left_map = transfer[0, 0]
    right_map = transfer[0, 1]
    span_block = span_stiff[0]
    before = shifted(span_block, "line", 1)
    identity = jnp.eye(block_order, dtype=jnp.float32)
    diag_block = span_block + before + (accel_scale * mass[0])[:, None] * identity
    coupled = (line_pos < line_count - 1).astype(jnp.float32)
    upper_block = -span_block * coupled
    lower_block = -before
    stored = []
    stride = 1
    while stride < line_count:
        factor = blocked_cholesky(diag_block)
        solved = cho_apply(factor, jnp.concatenate([lower_block, upper_block], axis=1))
        from_lower = shifted(solved, "line", stride)
        from_upper = shifted(solved, "line", -stride)
        new_diag = (
            diag_block
            - exact_dot(lower_block, from_lower[:, block_order:])
            - exact_dot(upper_block, from_upper[:, :block_order])
        )
        new_lower = -exact_dot(lower_block, from_lower[:, :block_order])
        new_upper = -exact_dot(upper_block, from_upper[:, block_order:])
        stored.append((factor, lower_block, upper_block))
        diag_block, lower_block, upper_block = (new_diag, new_lower, new_upper)
        stride = stride * 2
    final_factor = blocked_cholesky(diag_block)
    displacement, velocity, accel_now = (disp0, vel0, acc0)
    for window in range(2):
        next_velocity = shifted(velocity, "line", -1)
        offset = mean_wind - (exact_dot(velocity, left_map) + exact_dot(next_velocity, right_map))
        relative = arrived.astype(jnp.float32) + offset[None]
        weight = (seg_flags == window).astype(jnp.float32)
        window_partial_value = jnp.sum(
            weight[:, None, None] * relative * jnp.abs(relative), axis=(0, 1)
        )[None]
        summed = lax.psum(window_partial_value, "tm")
        span_load = drag * summed * window_scale
        passed = exact_dot(span_load, right_map.T)
        from_left = shifted(passed, "line", 1)
        force = exact_dot(span_load, left_map.T) + from_left
        right_side = force + mass * (
            accel_scale * displacement + velocity_scale * velocity + accel_now
        )
        vector = right_side[0]
        reach_now = 1
        for solve_factor, lower_one, upper_one in stored:
            solve_solved = cho_apply(solve_factor, vector)
            from_below = shifted(solve_solved, "line", reach_now)
            from_above = shifted(solve_solved, "line", -reach_now)
            vector = vector - exact_dot(lower_one, from_below) - exact_dot(upper_one, from_above)
            reach_now = reach_now * 2
        new_disp = cho_apply(final_factor, vector)[None]
        new_accel = accel_scale * (new_disp - displacement) - velocity_scale * velocity - accel_now
        velocity = velocity + half_step * (accel_now + new_accel)
        displacement, accel_now = (new_disp, new_accel)
    return (displacement, velocity)


MESH = pl.DeviceIdType.MESH


def halves(value):
    high = value.astype(jnp.bfloat16)
    return high, (value - high.astype(jnp.float32)).astype(jnp.bfloat16)


def split_dot(first, second, first_axis=1, second_axis=0):
    first_hi, first_lo = halves(first)
    second_hi, second_lo = halves(second)
    left = jnp.concatenate([first_hi, first_hi, first_lo], axis=first_axis)
    right = jnp.concatenate([second_hi, second_lo, second_hi], axis=second_axis)
    return lax.dot_general(
        left,
        right,
        (((first_axis,), (second_axis,)), ((), ())),
        preferred_element_type=jnp.float32,
    )


def single_dot(first, second):
    return jnp.dot(
        first.astype(jnp.bfloat16), second.astype(jnp.bfloat16), preferred_element_type=jnp.float32
    )


def eye_mask(order):
    rows = lax.broadcasted_iota(jnp.int32, (order, order), 0)
    return rows == lax.broadcasted_iota(jnp.int32, (order, order), 1)


LANES = 128


def to_column(row):
    mask = eye_mask(LANES)
    parts = [
        jnp.sum(jnp.where(mask, row[:, k : k + LANES], 0.0), axis=1, keepdims=True)
        for k in range(0, row.shape[1], LANES)
    ]
    return jnp.concatenate(parts, axis=0)


def to_row(column):
    mask = eye_mask(LANES)
    parts = [
        jnp.sum(jnp.where(mask, column[k : k + LANES], 0.0), axis=0, keepdims=True)
        for k in range(0, column.shape[0], LANES)
    ]
    return jnp.concatenate(parts, axis=1)


def vec_mat(column, matrix):
    return jnp.sum(column * matrix, axis=0, keepdims=True)


def mat_vec(matrix, row):
    return jnp.sum(matrix * row, axis=1, keepdims=True)


def newton_inverse(diag_ref, inverse_ref, bad_ref, bound_on_residual=0.03):
    order = diag_ref.shape[0]
    mask = eye_mask(order)
    diag = diag_ref[...]
    on_diag = jnp.where(mask, diag, 0.0)
    diag_row = jnp.sum(on_diag, axis=0, keepdims=True)
    diag_col = jnp.sum(on_diag, axis=1, keepdims=True)
    bound = jnp.max(
        jnp.sum(jnp.abs(diag), axis=0, keepdims=True) / diag_row, axis=1, keepdims=True
    )
    scale = jnp.minimum(1.0, 1.8 / bound)
    identity = jnp.where(mask, 1.0, 0.0)
    inverse_ref[...] = (scale / diag_col) * (2.0 * identity - diag * (scale / diag_row))
    current = inverse_ref[...]
    residual = identity - single_dot(diag_ref[...], current)
    estimate = (current + single_dot(current, residual)).astype(jnp.bfloat16)
    diag_hi, diag_lo = halves(diag_ref[...])
    residual = (
        identity
        - jnp.dot(diag_hi, estimate, preferred_element_type=jnp.float32)
        - jnp.dot(diag_lo, estimate, preferred_element_type=jnp.float32)
    )
    size = jnp.max(jnp.sum(jnp.abs(residual), axis=0, keepdims=True), axis=1, keepdims=True)
    bad_ref[...] = bad_ref[...] + jnp.where(size < bound_on_residual, 0.0, 1.0)
    series_hi, series_lo = halves(residual + single_dot(residual, residual))
    inverse_ref[...] = (
        estimate.astype(jnp.float32)
        + jnp.dot(estimate, series_hi, preferred_element_type=jnp.float32)
        + jnp.dot(estimate, series_lo, preferred_element_type=jnp.float32)
    )


def line_kernel(
    line_count,
    time_count,
    window_scale,
    levels,
    step_ref,
    sent_ref,
    mean_ref,
    drag_ref,
    maps_ref,
    span_ref,
    mass_ref,
    disp_in,
    vel_in,
    acc_in,
    disp_ref,
    vel_ref,
    bad_out,
    acc_ref,
    bad_ref,
    side_ref,
    diag_ref,
    inverse_ref,
    prev_span,
    prev_map,
    next_vel,
    couple,
    update,
    scaled,
    update_out,
    couple_out,
    vec_out,
    vec_in,
    load_out,
    load_in,
    sol_out,
    sol_in,
    span_sems,
    map_sems,
    vel_sems,
    update_sems,
    couple_sems,
    share_send_sems,
    share_recv_sems,
    vec_sems,
    load_send_sems,
    load_recv_sems,
    sol_sems,
    halfway,
    wind_ref,
    halfway_sems,
    wind_sems,
):
    line = lax.axis_index("line")
    time = lax.axis_index("tm")
    core = lax.rem(line, 2)
    order = span_ref.shape[1]
    last = line_count - 1

    barrier = pltpu.get_barrier_semaphore()
    partners = jnp.int32(0)
    for delta in (-1, 1):
        there = (line + delta >= 0) & (line + delta <= last)
        for turn in range(1, time_count):

            @pl.when(there)
            def _():
                pl.semaphore_signal(
                    barrier,
                    inc=1,
                    device_id=(line + delta, lax.rem(time + turn, time_count)),
                    device_id_type=MESH,
                )

        partners = partners + jnp.where(there, time_count - 1, 0)
    for turn in range(1, time_count):
        pl.semaphore_signal(
            barrier,
            inc=1,
            device_id=(line, lax.rem(time + turn, time_count)),
            device_id_type=MESH,
        )
    partners = partners + (time_count - 1)

    inner = max(2, line_count // 4)
    outer = line_count // inner
    place_x = lax.div(line, inner)
    place_y = lax.rem(line, inner)
    for turn in range(1, outer):
        pl.semaphore_signal(
            barrier,
            inc=1,
            device_id=(lax.rem(place_x + turn, outer) * inner + place_y, time),
            device_id_type=MESH,
        )
    for turn in range(1, inner):
        pl.semaphore_signal(
            barrier,
            inc=1,
            device_id=(place_x * inner + lax.rem(place_y + turn, inner), time),
            device_id_type=MESH,
        )
    partners = partners + (outer + inner - 2)
    stride = 1
    while stride < inner:
        for delta in (-stride, stride):
            near = (line + delta >= 0) & (line + delta <= last)
            if stride > 1:
                near = near & (core == 0)

            @pl.when(near)
            def _():
                pl.semaphore_signal(
                    barrier, inc=1, device_id=(line + delta, time), device_id_type=MESH
                )

            partners = partners + jnp.where(near, 1, 0)
        stride = stride * 2

    def remote(source, target, sems, to_line, to_time=None):
        return pltpu.make_async_remote_copy(
            src_ref=source,
            dst_ref=target,
            send_sem=sems[0],
            recv_sem=sems[1],
            device_id=(to_line, time if to_time is None else to_time),
            device_id_type=MESH,
        )

    def span_copy():
        return remote(span_ref.at[0], prev_span, (span_sems.at[0], span_sems.at[1]), line + 1)

    def map_copy():
        return remote(maps_ref.at[0, 1], prev_map, (map_sems.at[0], map_sems.at[1]), line + 1)

    def vel_copy(window):
        return remote(
            vel_ref,
            next_vel.at[window],
            (vel_sems.at[0, window], vel_sems.at[1, window]),
            line - 1,
        )

    blocks = order // LANES
    quarter = order // time_count

    def triangle(ref, block):
        start = block * LANES
        return ref.at[pl.ds(start, LANES), pl.ds(start, order - start)]

    def own_rows(ref, group):
        return ref.at[pl.ds(pl.multiple_of(group * quarter, quarter), quarter)]

    def update_copies(level, side):
        stride = jnp.left_shift(1, level)
        return [
            remote(
                triangle(update_out.at[side], block),
                triangle(update.at[level, 1 - side], block),
                (
                    update_sems.at[0, level, side, block],
                    update_sems.at[1, level, 1 - side, block],
                ),
                line + (2 * side - 1) * stride,
            )
            for block in range(blocks)
        ]

    def update_wait(level, side):
        for block in range(blocks):
            remote(
                triangle(update_out.at[side], block),
                triangle(update.at[level, side], block),
                (update_sems.at[0, level, side, block], update_sems.at[1, level, side, block]),
                line,
            ).wait_recv()

    def couple_copy(level, side):
        stride = jnp.left_shift(1, level)
        return remote(
            couple_out,
            own_rows(couple.at[level + 1, 1 - side], time),
            (couple_sems.at[0, level, side], couple_sems.at[1, level, 1 - side]),
            line + (2 * side - 1) * stride,
        )

    def couple_wait(level, side):
        remote(
            couple_out,
            own_rows(couple.at[level + 1, side], time),
            (couple_sems.at[0, level, side], couple_sems.at[1, level, side]),
            line,
        ).wait_recv()

    def share_copy(level, side, turn):
        rows = own_rows(couple.at[level + 1, side], time)
        return remote(
            rows,
            rows,
            (share_send_sems.at[level, side, turn], share_recv_sems.at[level, side, time]),
            line,
            lax.rem(time + turn, time_count),
        )

    def share_wait(level, side, turn):
        group = lax.rem(time + turn, time_count)
        rows = own_rows(couple.at[level + 1, side], group)
        remote(
            rows,
            rows,
            (share_send_sems.at[level, side, turn], share_recv_sems.at[level, side, group]),
            line,
        ).wait_recv()

    def vec_copy(window, level, side):
        stride = jnp.left_shift(1, level)
        return remote(
            vec_out.at[window, level, side],
            vec_in.at[window, level, 1 - side],
            (vec_sems.at[0, window, level, side], vec_sems.at[1, window, level, 1 - side]),
            line + (2 * side - 1) * stride,
        )

    def vec_wait(window, level, side):
        remote(
            vec_out.at[window, level, side],
            vec_in.at[window, level, side],
            (vec_sems.at[0, window, level, side], vec_sems.at[1, window, level, side]),
            line,
        ).wait_recv()

    def there(level, side):
        stride = jnp.left_shift(1, level)
        return (line - stride >= 0) if side == 0 else (line + stride <= last)

    def sends(level):
        return core == jnp.where(level == 0, 1, 0)

    vel_ref[...] = vel_in[...]
    disp_ref[...] = disp_in[...]
    acc_ref[...] = acc_in[...]
    bad_ref[...] = jnp.zeros_like(bad_ref)
    own_diag = jnp.where(eye_mask(order), accel_scale * to_column(mass_ref[...]), 0.0)
    diag_ref[...] = span_ref[0] + own_diag

    @pl.when(core == 1)
    def _():
        couple[0, 1] = -jnp.where(line < last, 1.0, 0.0) * span_ref[0]

    pl.semaphore_wait(barrier, partners)

    @pl.when(core == 0)
    def _():
        span_copy().start()

    @pl.when(line > 0)
    def _():
        vel_copy(0).start()

    @pl.when(line < last)
    def _():
        map_copy().start()

    @pl.when(line == last)
    def _():
        next_vel[...] = jnp.zeros_like(next_vel)

    def along_y(turn):
        to_y = lax.rem(place_y + turn, inner)
        return remote(
            sent_ref.at[:, to_y],
            halfway.at[:, place_y],
            (halfway_sems.at[0, to_y], halfway_sems.at[1, place_y]),
            place_x * inner + to_y,
        )

    def along_y_wait(turn):
        from_y = lax.rem(place_y + turn, inner)
        remote(
            sent_ref.at[:, from_y],
            halfway.at[:, from_y],
            (halfway_sems.at[0, from_y], halfway_sems.at[1, from_y]),
            line,
        ).wait_recv()

    def along_x(turn):
        to_x = lax.rem(place_x + turn, outer)
        return remote(
            halfway.at[to_x],
            wind_ref.at[place_x],
            (wind_sems.at[0, to_x], wind_sems.at[1, place_x]),
            to_x * inner + place_y,
        )

    def along_x_wait(turn):
        from_x = lax.rem(place_x + turn, outer)
        remote(
            halfway.at[from_x],
            wind_ref.at[from_x],
            (wind_sems.at[0, from_x], wind_sems.at[1, from_x]),
            line,
        ).wait_recv()

    for turn in range(1, inner):
        along_y(turn).start()
    halfway[:, place_y] = sent_ref[:, place_y]

    @pl.when(core == 1)
    def _():
        span_copy().wait_recv()
        diag_ref[...] = diag_ref[...] + prev_span[...]
        couple[0, 0] = -prev_span[...]

    def load_copy(window, turn):
        step = 0 if turn < time_count else 1
        return remote(
            load_out.at[window],
            load_in.at[window, step, time],
            (load_send_sems.at[window, turn], load_recv_sems.at[window, step, time]),
            line + step,
            lax.rem(time + turn, time_count),
        )

    def load_wait(window, step, group):
        remote(
            load_out.at[window],
            load_in.at[window, step, group],
            (load_send_sems.at[window, 0], load_recv_sems.at[window, step, group]),
            line,
        ).wait_recv()

    def begin_loads(window):
        velocity_col = to_column(vel_ref[...])
        own_offset = mean_ref[...] - vec_mat(velocity_col, maps_ref[0, 0])
        side_ref[...] = mass_ref[...] * (
            accel_scale * disp_ref[...] + velocity_scale * vel_ref[...] + acc_ref[...]
        )

        @pl.when((line < last) if window == 0 else (core == 0))
        def _():
            vel_wait(window)

        next_col = to_column(next_vel[window])
        offset = own_offset - vec_mat(next_col, maps_ref[0, 1])
        samples, width = wind_ref.shape[2:]

        def add(from_y, total):
            for from_x in range(outer):
                relative = wind_ref[from_x, from_y].astype(jnp.float32) + offset
                group = (from_x * inner + from_y) * time_count + time
                step = step_ref[group].astype(jnp.float32)
                total = total + (step if window == 1 else 1.0 - step) * (
                    relative * jnp.abs(relative)
                )
            return total

        total = lax.fori_loop(0, inner, add, jnp.zeros((samples, width), jnp.float32))
        load = drag_ref[...] * jnp.sum(total, axis=0, keepdims=True) * window_scale
        load_out[window] = load
        load_in[window, 0, time] = load
        for turn in range(1, time_count):
            load_copy(window, turn).start()

        @pl.when(line < last)
        def _():
            for turn in range(time_count, 2 * time_count):
                load_copy(window, turn).start()

    def end_loads(window):
        for turn in range(1, time_count):
            load_wait(window, 0, lax.rem(time + turn, time_count))

        @pl.when(line > 0)
        def _():
            for turn in range(time_count):
                load_wait(window, 1, lax.rem(time + turn, time_count))

        def summed(step):
            total = load_in[window, step, 0]
            for group in range(1, time_count):
                total = total + load_in[window, step, group]
            return total

        side_ref[...] = side_ref[...] + to_row(mat_vec(maps_ref[0, 0], summed(0)))

        @pl.when(line > 0)
        def _():
            if window == 0:
                map_copy().wait_recv()
            side_ref[...] = side_ref[...] + to_row(mat_vec(prev_map[...], summed(1)))

    def send_vector(window, level):
        @pl.when(sends(level))
        def _():
            column = to_column(side_ref[...])
            for side in range(2):

                @pl.when(there(level, side))
                def _():
                    vec_out[window, level, side, :, :order] = vec_mat(column, scaled[level, side])
                    vec_out[window, level, side, :, order:] = bad_ref[...]
                    vec_copy(window, level, side).start()

    def take_vector(window, level):
        @pl.when(core == 0)
        def _():
            for side in range(2):

                @pl.when(there(level, side))
                def _():
                    vec_wait(window, level, side)
                    side_ref[...] = side_ref[...] - vec_in[window, level, side, :, :order]
                    if window == 1:
                        bad_ref[...] = bad_ref[...] + vec_in[window, level, side, :, order:]

    def loads_left(window):
        for turn in range(1, time_count):
            load_copy(window, turn).wait_send()

        @pl.when(line < last)
        def _():
            for turn in range(time_count, 2 * time_count):
                load_copy(window, turn).wait_send()

    def vectors_left(window, level):
        for side in range(2):

            @pl.when(sends(level) & there(level, side))
            def _():
                vec_copy(window, level, side).wait_send()

    def factor_level(level, carry):
        before = jnp.maximum(level - 1, 0)

        @pl.when(level == levels)
        def _():
            send_vector(0, before)

        @pl.when(sends(level))
        def _():
            newton_inverse(diag_ref, inverse_ref, bad_ref)

        for side in range(2):
            sent = (level >= 1) & sends(before) & there(before, side)

            @pl.when(sent)
            def _():
                for copy in update_copies(before, side):
                    copy.wait_send()

            @pl.when(sent & (level < levels))
            def _():
                couple_copy(before, side).wait_send()

        def coupling(side):
            expected = (level >= 1) & (core == 0)

            @pl.when(expected & there(before, side))
            def _():
                for turn in range(1, time_count):
                    share_wait(before, side, turn)
                    share_copy(before, side, turn).wait_send()

            @pl.when(expected & jnp.logical_not(there(before, side)))
            def _():
                couple[level, side] = jnp.zeros((order, order), jnp.float32)

        @pl.when(sends(level) & (level < levels))
        def _():
            coupling(0)

            @pl.when(there(level, 0))
            def _():
                scaled[level, 0] = split_dot(inverse_ref[...], couple[level, 0], 1, 1)

            half = order // 2

            @pl.when(there(level, 0))
            def _():
                copies = update_copies(level, 0)
                for start in (0, half):
                    rows, columns = pl.ds(start, half), pl.ds(start, order - start)
                    update_out[0, rows, columns] = split_dot(
                        couple[level, 0, rows], scaled[level, 0, :, columns]
                    )
                    for block in range(start // LANES, (start + half) // LANES):
                        copies[block].start()

            coupling(1)

            @pl.when(there(level, 1))
            def _():
                scaled[level, 1] = split_dot(inverse_ref[...], couple[level, 1])

            @pl.when(level < levels - 1)
            def _():
                rows = pl.ds(pl.multiple_of(time * quarter, quarter), quarter)
                both = there(level, 0) & there(level, 1)

                @pl.when(both)
                def _():
                    couple_out[...] = -split_dot(couple[level, 0, rows], scaled[level, 1])

                @pl.when(jnp.logical_not(both))
                def _():
                    couple_out[...] = jnp.zeros_like(couple_out)

                for side in range(2):

                    @pl.when(there(level, side))
                    def _():
                        couple_copy(level, side).start()

            @pl.when(there(level, 1))
            def _():
                own = jnp.where(level == 0, 1.0, 0.0)
                copies = update_copies(level, 1)
                for start in (0, half):
                    rows, columns = pl.ds(start, half), pl.ds(start, order - start)
                    update_out[1, rows, columns] = (
                        split_dot(couple[level, 1, :, rows], scaled[level, 1, :, columns], 0, 0)
                        - own * span_ref[0, rows, columns]
                    )
                    for block in range(start // LANES, (start + half) // LANES):
                        copies[block].start()

        for side in range(2):

            @pl.when((level < levels - 1) & (core == 0) & there(level, side))
            def _():
                couple_wait(level, side)
                for turn in range(1, time_count):
                    share_copy(level, side, turn).start()

        @pl.when(level == 0)
        def _():
            for turn in range(1, inner):
                along_y_wait(turn)
            for turn in range(1, outer):
                along_x(turn).start()
            wind_ref[place_x] = halfway[place_x]

        @pl.when(level == 1)
        def _():
            for turn in range(1, outer):
                along_x_wait(turn)
            begin_loads(0)

        @pl.when(level == 2)
        def _():
            end_loads(0)
            send_vector(0, level - 2)
            take_vector(0, level - 2)

        @pl.when((level >= 2) & (level < levels))
        def _():
            send_vector(0, before)

        @pl.when(level >= 2)
        def _():
            take_vector(0, before)
            vectors_left(0, before)

        @pl.when(level == 3)
        def _():
            vectors_left(0, level - 3)
            for turn in range(1, outer):
                along_x(turn).wait_send()
            for turn in range(1, inner):
                along_y(turn).wait_send()
            loads_left(0)

            @pl.when(core == 0)
            def _():
                span_copy().wait_send()

            @pl.when(line < last)
            def _():
                map_copy().wait_send()

        @pl.when(level < levels)
        def _():
            @pl.when(core == 0)
            def _():
                for side in range(2):

                    @pl.when(there(level, side))
                    def _():
                        update_wait(level, side)
                        for block in range(blocks):
                            start = block * LANES
                            part = (pl.ds(start, LANES), pl.ds(start, order - start))
                            diag_ref[part] = diag_ref[part] - update[(level, side) + part]

                for block in range(blocks):
                    rows = pl.ds(block * LANES, LANES)
                    for other in range(block + 1, blocks):
                        columns = pl.ds(other * LANES, LANES)
                        diag_ref[columns, rows] = diag_ref[rows, columns].T

        return carry

    def vel_wait(window):
        remote(
            vel_ref,
            next_vel.at[window],
            (vel_sems.at[0, window], vel_sems.at[1, window]),
            line,
        ).wait_recv()

    lax.fori_loop(0, levels + 1, factor_level, 0)

    def sol_copy(window, side):
        return remote(
            sol_out.at[window],
            sol_in.at[window, 1 - side],
            (sol_sems.at[0, window, side], sol_sems.at[1, window, 1 - side]),
            line + 2 * side - 1,
        )

    def sol_wait(window, side):
        remote(
            sol_out.at[window],
            sol_in.at[window, side],
            (sol_sems.at[0, window, side], sol_sems.at[1, window, side]),
            line,
        ).wait_recv()

    def advance(solution_row):
        new_accel = (
            accel_scale * (solution_row - disp_ref[...])
            - velocity_scale * vel_ref[...]
            - acc_ref[...]
        )
        vel_ref[...] = vel_ref[...] + half_step * (acc_ref[...] + new_accel)
        disp_ref[...] = solution_row
        acc_ref[...] = new_accel

    @pl.when(line > 0)
    def _():
        vel_copy(0).wait_send()

    def finish(window):
        @pl.when(core == 0)
        def _():
            advance(vec_mat(to_column(side_ref[...]), inverse_ref[...]))
            sol_out[window, :, :order] = disp_ref[...]
            sol_out[window, :, order : 2 * order] = vel_ref[...]
            sol_out[window, :, 2 * order :] = bad_ref[...]
            sol_copy(window, 1).start()

            @pl.when(line > 0)
            def _():
                sol_copy(window, 0).start()

        @pl.when(core == 1)
        def _():
            value = vec_mat(to_column(side_ref[...]), inverse_ref[...])
            sol_wait(window, 0)
            behind = mat_vec(scaled[0, 0], sol_in[window, 0, :, :order])
            side_ref[...] = value - to_row(behind)
            if window == 1:
                bad_ref[...] = sol_in[window, 0, :, 2 * order :]

            @pl.when(line < last)
            def _():
                sol_wait(window, 1)
                ahead = mat_vec(scaled[0, 1], sol_in[window, 1, :, :order])
                side_ref[...] = side_ref[...] - to_row(ahead)
                if window == 0:
                    next_vel[1] = sol_in[window, 1, :, order : 2 * order]

            advance(side_ref[...])
            if window == 0:
                vel_copy(1).start()

    finish(0)

    begin_loads(1)
    end_loads(1)

    def reduce_level(level, carry):
        send_vector(1, level)
        take_vector(1, level)
        return carry

    lax.fori_loop(0, levels, reduce_level, 0)

    @pl.when(core == 1)
    def _():
        vel_copy(1).wait_send()

    finish(1)
    bad_out[...] = bad_ref[...]

    loads_left(1)

    for window in range(2):

        @pl.when(core == 0)
        def _():
            sol_copy(window, 1).wait_send()

            @pl.when(line > 0)
            def _():
                sol_copy(window, 0).wait_send()

    def drain(level, carry):
        vectors_left(1, level)
        return carry

    lax.fori_loop(0, levels, drain, 0)


def run_line(
    line_count,
    time_count,
    window_scale,
    segment_step,
    wind_field,
    mean_wind,
    drag,
    transfer,
    span_stiff,
    mass,
    disp0,
    vel0,
    acc0,
):
    order = span_stiff.shape[-1]
    width = mean_wind.shape[-1]
    levels = (line_count - 1).bit_length()
    row = jax.ShapeDtypeStruct((1, order), jnp.float32)
    inner = max(2, line_count // 4)
    outer = line_count // inner
    wind_field = wind_field.reshape((outer, inner) + wind_field.shape[1:])

    def body(*refs):
        line_kernel(line_count, time_count, window_scale, levels, *refs)

    vmem = pl.BlockSpec(memory_space=pltpu.VMEM)
    dma = pltpu.SemaphoreType.DMA

    def buffer(*shape):
        return pltpu.VMEM(shape, jnp.float32)

    return pl.pallas_call(
        body,
        out_shape=(row, row, jax.ShapeDtypeStruct((1, LANES), jnp.float32)),
        in_specs=[pl.BlockSpec(memory_space=pltpu.SMEM)] + [vmem] * 9,
        out_specs=[vmem] * 3,
        scratch_shapes=[
            buffer(1, order),
            buffer(1, LANES),
            buffer(1, order),
            buffer(order, order),
            buffer(order, order),
            buffer(order, order),
            buffer(order, width),
            buffer(2, 1, order),
            buffer(levels, 2, order, order),
            buffer(levels, 2, order, order),
            buffer(levels, 2, order, order),
            buffer(2, order, order),
            buffer(order // time_count, order),
            buffer(2, levels, 2, 1, order + LANES),
            buffer(2, levels, 2, 1, order + LANES),
            buffer(2, 1, width),
            buffer(2, 2, time_count, 1, width),
            buffer(2, 1, 2 * order + LANES),
            buffer(2, 2, 1, 2 * order + LANES),
            dma((2,)),
            dma((2,)),
            dma((2, 2)),
            dma((2, levels, 2, order // LANES)),
            dma((2, levels, 2)),
            dma((levels, 2, time_count)),
            dma((levels, 2, time_count)),
            dma((2, 2, levels, 2)),
            dma((2, 2 * time_count)),
            dma((2, 2, time_count)),
            dma((2, 2, 2)),
            pltpu.VMEM(wind_field.shape, wind_field.dtype),
            pltpu.VMEM(wind_field.shape, wind_field.dtype),
            dma((2, inner)),
            dma((2, outer)),
        ],
        compiler_params=pltpu.CompilerParams(
            collective_id=0, has_side_effects=True, vmem_limit_bytes=60 * 2**20
        ),
        cost_estimate=pl.CostEstimate(
            flops=100 * order**3, bytes_accessed=5 * 2**20, transcendentals=0
        ),
    )(segment_step, wind_field, mean_wind, drag, transfer, span_stiff, mass, disp0, vel0, acc0)


def local(
    gust_coef,
    mean_wind,
    drag,
    span_column,
    segment_step,
    transfer,
    span_stiff,
    mass,
    disp0,
    vel0,
    acc0,
):
    line_count = lax.axis_size("line")
    time_count = lax.axis_size("tm")
    time_pos = lax.axis_index("tm")
    span_count = span_column.shape[0]
    seg_count = segment_step.shape[0]
    trig_rows = trig_table(TS, KF)
    spectra = gust_coef.reshape(2 * KF, span_count * Q)
    wind_field = jnp.dot(trig_rows, spectra, preferred_element_type=jnp.float32).astype(
        jnp.bfloat16
    )
    wind_field = wind_field.reshape(TS, span_count, Q)
    wind_field = wind_field.at[:, span_column].get(mode="promise_in_bounds").transpose(1, 0, 2)
    window_scale = 1.0 / (TS * (seg_count // 2))
    fast_disp, fast_vel, bad = run_line(
        line_count,
        time_count,
        window_scale,
        segment_step,
        wind_field,
        mean_wind,
        drag,
        transfer,
        span_stiff,
        mass,
        disp0,
        vel0,
        acc0,
    )

    def checked():
        arrived = lax.all_to_all(wind_field, "line", split_axis=0, concat_axis=0, tiled=True)
        seg_index = jnp.arange(line_count, dtype=jnp.int32) * time_count + time_pos
        seg_flags = jnp.take(segment_step, seg_index)
        return checked_loop(
            line_count,
            time_count,
            arrived,
            seg_flags,
            mean_wind,
            drag,
            transfer,
            span_stiff,
            mass,
            disp0,
            vel0,
            acc0,
            window_scale,
        )

    def chosen():
        return jnp.concatenate(checked(), axis=0)

    both = lax.cond(
        bad[0, 0] < 0.5, lambda: jnp.concatenate([fast_disp, fast_vel], axis=0), chosen
    )
    return both[:1], both[1:]


def solution(mesh):
    return jax.shard_map(
        local,
        mesh=mesh,
        in_specs=(
            P(("line", "tm"), None, None, None),
            P("line", None),
            P("line", None),
            P(),
            P(),
            P("line", None, None, None),
            P("line", None, None),
            P("line", None),
            P("line", None),
            P("line", None),
            P("line", None),
        ),
        out_specs=(P("line", None), P("line", None)),
        check_vma=False,
    )
```
